32 devices in a mesh: group: 2 (over y), slab: 4 (over z), plane: 4 (over x, core).
Axes of the slice: x: 2, y: 2, z: 4, core: 2. Of those that a mesh axis runs over, the one named last changes fastest.
Arguments:
- fields: float32 [2, 32, 128, 1024], P('group', None, 'slab', 'plane'), may hold values from 0 to 2
- evap_rates: float32 [32], replicated, may hold values from 0.05 to 0.5
- coal_kernel: bfloat16 [32, 1024], replicated, may hold values from -0.1875 to 0.1875
- plume_width: float32 [8], replicated, may hold values from 1 to 8
- owner_map: int32 [16, 2048], P(('slab', 'plane')), may hold values from 0 to 15, as said below
- deposit_cell: int32 [16, 2048], P(('slab', 'plane')), may hold values from 0 to 8191
- plume_ids: int32 [16, 2048], P(('slab', 'plane')), may hold values from 0 to 7
Outputs:
- new_fields: float32 [2, 32, 128, 1024], P('group', None, 'slab', 'plane')
The draws below stay inside these ranges and needn't reach their ends.
Inputs may be any that keep to these rules, and one draw needn't show every extreme that they name: `owner_map`: among the 2048 rows of one index of the first dimension, at most 256 name any one spray block, and one block is named by exactly 256 of them at every index.
All inputs are finite; a program needn't handle non-finite values.
Results may differ from the reference program's by a relative error of at most 0.0014.
Values may be sent and summed in bfloat16 or wider, within the bound.
A program may use at most 64 MiB of HBM per device.

```python
import math
import jax
import jax.numpy as jnp
import numpy as np
from jax import lax

SEC = 32
PLUMES = 8
CA = 32
CB = 256
NA = 128
NB = 1024
OWNERS = 16
EXIT_ROWS = 2048
CAP = 256
N_SLAB = 4
N_PLANE = 4


def draw_owner_map(key, part):
    key_hot, key_order, key_rows = jax.random.split(key, 3)
    hottest = jax.random.randint(key_hot, (), 0, OWNERS).astype(jnp.int32)
    labels = jax.random.permutation(key_order, OWNERS - 1).astype(jnp.int32)
    others = jnp.where(labels >= hottest, labels + 1, labels).astype(jnp.int32)
    heavy = OWNERS // 2
    pool_index = np.concatenate([np.repeat(np.arange(heavy), CAP), np.repeat(np.arange(heavy, OWNERS - 1), CAP // 4)]).astype(np.int32)
    slot_pool = others[pool_index]

    def draw_block(block_key):
        key_pick, key_place = jax.random.split(block_key)
        chosen = jax.random.permutation(key_pick, slot_pool)[:EXIT_ROWS - CAP]
        listing = jnp.concatenate([jnp.full((CAP,), hottest, jnp.int32), chosen.astype(jnp.int32)])
        return jax.random.permutation(key_place, listing)
    return jax.vmap(draw_block)(jax.random.split(key_rows, OWNERS))


def set_ends(array, own_key, least, top_value):
    dims = array.shape
    place = [jax.random.randint(jax.random.fold_in(own_key, axis), (), 0, dims[axis]) for axis in range(len(dims))]
    array = array.at[tuple(place)].set(least)
    longest = dims.index(max(dims))
    place[longest] = (place[longest] + 1) % dims[longest]
    return array.at[tuple(place)].set(top_value)


def level_of(key, shape, shards, least, top_value):
    def one(dim, shards_of):
        heights = jax.random.uniform(jax.random.fold_in(jax.random.fold_in(key, 6), dim), (shards_of,), jnp.float32, least / len(shards), top_value / len(shards))
        return jnp.repeat(jnp.exp(heights), shape[dim] // shards_of).reshape((-1,) + (1,) * (len(shape) - dim - 1))

    gain = one(*shards[0])
    for cut in shards[1:]:
        gain = gain * one(*cut)
    return gain


def scatter_about(stream_key, extent, deviation, bound, kind=jnp.bfloat16):
    return jnp.clip(deviation * jax.random.normal(stream_key, extent, jnp.float32), -bound, bound).astype(kind)


def setup_inputs(seed: int = 0) -> dict:
    arg_keys = jax.random.split(jax.random.key(seed), 8)
    fields = jnp.clip(2.0 * jax.random.uniform(arg_keys[0], (2, SEC, NA, NB), jnp.float32) ** level_of(arg_keys[0], (2, SEC, NA, NB), ((0, 2), (2, 4), (3, 4)), -0.2, 0.2), 0.0, 2.0)
    evap_rates = jnp.clip(jnp.exp(jax.random.uniform(arg_keys[1], (SEC,), jnp.float32, math.log(0.05), math.log(0.5))), 0.05, 0.5)
    coal_kernel = scatter_about(arg_keys[2], (SEC, SEC * SEC), (SEC * SEC) ** -0.5, 0.1875)
    plume_width = jnp.clip(jnp.exp(jax.random.uniform(arg_keys[3], (PLUMES,), jnp.float32, math.log(1.0), math.log(8.0))), 1.0, 8.0)
    owner_map = draw_owner_map(jax.random.fold_in(arg_keys[7], 71), 0)
    deposit_cell = set_ends(jax.random.randint(arg_keys[5], (OWNERS, EXIT_ROWS), 0, CA * CB), jax.random.fold_in(arg_keys[5], 1), 0, (CA * CB) - 1).astype(jnp.int32)
    plume_ids = set_ends(jax.random.randint(arg_keys[6], (OWNERS, EXIT_ROWS), 0, PLUMES), jax.random.fold_in(arg_keys[6], 1), 0, PLUMES - 1).astype(jnp.int32)
    return dict(fields=fields, evap_rates=evap_rates, coal_kernel=coal_kernel, plume_width=plume_width, owner_map=owner_map, deposit_cell=deposit_cell, plume_ids=plume_ids)


cfl_nozzle = 0.35
diffusion = 0.2
relax_rate = 5.0
relax_step = 0.1
collide_step = 0.25

def laplace(padded):
    center = padded[:, 1:-1, 1:-1]
    return padded[:, :-2, 1:-1] + padded[:, 2:, 1:-1] + padded[:, 1:-1, :-2] + padded[:, 1:-1, 2:] - 4.0 * center

def nozzle_update(padded):
    center = padded[:, 1:-1, 1:-1]
    channels, span_axial, span_cross = center.shape
    layers = channels // 4
    blocks = center.reshape(4, layers, span_axial, span_cross)
    spread = laplace(padded).reshape(4, layers, span_axial, span_cross)
    previous = jnp.concatenate([jnp.zeros_like(blocks[:, :1]), blocks[:, :-1]], axis=1)
    upwind = blocks - previous
    density = blocks[0]
    mass_flux = blocks[1]
    quality = blocks[2]
    enthalpy = blocks[3]
    relaxing = relax_rate / (1.0 + density * density)
    new_density = density - cfl_nozzle * upwind[1] + diffusion * spread[0]
    new_flux = mass_flux - cfl_nozzle * (upwind[1] + upwind[2]) + diffusion * spread[1]
    new_quality = quality + relax_step * relaxing * (enthalpy - quality) - cfl_nozzle * upwind[2] + diffusion * spread[2]
    new_enthalpy = enthalpy - cfl_nozzle * upwind[3] + diffusion * spread[3]
    stacked = jnp.stack([new_density, new_flux, new_quality, new_enthalpy])
    return stacked.reshape(channels, span_axial, span_cross)

def spray_transport(padded, evap_rates):
    center = padded[:, 1:-1, 1:-1]
    sections = center.shape[0]
    speeds = 0.2 + 0.5 * jnp.arange(sections, dtype=jnp.float32) / (sections - 1)
    shifted = center - speeds[:, None, None] * (center - padded[:, :-2, 1:-1]) + diffusion * laplace(padded)
    evaporated = evap_rates[:, None, None] * center
    gained = jnp.concatenate([evaporated[1:], jnp.zeros_like(evaporated[:1])], axis=0)
    return shifted - evaporated + gained

def collide(flattened, coal_kernel):
    sections, cell_count = flattened.shape
    block_size = min(2048, cell_count)
    pieces = flattened.reshape(sections, cell_count // block_size, block_size).transpose(1, 0, 2)
    kernel_wide = coal_kernel.astype(jnp.float32)

    def collide_block(segment):
        pair_terms = (segment[:, None, :] * segment[None, :, :]).reshape(sections * sections, block_size)
        pair_terms = pair_terms.astype(jnp.bfloat16).astype(jnp.float32)
        return jnp.dot(kernel_wide, pair_terms, precision=lax.Precision.HIGHEST)
    return lax.map(collide_block, pieces).transpose(1, 0, 2).reshape(sections, cell_count)

def spray_update(padded, evap_rates, coal_kernel):
    shifted = spray_transport(padded, evap_rates)
    sections, span_axial, span_cross = shifted.shape
    flattened = shifted.reshape(sections, span_axial * span_cross)
    midpoint = flattened + 0.5 * collide_step * collide(flattened, coal_kernel)
    advanced = flattened + collide_step * collide(midpoint, coal_kernel)
    return advanced.reshape(sections, span_axial, span_cross)

def row_masses(coarse, plume_ids, plume_width):
    mass_flux = coarse[1]
    quality = coarse[2]
    enthalpy = coarse[3]
    strength = jnp.sqrt(1.0 + mass_flux * mass_flux)
    center = (SEC - 1) * jax.nn.sigmoid(enthalpy - 2.0 * quality)
    matches = plume_ids[:, None] == jnp.arange(plume_width.shape[0], dtype=jnp.int32)[None, :]
    spread_width = lax.optimization_barrier(jnp.sum(jnp.where(matches, plume_width[None, :], 0.0), axis=1))
    levels = jnp.arange(SEC, dtype=jnp.float32)
    scaled = (levels[:, None] - center[None, :]) / spread_width[None, :]
    weights = 1.0 / (1.0 + scaled * scaled)
    masses = strength[None, :] * weights / lax.optimization_barrier(jnp.sum(weights, axis=0, keepdims=True))
    return masses.astype(jnp.bfloat16)

def reference(fields, evap_rates, coal_kernel, plume_width, owner_map, deposit_cell, plume_ids):
    widths = ((0, 0), (1, 1), (1, 1))
    nozzle = nozzle_update(jnp.pad(fields[0], widths))
    spray_field = spray_update(jnp.pad(fields[1], widths), evap_rates, coal_kernel)
    layers = SEC // 4
    exit_layer = nozzle.reshape(4, layers, NA, NB)[:, layers - 1]
    coarse = exit_layer.reshape(4, NA // 2, 2, NB // 2, 2).mean(axis=(2, 4))
    coarse = coarse.reshape(4, N_SLAB, CA // 2, N_PLANE, CB // 2).transpose(0, 1, 3, 2, 4)
    coarse = coarse.reshape(4, OWNERS * EXIT_ROWS)
    masses = row_masses(coarse, plume_ids.reshape(-1), plume_width)
    owners = owner_map.reshape(-1)
    target_cells = deposit_cell.reshape(-1)
    target_axial = owners // N_PLANE * CA + target_cells // CB
    target_cross = owners % N_PLANE * CB + target_cells % CB
    deposit = jnp.zeros((SEC, NA, NB), jnp.float32).at[:, target_axial, target_cross].add(masses.astype(jnp.float32))
    return jnp.stack([nozzle, spray_field + deposit])
```

```python
import functools

import jax
import jax.numpy as jnp
import numpy as np
from jax import lax
from jax.experimental import pallas as pl
from jax.experimental.pallas import tpu as pltpu
from jax.sharding import PartitionSpec as P

MESH = pl.DeviceIdType.MESH
F32 = jnp.float32
BF16 = jnp.bfloat16
LANES = 128
SLOTS = 256
CHUNK = 4
SOURCES = 4
PIECES = 4
VMEM_BYTES = 56 * 1024 * 1024

cfl_nozzle = 0.35
diffusion = 0.2
relax_rate = 5.0
relax_step = 0.1
collide_step = 0.25


def fold_matrix(sections):
    kept = [(i, j) for i in range(sections) for j in range(i // 8 * 8, sections)]
    fold = np.zeros((sections * sections, len(kept)), np.float32)
    for q, (i, j) in enumerate(kept):
        fold[i * sections + j, q] = 1.0
        if j // 8 > i // 8:
            fold[j * sections + i, q] = 1.0
    return fold


def pair_terms(m):
    sections, width = m.shape
    pieces = []
    for i in range(sections):
        low = i // 8 * 8
        pieces.append(jnp.broadcast_to(m[i : i + 1], (sections - low, width)) * m[low:])
    return jnp.concatenate(pieces, axis=0).astype(BF16)


def split_hi_lo(x):
    hi = x.astype(BF16)
    lo = (x - hi.astype(F32)).astype(BF16)
    return hi, lo


def dot_last(a, b):
    return lax.dot_general(a, b, (((1,), (1,)), ((), ())), preferred_element_type=F32)


def kernel(
    n_slab, n_plane, sections, ca, cb, exit_rows,
    fields_hbm, evap_hbm, coal_hbm, fold_hbm, owner_hbm, cell_hbm, pid_hbm,
    obuf, recv_buf,
    fbuf, tbuf, hbuf, fold, cols_out, cols_in, par, send_buf,
    evap_ref, coal_ref, owner_ref, cell_ref, pid_ref, picks, in_slot,
    in_sem, arg_sem, halo_send, halo_recv, row_send, row_recv,
):
    owners = n_slab * n_plane
    rows = sections * ca
    g = lax.axis_index("group")
    s = lax.axis_index("slab")
    p = lax.axis_index("plane")
    me = s * n_plane + p

    load = pltpu.make_async_copy(fields_hbm, fbuf, in_sem)
    load.start()
    nozzle_args = [
        pltpu.make_async_copy(source, target, arg_sem.at[k])
        for k, (source, target) in enumerate(
            ((owner_hbm, owner_ref), (cell_hbm, cell_ref), (pid_hbm, pid_ref))
        )
    ]
    spray_args = [
        pltpu.make_async_copy(source, target, arg_sem.at[k])
        for k, (source, target) in enumerate(
            ((evap_hbm, evap_ref), (coal_hbm, coal_ref), (fold_hbm, fold))
        )
    ]

    @pl.when(g == 0)
    def _():
        for copy in nozzle_args:
            copy.start()

    @pl.when(g == 1)
    def _():
        for copy in spray_args:
            copy.start()

    barrier = pltpu.get_barrier_semaphore()
    sides = [
        (s > 0, (g, s - 1, p)),
        (s < n_slab - 1, (g, s + 1, p)),
        (p > 0, (g, s, p - 1)),
        (p < n_plane - 1, (g, s, p + 1)),
    ]
    near = 0
    for there, target in sides:
        near = near + there.astype(jnp.int32)

        @pl.when(there)
        def _():
            pl.semaphore_signal(barrier, inc=1, device_id=target, device_id_type=MESH)

    @pl.when(g == 1)
    def _():
        @pl.loop(0, owners)
        def _(o):
            pl.semaphore_signal(
                barrier, inc=1, device_id=(0, o // n_plane, o % n_plane), device_id_type=MESH
            )

    load.wait()

    def lines(a, h):
        return pl.ds(a // 8 * 16 + h * 8 + a % 8, sections, stride=2 * ca)

    def gather_row(ref, a):
        return jnp.concatenate([ref[lines(a, h), :] for h in range(2)], axis=1)

    def half(ref, h):
        return ref[...].reshape(rows // 8, 2, 8, LANES)[:, h].reshape(rows, LANES)

    def halo(kind, target):
        source, landing = (
            (tbuf.at[ca], tbuf.at[0]),
            (tbuf.at[1], tbuf.at[ca + 1]),
            (cols_out.at[1], cols_in.at[0]),
            (cols_out.at[0], cols_in.at[1]),
        )[kind]
        return pltpu.make_async_remote_copy(
            src_ref=source,
            dst_ref=landing,
            send_sem=halo_send.at[kind],
            recv_sem=halo_recv.at[kind],
            device_id=target,
            device_id_type=MESH,
        )

    outgoing = (sides[1], sides[0], sides[3], sides[2])
    def start_halo(kinds):
        for kind in kinds:

            @pl.when(outgoing[kind][0])
            def _():
                halo(kind, outgoing[kind][1]).start()

    def extract_columns():
        for a in (0, ca - 1):
            tbuf[a + 1] = gather_row(fbuf, a)

        lane = lax.broadcasted_iota(jnp.int32, (8, LANES), 1)
        for h, at in ((0, 0), (1, LANES - 1)):
            select = (lane == at).astype(BF16)
            cols_out[h] = dot_last(select, half(fbuf, h).astype(BF16))[0:1]

    def fill_rows():
        @pl.loop(1, ca - 1)
        def _(a):
            tbuf[a + 1] = gather_row(fbuf, a)

        for kind, landing in enumerate((tbuf.at[0], tbuf.at[ca + 1], cols_in.at[0], cols_in.at[1])):

            @pl.when(jnp.logical_not(sides[kind][0]))
            def _():
                landing[...] = jnp.zeros(landing.shape, F32)

    def finish_halo():
        for kind in range(4):

            @pl.when(outgoing[kind][0])
            def _():
                halo(kind, outgoing[kind][1]).wait_send()

            @pl.when(sides[kind][0])
            def _():
                halo(kind, outgoing[kind][1]).wait_recv()

        sub = lax.broadcasted_iota(jnp.int32, (16, cb), 0)
        lanes = lax.broadcasted_iota(jnp.int32, (16, cb), 1)
        stack = jnp.concatenate([cols_in[0], cols_in[1], jnp.zeros((14, rows), F32)], axis=0)
        place = jnp.logical_or(
            jnp.logical_and(sub == 0, lanes == 0), jnp.logical_and(sub == 1, lanes == cb - 1)
        ).astype(BF16)
        placed = jnp.dot(stack.T.astype(BF16), place, preferred_element_type=F32)
        for h in range(2):
            hbuf[h] = placed[:, h * LANES : (h + 1) * LANES]

    col_lane = lax.broadcasted_iota(jnp.int32, (sections, cb), 1)
    col_row = lax.broadcasted_iota(jnp.int32, (sections, cb), 0)

    def column_halo(a):
        return jnp.concatenate(
            [hbuf[h, pl.ds(a, sections, stride=ca), :] for h in range(2)], axis=1
        )

    def neighbours(a):
        c = tbuf[a + 1]
        up = tbuf[a]
        left = jnp.where(col_lane == 0, 0.0, pltpu.roll(c, 1, 1))
        right = jnp.where(col_lane == cb - 1, 0.0, pltpu.roll(c, cb - 1, 1))
        lap = up + tbuf[a + 2] + (left + right + column_halo(a)) - 4.0 * c
        return c, up, lap

    def scatter_row(a, value):
        for h in range(2):
            obuf[lines(a, h), :] = value[:, h * LANES : (h + 1) * LANES]

    @pl.when(g == 0)
    def _():
        for copy in nozzle_args:
            copy.wait()
        owner = owner_ref[...]
        slots = []
        below = lax.broadcasted_iota(jnp.int32, (256, 256), 0)
        after = lax.broadcasted_iota(jnp.int32, (256, 256), 1)
        upto = (below <= after).astype(BF16)
        names = lax.broadcasted_iota(jnp.int32, (owners, 256), 0)
        carry = jnp.zeros((owners, 1), F32)
        for j in range(exit_rows // 256):
            hit = (owner[:, j * 256 : (j + 1) * 256] == names).astype(F32)
            count = jnp.dot(hit.astype(BF16), upto, preferred_element_type=F32) + carry
            slots.append(jnp.sum(hit * (count - 1.0), axis=0, keepdims=True))
            carry = count[:, 255:256]
        slot = jnp.concatenate(slots, axis=1)
        cell = cell_ref[...]
        across = jnp.bitwise_and(cell, cb - 1)
        along = jnp.right_shift(cell, cb.bit_length() - 1)
        par[4:5] = (pid_ref[...] * ca + along).astype(F32)
        par[5:6] = across.astype(F32)
        number = lax.broadcasted_iota(jnp.int32, (1, exit_rows), 1)
        half_cb = cb // 2
        par[6:7] = jnp.bitwise_and(number, half_cb - 1).astype(F32)
        par[7:8] = (jnp.right_shift(number, half_cb.bit_length() - 1) + 1).astype(F32)
        places = lax.broadcasted_iota(jnp.int32, (SLOTS, exit_rows), 0).astype(F32)
        in_slot[...] = (slot == places).astype(BF16)
        group = 16
        label = jnp.right_shift(lax.broadcasted_iota(jnp.int32, (group * 8, exit_rows), 0), 3)

        @pl.loop(0, owners // group)
        def _(b):
            picks[pl.ds(pl.multiple_of(b * group * 8, group * 8), group * 8)] = (
                owner == label + b * group
            ).astype(BF16)

        halve = jnp.where(
            jnp.right_shift(lax.broadcasted_iota(jnp.int32, (cb, cb // 2), 0), 1)
            == lax.broadcasted_iota(jnp.int32, (cb, cb // 2), 1),
            0.25,
            0.0,
        ).astype(BF16)

        layers = sections // 4
        plane_row = lax.broadcasted_iota(jnp.int32, (ca, cb), 0)
        plane_lane = lax.broadcasted_iota(jnp.int32, (ca, cb), 1)

        def plane(k):
            tiles = fbuf[pl.ds(k * 2 * ca, 2 * ca), :].reshape(ca // 8, 2, 8, LANES)
            return jnp.concatenate([tiles[:, h].reshape(ca, LANES) for h in range(2)], axis=1)

        def plane_lap(c):
            up = jnp.where(plane_row == 0, 0.0, pltpu.roll(c, 1, 0))
            down = jnp.where(plane_row == ca - 1, 0.0, pltpu.roll(c, ca - 1, 0))
            left = jnp.where(plane_lane == 0, 0.0, pltpu.roll(c, 1, 1))
            right = jnp.where(plane_lane == cb - 1, 0.0, pltpu.roll(c, cb - 1, 1))
            return up + down + (left + right) - 4.0 * c

        last = [v * layers + layers - 1 for v in range(4)]
        d, m, q, e = (plane(k) for k in last)
        if layers > 1:
            dm, dq, de = (x - plane(k - 1) for x, k in zip((m, q, e), last[1:]))
        else:
            dm, dq, de = m, q, e
        relaxing = relax_rate / (1.0 + d * d)
        skew = e - 2.0 * q
        new_flux = m - cfl_nozzle * (dm + dq) + diffusion * plane_lap(m)
        new_skew = (
            skew
            - cfl_nozzle * (de - 2.0 * dq)
            - (2.0 * relax_step) * relaxing * (e - q)
            + diffusion * plane_lap(skew)
        )
        planes = jnp.concatenate([new_flux, new_skew, diffusion * m, diffusion * skew], axis=0)
        paired = planes + pltpu.roll(planes, 4 * ca - 1, 0)
        edge_rows = jnp.concatenate(
            [planes[(2 + v) * ca + a : (2 + v) * ca + a + 1] for a in (0, ca - 1) for v in range(2)]
            + [jnp.zeros((4, cb), F32)],
            axis=0,
        )
        summed = jnp.concatenate([paired[: 2 * ca], edge_rows], axis=0)
        hi = summed.astype(BF16)
        rest = summed - hi.astype(F32)
        mid, low = split_hi_lo(rest)
        count = 2 * ca + 8
        sums = jnp.dot(
            jnp.concatenate([hi, mid, low], axis=0), halve, preferred_element_type=F32
        )
        coarse = sums[:count] + sums[count : 2 * count] + sums[2 * count :]
        for v in range(2):
            for k, part in enumerate(split_hi_lo(coarse[v * ca : (v + 1) * ca])):
                part = part.astype(F32)
                for i in range(ca // 2):
                    par[2 * v + k : 2 * v + k + 1, i * (cb // 2) : (i + 1) * (cb // 2)] = part[
                        2 * i : 2 * i + 1
                    ]
        side_hi, side_lo = split_hi_lo(0.25 * paired[2 * ca :])
        lane = lax.broadcasted_iota(jnp.int32, (8, cb), 1)
        line = lax.broadcasted_iota(jnp.int32, (8, cb), 0)
        ends = jnp.logical_or(
            jnp.logical_and(line == 0, lane == 0), jnp.logical_and(line == 1, lane == cb - 1)
        ).astype(BF16)
        side = dot_last(ends, jnp.concatenate([side_hi, side_lo], axis=0))
        edge_hi, edge_lo = split_hi_lo(coarse[2 * ca :])
        edge_hi, edge_lo = edge_hi.astype(F32), edge_lo.astype(F32)
        edges = jnp.concatenate(
            [x[n : n + 1] for n in range(4) for x in (edge_hi, edge_lo)] + [side], axis=0
        ).astype(BF16)

        values = par[...].astype(BF16)
        tiled = jnp.concatenate([values] * group, axis=0)

        @pl.loop(0, owners // group)
        def _(b):
            picked = tiled * picks[pl.ds(pl.multiple_of(b * group * 8, group * 8), group * 8)]
            packed = dot_last(picked, in_slot[...]).reshape(group, 8, SLOTS)
            send_buf[pl.ds(b * group, group)] = jnp.concatenate(
                [
                    packed[:, :, :LANES].astype(BF16),
                    packed[:, :, LANES:].astype(BF16),
                    jnp.broadcast_to(edges[None], (group, 16, LANES)),
                ],
                axis=1,
            )

        pl.semaphore_wait(barrier, near + owners)

        @pl.loop(0, owners)
        def _(k):
            o = lax.rem(k + me, owners)
            pltpu.make_async_remote_copy(
                src_ref=send_buf.at[o],
                dst_ref=recv_buf.at[me],
                send_sem=row_send.at[o],
                recv_sem=row_recv.at[me],
                device_id=(1, o // n_plane, o % n_plane),
                device_id_type=MESH,
            ).start()

        extract_columns()
        start_halo((0, 1, 2, 3))
        fill_rows()
        finish_halo()

        @pl.loop(0, ca // CHUNK)
        def _(step):
            for t in range(CHUNK):
                a = step * CHUNK + t
                c, _, lap = neighbours(a)
                back = jnp.where(jnp.bitwise_and(col_row, layers - 1) == 0, 0.0, pltpu.roll(c, 1, 0))
                du = c - back
                d, m, q, e = (c[v * layers : (v + 1) * layers] for v in range(4))
                dm, dq, de = (du[v * layers : (v + 1) * layers] for v in (1, 2, 3))
                relaxing = relax_rate / (1.0 + d * d)
                fresh = diffusion * lap + jnp.concatenate(
                    [
                        d - cfl_nozzle * dm,
                        m - cfl_nozzle * (dm + dq),
                        q + relax_step * relaxing * (e - q) - cfl_nozzle * dq,
                        e - cfl_nozzle * de,
                    ],
                    axis=0,
                )
                scatter_row(a, fresh)

        @pl.loop(0, owners)
        def _(o):
            pltpu.make_async_remote_copy(
                src_ref=send_buf.at[o],
                dst_ref=recv_buf.at[me],
                send_sem=row_send.at[o],
                recv_sem=row_recv.at[me],
                device_id=(1, o // n_plane, o % n_plane),
                device_id_type=MESH,
            ).wait_send()

    @pl.when(g == 1)
    def _():
        extract_columns()
        pl.semaphore_wait(barrier, near)
        start_halo((0, 1, 2, 3))
        fill_rows()
        for copy in spray_args:
            copy.wait()
        folded = jnp.dot(coal_ref[...], fold[...], preferred_element_type=F32).astype(BF16)
        evap = jnp.zeros((sections, cb), F32)
        for k in range(sections):
            evap = jnp.where(col_row == k, evap_ref[k], evap)
        speeds = 0.2 + 0.5 * col_row.astype(F32) / (sections - 1)

        finish_halo()

        @pl.loop(0, ca // CHUNK)
        def _(step):
            parts = []
            for t in range(CHUNK):
                c, up, lap = neighbours(step * CHUNK + t)
                lost = evap * c
                gained = jnp.where(
                    col_row == sections - 1, 0.0, pltpu.roll(lost, sections - 1, 0)
                )
                parts.append(c - speeds * (c - up) + diffusion * lap - lost + gained)
            moved = jnp.concatenate(parts, axis=1)
            first = jnp.dot(folded, pair_terms(moved), preferred_element_type=F32)
            middle = moved + (0.5 * collide_step) * first
            second = jnp.dot(folded, pair_terms(middle), preferred_element_type=F32)
            mixed = moved + collide_step * second
            for t in range(CHUNK):
                scatter_row(step * CHUNK + t, mixed[:, t * cb : (t + 1) * cb])

        @pl.loop(0, owners)
        def _(o):
            pltpu.make_async_remote_copy(
                src_ref=send_buf.at[o],
                dst_ref=recv_buf.at[o],
                send_sem=row_send.at[o],
                recv_sem=row_recv.at[o],
                device_id=(0, s, p),
                device_id_type=MESH,
            ).wait_recv()


def finish(
    n_plane, owners, sections, ca, cb,
    held, rows_in, width_hbm,
    out_hbm,
    obuf, flat, par, mass, right, mask, width_ref, arg_sem, out_sem,
):
    plumes = width_ref.shape[0]
    rows = sections * ca
    g = lax.axis_index("group")

    @pl.when(g == 0)
    def _():
        copy = pltpu.make_async_copy(held, out_hbm, out_sem.at[0])
        copy.start()
        copy.wait()

    @pl.when(g == 1)
    def _():
        fetch = pltpu.make_async_copy(width_hbm, width_ref, arg_sem)
        fetch.start()
        pad = n_plane * 32
        half_cb = cb // 2
        flat[pl.ds(0, pad)] = jnp.zeros((pad, LANES), F32)
        flat[pl.ds(pad + owners * 32, pad)] = jnp.zeros((pad, LANES), F32)

        @pl.loop(0, owners // 8)
        def _(b):
            at = pl.ds(pl.multiple_of(pad + b * 256, 128), 256)
            flat[at] = rows_in[pl.ds(b * 8, 8)].astype(F32).reshape(256, LANES)

        fetch.wait()
        sub = lax.broadcasted_iota(jnp.int32, (8, LANES), 0)

        @pl.loop(0, owners // 8)
        def _(b):
            def take(shift, line):
                return flat[pl.ds(pad + (b * 8 + shift) * 32 + line, 8, stride=32), :]

            plane_at = lax.rem(b * 8 + sub, n_plane)
            first_plane = plane_at == 0
            last_plane = plane_at == n_plane - 1
            above = [take(-n_plane, 16 + 4 + x) for x in range(4)]
            below = [take(n_plane, 16 + x) for x in range(4)]
            before = jnp.where(first_plane, 0.0, take(-1, 16 + 9))
            behind = jnp.where(last_plane, 0.0, take(1, 16 + 8))

            def pick(table, index):
                return jnp.take_along_axis(table, index, axis=1, mode="promise_in_bounds")

            for h in range(2):
                got = [take(0, h * 8 + x) for x in range(8)]
                spot = got[6].astype(jnp.int32)
                line = got[7].astype(jnp.int32)
                slot_line = 2 * jnp.maximum(line - 1, 0)
                flux = got[0] + got[1]
                skew = got[2] + got[3]
                for tables, here in ((above, line == 1), (below, line == ca // 2)):
                    f0, f1, u0, u1 = (pick(table, spot) for table in tables)
                    flux += jnp.where(here, f0 + f1, 0.0)
                    skew += jnp.where(here, u0 + u1, 0.0)
                for table, here in ((before, spot == 0), (behind, spot == half_cb - 1)):
                    f0, u0, f1, u1 = (pick(table, slot_line + ca * x) for x in range(4))
                    flux += jnp.where(here, f0 + f1, 0.0)
                    skew += jnp.where(here, u0 + u1, 0.0)
                code = got[4].astype(jnp.int32)
                plume = jnp.right_shift(code, ca.bit_length() - 1)
                spread = jnp.full((8, LANES), width_ref[0], F32)
                for k in range(1, plumes):
                    spread = jnp.where(plume == k, width_ref[k], spread)
                values = (
                    jnp.where(line > 0, jnp.sqrt(1.0 + flux * flux), 0.0),
                    (sections - 1) * jax.nn.sigmoid(skew),
                    1.0 / spread,
                    jnp.bitwise_and(code, ca - 1).astype(F32),
                    got[5],
                )
                for x, value in enumerate(values):
                    par[x, pl.ds(pl.multiple_of(b * 8, 8), 8), h * LANES : (h + 1) * LANES] = value

        level = lax.broadcasted_iota(jnp.int32, (sections, SLOTS), 0).astype(F32)
        index_a = lax.broadcasted_iota(jnp.int32, (ca, SLOTS), 0).astype(F32)
        index_b = lax.broadcasted_iota(jnp.int32, (cb, SLOTS), 0).astype(F32)

        @pl.loop(0, owners // SOURCES)
        def _(step):
            for t in range(SOURCES):
                o = step * SOURCES + t
                strength, center, inverse, along, across = (
                    par[x, pl.ds(o, 1), :] for x in range(5)
                )
                scaled = (level - center) * inverse
                weights = 1.0 / (1.0 + scaled * scaled)
                at = pl.ds(t * SLOTS, SLOTS)
                mass[:, at] = weights * (strength / jnp.sum(weights, axis=0, keepdims=True))
                mask[:, at] = (along == index_a).astype(BF16)
                right[:, at] = (across == index_b).astype(BF16)
            left = jnp.concatenate(
                [
                    jnp.broadcast_to(mass[k : k + 1], (ca, SOURCES * SLOTS)).astype(BF16) * mask[...]
                    for k in range(sections)
                ],
                axis=0,
            )
            added = dot_last(left, right[...])
            tiles = jnp.stack(
                [added[:, h * LANES : (h + 1) * LANES].reshape(rows // 8, 8, LANES) for h in range(2)],
                axis=1,
            ).reshape(2 * rows, LANES)

            @pl.when(step == 0)
            def _():
                obuf[...] = held[...] + tiles

            @pl.when(step > 0)
            def _():
                obuf[...] += tiles

        store = pltpu.make_async_copy(obuf, out_hbm, out_sem.at[0])
        store.start()
        store.wait()


def body(n_slab, n_plane, fields, evap_rates, coal_kernel, plume_width, owner_map, deposit_cell, plume_ids):
    _, sections, ca, cb = fields.shape
    exit_rows = owner_map.shape[1]
    owners = n_slab * n_plane
    rows = sections * ca
    fold = jnp.asarray(fold_matrix(sections), BF16)
    kept = fold.shape[1]
    hbm = pl.BlockSpec(memory_space=pl.ANY)
    vmem = pl.BlockSpec(memory_space=pltpu.VMEM)
    held, rows_in = pl.pallas_call(
        functools.partial(kernel, n_slab, n_plane, sections, ca, cb, exit_rows),
        out_shape=[
            pltpu.VMEM((2 * rows, LANES), F32),
            pltpu.VMEM((owners, 32, LANES), BF16),
        ],
        in_specs=[hbm] * 7,
        out_specs=[vmem] * 2,
        scratch_shapes=[
            pltpu.VMEM((2 * rows, LANES), F32),
            pltpu.VMEM((ca + 2, sections, cb), F32),
            pltpu.VMEM((2, rows, LANES), F32),
            pltpu.VMEM((sections * sections, kept), BF16),
            pltpu.VMEM((2, 1, rows), F32),
            pltpu.VMEM((2, 1, rows), F32),
            pltpu.VMEM((8, exit_rows), F32),
            pltpu.VMEM((owners, 32, LANES), BF16),
            pltpu.SMEM(evap_rates.shape, F32),
            pltpu.VMEM(coal_kernel.shape, BF16),
            pltpu.VMEM((1, exit_rows), jnp.int32),
            pltpu.VMEM((1, exit_rows), jnp.int32),
            pltpu.VMEM((1, exit_rows), jnp.int32),
            pltpu.VMEM((owners * 8, exit_rows), BF16),
            pltpu.VMEM((SLOTS, exit_rows), BF16),
            pltpu.SemaphoreType.DMA,
            pltpu.SemaphoreType.DMA((4,)),
            pltpu.SemaphoreType.DMA((4,)),
            pltpu.SemaphoreType.DMA((4,)),
            pltpu.SemaphoreType.DMA((owners,)),
            pltpu.SemaphoreType.DMA((owners,)),
        ],
        compiler_params=pltpu.CompilerParams(
            collective_id=0, has_side_effects=True, vmem_limit_bytes=VMEM_BYTES
        ),
    )(
        fields.reshape(rows // 8, 8, 2, LANES).transpose(0, 2, 1, 3).reshape(2 * rows, LANES), evap_rates, coal_kernel, fold,
        owner_map, deposit_cell, plume_ids,
    )
    span = SOURCES * SLOTS
    out = pl.pallas_call(
        functools.partial(finish, n_plane, owners, sections, ca, cb),
        out_shape=jax.ShapeDtypeStruct((2 * rows, LANES), F32),
        in_specs=[vmem, vmem, hbm],
        out_specs=hbm,
        scratch_shapes=[
            pltpu.VMEM((2 * rows, LANES), F32),
            pltpu.VMEM(((owners + 2 * n_plane) * 32, LANES), F32),
            pltpu.VMEM((5, owners, SLOTS), F32),
            pltpu.VMEM((sections, span), F32),
            pltpu.VMEM((cb, span), BF16),
            pltpu.VMEM((ca, span), BF16),
            pltpu.SMEM(plume_width.shape, F32),
            pltpu.SemaphoreType.DMA,
            pltpu.SemaphoreType.DMA((PIECES,)),
        ],
        compiler_params=pltpu.CompilerParams(vmem_limit_bytes=VMEM_BYTES),
    )(
        pltpu.with_memory_space_constraint(held, pltpu.VMEM),
        pltpu.with_memory_space_constraint(rows_in, pltpu.VMEM),
        plume_width,
    )
    out = out.reshape(rows // 8, 2, 8, LANES).transpose(0, 2, 1, 3)
    return out.reshape(1, sections, ca, cb)


def solution(mesh):
    return jax.shard_map(
        functools.partial(body, mesh.shape["slab"], mesh.shape["plane"]),
        mesh=mesh,
        in_specs=(
            P("group", None, "slab", "plane"),
            P(),
            P(),
            P(),
            P(("slab", "plane"), None),
            P(("slab", "plane"), None),
            P(("slab", "plane"), None),
        ),
        out_specs=P("group", None, "slab", "plane"),
        check_vma=False,
    )
```

```python
import functools

import jax
import jax.numpy as jnp
import numpy as np
from jax import lax
from jax.experimental import pallas as pl
from jax.experimental.pallas import tpu as pltpu
from jax.sharding import PartitionSpec as P

MESH = pl.DeviceIdType.MESH
F32 = jnp.float32
BF16 = jnp.bfloat16
LANES = 128
SLOTS = 256
CHUNK = 4
PAD = 8
SOURCES = 4
PIECES = 2
VMEM_BYTES = 56 * 1024 * 1024

cfl_nozzle = 0.35
diffusion = 0.2
relax_rate = 5.0
relax_step = 0.1
collide_step = 0.25


def fold_matrix(sections):
    kept = [(i, j) for i in range(sections) for j in range(i // 8 * 8, sections)]
    fold = np.zeros((sections * sections, len(kept)), np.float32)
    for q, (i, j) in enumerate(kept):
        fold[i * sections + j, q] = 1.0
        if j // 8 > i // 8:
            fold[j * sections + i, q] = 1.0
    return fold


def pair_terms(m):
    sections, width = m.shape
    pieces = []
    for i in range(sections):
        low = i // 8 * 8
        pieces.append(jnp.broadcast_to(m[i : i + 1], (sections - low, width)) * m[low:])
    return jnp.concatenate(pieces, axis=0).astype(BF16)


def split_hi_lo(x):
    hi = x.astype(BF16)
    lo = (x - hi.astype(F32)).astype(BF16)
    return hi, lo


def dot_last(a, b):
    return lax.dot_general(a, b, (((1,), (1,)), ((), ())), preferred_element_type=F32)


def kernel(
    n_slab, n_plane, sections, ca, cb, exit_rows,
    fields_hbm, evap_hbm, coal_hbm, fold_hbm, owner_hbm, cell_hbm, pid_hbm,
    obuf, recv_buf,
    fbuf, tbuf, edge_in, hbuf, fold, cols_out, cols_in, par, send_buf,
    evap_ref, coal_ref, owner_ref, cell_ref, pid_ref, picks, in_slot,
    in_sem, arg_sem, halo_send, halo_recv, row_send, row_recv,
):
    owners = n_slab * n_plane
    rows = sections * ca
    g = lax.axis_index("group")
    s = lax.axis_index("slab")
    p = lax.axis_index("plane")
    me = s * n_plane + p

    fpad = fbuf.reshape(sections, 2 * ca + PAD, LANES).at[:, pl.ds(0, 2 * ca), :]
    opad = obuf.reshape(sections, 2 * ca + PAD, LANES).at[:, pl.ds(0, 2 * ca), :]
    load = pltpu.make_async_copy(
        fields_hbm.reshape(sections, 2 * ca, LANES), fpad, in_sem
    )
    load.start()
    nozzle_args = [
        pltpu.make_async_copy(source, target, arg_sem.at[k])
        for k, (source, target) in enumerate(
            ((owner_hbm, owner_ref), (cell_hbm, cell_ref), (pid_hbm, pid_ref))
        )
    ]
    spray_args = [
        pltpu.make_async_copy(source, target, arg_sem.at[k])
        for k, (source, target) in enumerate(
            ((evap_hbm, evap_ref), (coal_hbm, coal_ref), (fold_hbm, fold))
        )
    ]

    @pl.when(g == 0)
    def _():
        for copy in nozzle_args:
            copy.start()

    @pl.when(g == 1)
    def _():
        for copy in spray_args:
            copy.start()

    barrier = pltpu.get_barrier_semaphore()
    sides = [
        (s > 0, (g, s - 1, p)),
        (s < n_slab - 1, (g, s + 1, p)),
        (p > 0, (g, s, p - 1)),
        (p < n_plane - 1, (g, s, p + 1)),
    ]
    near = 0
    for there, target in sides:
        near = near + there.astype(jnp.int32)

        @pl.when(there)
        def _():
            pl.semaphore_signal(barrier, inc=1, device_id=target, device_id_type=MESH)

    @pl.when(g == 1)
    def _():
        @pl.loop(0, owners)
        def _(o):
            pl.semaphore_signal(
                barrier, inc=1, device_id=(0, o // n_plane, o % n_plane), device_id_type=MESH
            )

    load.wait()

    def lines(a, h):
        return pl.ds(a // 8 * 16 + h * 8 + a % 8, sections, stride=2 * ca + PAD)

    def gather_row(ref, a):
        return jnp.concatenate([ref[lines(a, h), :] for h in range(2)], axis=1)

    def half(ref, h):
        return ref[...].reshape(rows // 8, 2, 8, LANES)[:, h].reshape(rows, LANES)

    def halo(kind, target):
        source, landing = (
            (tbuf.at[ca], edge_in.at[0]),
            (tbuf.at[1], edge_in.at[1]),
            (cols_out.at[1], cols_in.at[0]),
            (cols_out.at[0], cols_in.at[1]),
        )[kind]
        return pltpu.make_async_remote_copy(
            src_ref=source,
            dst_ref=landing,
            send_sem=halo_send.at[kind],
            recv_sem=halo_recv.at[kind],
            device_id=target,
            device_id_type=MESH,
        )

    outgoing = (sides[1], sides[0], sides[3], sides[2])
    def start_halo(kinds):
        for kind in kinds:

            @pl.when(outgoing[kind][0])
            def _():
                halo(kind, outgoing[kind][1]).start()

    def extract_columns():
        for a in (0, ca - 1):
            tbuf[a + 1] = gather_row(fbuf, a)

        lane = lax.broadcasted_iota(jnp.int32, (8, LANES), 1)
        for h, at in ((0, 0), (1, LANES - 1)):
            select = (lane == at).astype(BF16)
            cols_out[h] = dot_last(select, half(fpad, h).astype(BF16))[0:1]

    def fill_rows():
        @pl.loop(1, ca - 1)
        def _(a):
            tbuf[a + 1] = gather_row(fbuf, a)

        for kind, landing in enumerate((edge_in.at[0], edge_in.at[1], cols_in.at[0], cols_in.at[1])):

            @pl.when(jnp.logical_not(sides[kind][0]))
            def _():
                landing[...] = jnp.zeros(landing.shape, F32)

    def wait_halo():
        for kind in range(4):

            @pl.when(outgoing[kind][0])
            def _():
                halo(kind, outgoing[kind][1]).wait_send()

            @pl.when(sides[kind][0])
            def _():
                halo(kind, outgoing[kind][1]).wait_recv()

    def placed_columns():
        sub = lax.broadcasted_iota(jnp.int32, (16, cb), 0)
        lanes = lax.broadcasted_iota(jnp.int32, (16, cb), 1)
        stack = jnp.concatenate([cols_in[0], cols_in[1], jnp.zeros((14, rows), F32)], axis=0)
        place = jnp.logical_or(
            jnp.logical_and(sub == 0, lanes == 0), jnp.logical_and(sub == 1, lanes == cb - 1)
        ).astype(BF16)
        return jnp.dot(stack.T.astype(BF16), place, preferred_element_type=F32)

    col_lane = lax.broadcasted_iota(jnp.int32, (sections, cb), 1)
    col_row = lax.broadcasted_iota(jnp.int32, (sections, cb), 0)

    def column_halo(a):
        return jnp.concatenate(
            [hbuf[h, pl.ds(a, sections, stride=ca + PAD), :] for h in range(2)], axis=1
        )

    def neighbours(a, with_columns):
        c = tbuf[a + 1]
        up = tbuf[a]
        left = jnp.where(col_lane == 0, 0.0, pltpu.roll(c, 1, 1))
        right = jnp.where(col_lane == cb - 1, 0.0, pltpu.roll(c, cb - 1, 1))
        beside = left + right
        if with_columns:
            beside += column_halo(a)
        lap = up + tbuf[a + 2] + beside - 4.0 * c
        return c, up, lap

    def scatter_row(a, value):
        for h in range(2):
            obuf[lines(a, h), :] = value[:, h * LANES : (h + 1) * LANES]

    @pl.when(g == 0)
    def _():
        for copy in nozzle_args:
            copy.wait()
        owner = owner_ref[...]
        slots = []
        below = lax.broadcasted_iota(jnp.int32, (256, 256), 0)
        after = lax.broadcasted_iota(jnp.int32, (256, 256), 1)
        upto = (below <= after).astype(BF16)
        names = lax.broadcasted_iota(jnp.int32, (owners, 256), 0)
        carry = jnp.zeros((owners, 1), F32)
        for j in range(exit_rows // 256):
            hit = (owner[:, j * 256 : (j + 1) * 256] == names).astype(F32)
            count = jnp.dot(hit.astype(BF16), upto, preferred_element_type=F32) + carry
            slots.append(jnp.sum(hit * (count - 1.0), axis=0, keepdims=True))
            carry = count[:, 255:256]
        slot = jnp.concatenate(slots, axis=1)
        cell = cell_ref[...]
        across = jnp.bitwise_and(cell, cb - 1)
        along = jnp.right_shift(cell, cb.bit_length() - 1)
        par[4:5] = (pid_ref[...] * ca + along).astype(F32)
        par[5:6] = across.astype(F32)
        number = lax.broadcasted_iota(jnp.int32, (1, exit_rows), 1)
        half_cb = cb // 2
        par[6:7] = jnp.bitwise_and(number, half_cb - 1).astype(F32)
        par[7:8] = (jnp.right_shift(number, half_cb.bit_length() - 1) + 1).astype(F32)
        places = lax.broadcasted_iota(jnp.int32, (SLOTS, exit_rows), 0).astype(F32)
        in_slot[...] = (slot == places).astype(BF16)
        group = 16
        label = jnp.right_shift(lax.broadcasted_iota(jnp.int32, (group * 8, exit_rows), 0), 3)

        @pl.loop(0, owners // group)
        def _(b):
            picks[pl.ds(pl.multiple_of(b * group * 8, group * 8), group * 8)] = (
                owner == label + b * group
            ).astype(BF16)

        halve = jnp.where(
            jnp.right_shift(lax.broadcasted_iota(jnp.int32, (cb, cb // 2), 0), 1)
            == lax.broadcasted_iota(jnp.int32, (cb, cb // 2), 1),
            0.25,
            0.0,
        ).astype(BF16)

        layers = sections // 4
        plane_row = lax.broadcasted_iota(jnp.int32, (ca, cb), 0)
        plane_lane = lax.broadcasted_iota(jnp.int32, (ca, cb), 1)

        def plane(k):
            tiles = fbuf[pl.ds(k * (2 * ca + PAD), 2 * ca), :].reshape(ca // 8, 2, 8, LANES)
            return jnp.concatenate([tiles[:, h].reshape(ca, LANES) for h in range(2)], axis=1)

        def plane_lap(c):
            up = jnp.where(plane_row == 0, 0.0, pltpu.roll(c, 1, 0))
            down = jnp.where(plane_row == ca - 1, 0.0, pltpu.roll(c, ca - 1, 0))
            left = jnp.where(plane_lane == 0, 0.0, pltpu.roll(c, 1, 1))
            right = jnp.where(plane_lane == cb - 1, 0.0, pltpu.roll(c, cb - 1, 1))
            return up + down + (left + right) - 4.0 * c

        last = [v * layers + layers - 1 for v in range(4)]
        d, m, q, e = (plane(k) for k in last)
        if layers > 1:
            dm, dq, de = (x - plane(k - 1) for x, k in zip((m, q, e), last[1:]))
        else:
            dm, dq, de = m, q, e
        relaxing = relax_rate / (1.0 + d * d)
        skew = e - 2.0 * q
        new_flux = m - cfl_nozzle * (dm + dq) + diffusion * plane_lap(m)
        new_skew = (
            skew
            - cfl_nozzle * (de - 2.0 * dq)
            - (2.0 * relax_step) * relaxing * (e - q)
            + diffusion * plane_lap(skew)
        )
        planes = jnp.concatenate([new_flux, new_skew, diffusion * m, diffusion * skew], axis=0)
        paired = planes + pltpu.roll(planes, 4 * ca - 1, 0)
        edge_rows = jnp.concatenate(
            [planes[(2 + v) * ca + a : (2 + v) * ca + a + 1] for a in (0, ca - 1) for v in range(2)]
            + [jnp.zeros((4, cb), F32)],
            axis=0,
        )
        summed = jnp.concatenate([paired[: 2 * ca], edge_rows], axis=0)
        hi = summed.astype(BF16)
        rest = summed - hi.astype(F32)
        mid, low = split_hi_lo(rest)
        count = 2 * ca + 8
        sums = jnp.dot(
            jnp.concatenate([hi, mid, low], axis=0), halve, preferred_element_type=F32
        )
        coarse = sums[:count] + sums[count : 2 * count] + sums[2 * count :]
        for v in range(2):
            for k, part in enumerate(split_hi_lo(coarse[v * ca : (v + 1) * ca])):
                part = part.astype(F32)
                for i in range(ca // 2):
                    par[2 * v + k : 2 * v + k + 1, i * (cb // 2) : (i + 1) * (cb // 2)] = part[
                        2 * i : 2 * i + 1
                    ]
        side_hi, side_lo = split_hi_lo(0.25 * paired[2 * ca :])
        lane = lax.broadcasted_iota(jnp.int32, (8, cb), 1)
        line = lax.broadcasted_iota(jnp.int32, (8, cb), 0)
        ends = jnp.logical_or(
            jnp.logical_and(line == 0, lane == 0), jnp.logical_and(line == 1, lane == cb - 1)
        ).astype(BF16)
        side = dot_last(ends, jnp.concatenate([side_hi, side_lo], axis=0))
        edge_hi, edge_lo = split_hi_lo(coarse[2 * ca :])
        edge_hi, edge_lo = edge_hi.astype(F32), edge_lo.astype(F32)
        edges = jnp.concatenate(
            [x[n : n + 1] for n in range(4) for x in (edge_hi, edge_lo)] + [side], axis=0
        ).astype(BF16)

        values = par[...].astype(BF16)
        tiled = jnp.concatenate([values] * group, axis=0)

        @pl.loop(0, owners // group)
        def _(b):
            picked = tiled * picks[pl.ds(pl.multiple_of(b * group * 8, group * 8), group * 8)]
            packed = dot_last(picked, in_slot[...]).reshape(group, 8, SLOTS)
            send_buf[pl.ds(b * group, group)] = jnp.concatenate(
                [
                    packed[:, :, :LANES].astype(BF16),
                    packed[:, :, LANES:].astype(BF16),
                    jnp.broadcast_to(edges[None], (group, 16, LANES)),
                ],
                axis=1,
            )

        pl.semaphore_wait(barrier, near + owners)

        @pl.loop(0, owners)
        def _(k):
            o = lax.rem(k + me, owners)
            pltpu.make_async_remote_copy(
                src_ref=send_buf.at[o],
                dst_ref=recv_buf.at[me],
                send_sem=row_send.at[o],
                recv_sem=row_recv.at[me],
                device_id=(1, o // n_plane, o % n_plane),
                device_id_type=MESH,
            ).start()

        extract_columns()
        start_halo((0, 1, 2, 3))
        fill_rows()
        for a in (0, ca + 1):
            tbuf[a] = jnp.zeros((sections, cb), F32)

        @pl.loop(0, ca // CHUNK)
        def _(step):
            for t in range(CHUNK):
                a = step * CHUNK + t
                c, _, lap = neighbours(a, False)
                back = jnp.where(jnp.bitwise_and(col_row, layers - 1) == 0, 0.0, pltpu.roll(c, 1, 0))
                du = c - back
                d, m, q, e = (c[v * layers : (v + 1) * layers] for v in range(4))
                dm, dq, de = (du[v * layers : (v + 1) * layers] for v in (1, 2, 3))
                relaxing = relax_rate / (1.0 + d * d)
                fresh = diffusion * lap + jnp.concatenate(
                    [
                        d - cfl_nozzle * dm,
                        m - cfl_nozzle * (dm + dq),
                        q + relax_step * relaxing * (e - q) - cfl_nozzle * dq,
                        e - cfl_nozzle * de,
                    ],
                    axis=0,
                )
                scatter_row(a, fresh)

        wait_halo()
        placed = diffusion * placed_columns()
        opad[...] += jnp.stack(
            [placed[:, h * LANES : (h + 1) * LANES].reshape(rows // 8, 8, LANES) for h in range(2)],
            axis=1,
        ).reshape(sections, 2 * ca, LANES)
        for side, a in enumerate((0, ca - 1)):
            for h in range(2):
                obuf[lines(a, h), :] += diffusion * edge_in[side, :, h * LANES : (h + 1) * LANES]

        @pl.loop(0, owners)
        def _(o):
            pltpu.make_async_remote_copy(
                src_ref=send_buf.at[o],
                dst_ref=recv_buf.at[me],
                send_sem=row_send.at[o],
                recv_sem=row_recv.at[me],
                device_id=(1, o // n_plane, o % n_plane),
                device_id_type=MESH,
            ).wait_send()

    @pl.when(g == 1)
    def _():
        extract_columns()
        pl.semaphore_wait(barrier, near)
        start_halo((0, 1, 2, 3))
        fill_rows()
        for copy in spray_args:
            copy.wait()
        folded = jnp.dot(coal_ref[...], fold[...], preferred_element_type=F32).astype(BF16)
        evap = jnp.zeros((sections, cb), F32)
        for k in range(sections):
            evap = jnp.where(col_row == k, evap_ref[k], evap)
        speeds = 0.2 + 0.5 * col_row.astype(F32) / (sections - 1)

        wait_halo()
        for side, a in enumerate((0, ca + 1)):
            tbuf[a] = edge_in[side]
        placed = placed_columns()
        for h in range(2):
            hbuf.reshape(2, sections, ca + PAD, LANES)[h, :, pl.ds(0, ca), :] = placed[
                :, h * LANES : (h + 1) * LANES
            ].reshape(sections, ca, LANES)

        @pl.loop(0, ca // CHUNK)
        def _(step):
            parts = []
            for t in range(CHUNK):
                c, up, lap = neighbours(step * CHUNK + t, True)
                lost = evap * c
                gained = jnp.where(
                    col_row == sections - 1, 0.0, pltpu.roll(lost, sections - 1, 0)
                )
                parts.append(c - speeds * (c - up) + diffusion * lap - lost + gained)
            moved = jnp.concatenate(parts, axis=1)
            first = jnp.dot(folded, pair_terms(moved), preferred_element_type=F32)
            middle = moved + (0.5 * collide_step) * first
            second = jnp.dot(folded, pair_terms(middle), preferred_element_type=F32)
            mixed = moved + collide_step * second
            for t in range(CHUNK):
                scatter_row(step * CHUNK + t, mixed[:, t * cb : (t + 1) * cb])

        @pl.loop(0, owners)
        def _(o):
            pltpu.make_async_remote_copy(
                src_ref=send_buf.at[o],
                dst_ref=recv_buf.at[o],
                send_sem=row_send.at[o],
                recv_sem=row_recv.at[o],
                device_id=(0, s, p),
                device_id_type=MESH,
            ).wait_recv()


def finish(
    n_plane, owners, sections, ca, cb,
    held, rows_in, width_hbm,
    out_hbm,
    obuf, flat, par, mass, left_even, left_odd, right_even, right_odd, width_ref, arg_sem, out_sem,
):
    plumes = width_ref.shape[0]
    rows = sections * ca
    g = lax.axis_index("group")
    whole = held.reshape(sections, 2 * ca + PAD, LANES).at[:, pl.ds(0, 2 * ca), :]
    out_whole = out_hbm.reshape(sections, 2 * ca, LANES)

    @pl.when(g == 0)
    def _():
        copy = pltpu.make_async_copy(whole, out_whole, out_sem.at[0])
        copy.start()
        copy.wait()

    @pl.when(g == 1)
    def _():
        fetch = pltpu.make_async_copy(width_hbm, width_ref, arg_sem)
        fetch.start()
        fill = pltpu.make_async_copy(whole, obuf, out_sem.at[PIECES])
        fill.start()
        pad = n_plane * 32
        half_cb = cb // 2
        flat[pl.ds(0, pad)] = jnp.zeros((pad, LANES), F32)
        flat[pl.ds(pad + owners * 32, pad)] = jnp.zeros((pad, LANES), F32)

        @pl.loop(0, owners // 8)
        def _(b):
            at = pl.ds(pl.multiple_of(pad + b * 256, 128), 256)
            flat[at] = rows_in[pl.ds(b * 8, 8)].astype(F32).reshape(256, LANES)

        fetch.wait()
        sub = lax.broadcasted_iota(jnp.int32, (8, LANES), 0)

        @pl.loop(0, owners // 8)
        def _(b):
            def take(shift, line):
                return flat[pl.ds(pad + (b * 8 + shift) * 32 + line, 8, stride=32), :]

            plane_at = lax.rem(b * 8 + sub, n_plane)
            first_plane = plane_at == 0
            last_plane = plane_at == n_plane - 1
            above = [take(-n_plane, 16 + 4 + x) for x in range(4)]
            below = [take(n_plane, 16 + x) for x in range(4)]
            before = jnp.where(first_plane, 0.0, take(-1, 16 + 9))
            behind = jnp.where(last_plane, 0.0, take(1, 16 + 8))

            def pick(table, index):
                return jnp.take_along_axis(table, index, axis=1, mode="promise_in_bounds")

            for h in range(2):
                got = [take(0, h * 8 + x) for x in range(8)]
                spot = got[6].astype(jnp.int32)
                line = got[7].astype(jnp.int32)
                slot_line = 2 * jnp.maximum(line - 1, 0)
                flux = got[0] + got[1]
                skew = got[2] + got[3]
                for tables, here in ((above, line == 1), (below, line == ca // 2)):
                    f0, f1, u0, u1 = (pick(table, spot) for table in tables)
                    flux += jnp.where(here, f0 + f1, 0.0)
                    skew += jnp.where(here, u0 + u1, 0.0)
                for table, here in ((before, spot == 0), (behind, spot == half_cb - 1)):
                    f0, u0, f1, u1 = (pick(table, slot_line + ca * x) for x in range(4))
                    flux += jnp.where(here, f0 + f1, 0.0)
                    skew += jnp.where(here, u0 + u1, 0.0)
                code = got[4].astype(jnp.int32)
                plume = jnp.right_shift(code, ca.bit_length() - 1)
                spread = jnp.full((8, LANES), width_ref[0], F32)
                for k in range(1, plumes):
                    spread = jnp.where(plume == k, width_ref[k], spread)
                values = (
                    jnp.where(line > 0, jnp.sqrt(1.0 + flux * flux), 0.0),
                    (sections - 1) * jax.nn.sigmoid(skew),
                    1.0 / spread,
                    jnp.bitwise_and(code, ca - 1).astype(F32),
                    got[5],
                )
                for x, value in enumerate(values):
                    par[x, pl.ds(pl.multiple_of(b * 8, 8), 8), h * LANES : (h + 1) * LANES] = value

        span = SOURCES * SLOTS
        level = lax.broadcasted_iota(jnp.int32, (sections, span), 0).astype(F32)
        index_a = lax.broadcasted_iota(jnp.int32, (ca, span), 0).astype(F32)
        index_b = lax.broadcasted_iota(jnp.int32, (cb, span), 0).astype(F32)

        def build(step, left, right):
            strength, center, inverse, along, across = (
                jnp.concatenate(
                    [par[x, pl.ds(step * SOURCES + t, 1), :] for t in range(SOURCES)], axis=1
                )
                for x in range(5)
            )
            scaled = (level - center) * inverse
            weights = 1.0 / (1.0 + scaled * scaled)
            mass[...] = weights * (strength / jnp.sum(weights, axis=0, keepdims=True))
            mask = (along == index_a).astype(BF16)
            right[...] = (across == index_b).astype(BF16)
            for k in range(sections):
                left[k * ca : (k + 1) * ca] = (
                    jnp.broadcast_to(mass[k : k + 1], (ca, span)).astype(BF16) * mask
                )

        def add(left, right, first, count):
            added = dot_last(left[first * ca : (first + count) * ca], right[...])
            tiles = jnp.stack(
                [
                    added[:, h * LANES : (h + 1) * LANES].reshape(count * ca // 8, 8, LANES)
                    for h in range(2)
                ],
                axis=1,
            )
            obuf[first : first + count] += tiles.reshape(count, 2 * ca, LANES)

        build(0, left_even, right_even)
        fill.wait()
        steps = owners // SOURCES

        @pl.loop(0, steps // 2 - 1)
        def _(i):
            add(left_even, right_even, 0, sections)
            build(2 * i + 1, left_odd, right_odd)
            add(left_odd, right_odd, 0, sections)
            build(2 * i + 2, left_even, right_even)

        add(left_even, right_even, 0, sections)
        build(steps - 1, left_odd, right_odd)
        each = sections // PIECES
        stores = []
        for c in range(PIECES):
            add(left_odd, right_odd, c * each, each)
            at = pl.ds(c * each, each)
            stores.append(
                pltpu.make_async_copy(obuf.at[at], out_whole.at[at], out_sem.at[c])
            )
            stores[-1].start()
        for store in stores:
            store.wait()


def body(n_slab, n_plane, fields, evap_rates, coal_kernel, plume_width, owner_map, deposit_cell, plume_ids):
    _, sections, ca, cb = fields.shape
    exit_rows = owner_map.shape[1]
    owners = n_slab * n_plane
    rows = sections * ca
    fold = jnp.asarray(fold_matrix(sections), BF16)
    kept = fold.shape[1]
    hbm = pl.BlockSpec(memory_space=pl.ANY)
    vmem = pl.BlockSpec(memory_space=pltpu.VMEM)
    held, rows_in = pl.pallas_call(
        functools.partial(kernel, n_slab, n_plane, sections, ca, cb, exit_rows),
        out_shape=[
            pltpu.VMEM((2 * rows + sections * PAD, LANES), F32),
            pltpu.VMEM((owners, 32, LANES), BF16),
        ],
        in_specs=[hbm] * 7,
        out_specs=[vmem] * 2,
        scratch_shapes=[
            pltpu.VMEM((2 * rows + sections * PAD, LANES), F32),
            pltpu.VMEM((ca + 2, sections, cb), F32),
            pltpu.VMEM((2, sections, cb), F32),
            pltpu.VMEM((2, rows + sections * PAD, LANES), F32),
            pltpu.VMEM((sections * sections, kept), BF16),
            pltpu.VMEM((2, 1, rows), F32),
            pltpu.VMEM((2, 1, rows), F32),
            pltpu.VMEM((8, exit_rows), F32),
            pltpu.VMEM((owners, 32, LANES), BF16),
            pltpu.SMEM(evap_rates.shape, F32),
            pltpu.VMEM(coal_kernel.shape, BF16),
            pltpu.VMEM((1, exit_rows), jnp.int32),
            pltpu.VMEM((1, exit_rows), jnp.int32),
            pltpu.VMEM((1, exit_rows), jnp.int32),
            pltpu.VMEM((owners * 8, exit_rows), BF16),
            pltpu.VMEM((SLOTS, exit_rows), BF16),
            pltpu.SemaphoreType.DMA,
            pltpu.SemaphoreType.DMA((4,)),
            pltpu.SemaphoreType.DMA((4,)),
            pltpu.SemaphoreType.DMA((4,)),
            pltpu.SemaphoreType.DMA((owners,)),
            pltpu.SemaphoreType.DMA((owners,)),
        ],
        compiler_params=pltpu.CompilerParams(
            collective_id=0, has_side_effects=True, vmem_limit_bytes=VMEM_BYTES
        ),
    )(
        fields.reshape(rows // 8, 8, 2, LANES).transpose(0, 2, 1, 3).reshape(2 * rows, LANES), evap_rates, coal_kernel, fold,
        owner_map, deposit_cell, plume_ids,
    )
    span = SOURCES * SLOTS
    out = pl.pallas_call(
        functools.partial(finish, n_plane, owners, sections, ca, cb),
        out_shape=jax.ShapeDtypeStruct((2 * rows, LANES), F32),
        in_specs=[vmem, vmem, hbm],
        out_specs=hbm,
        scratch_shapes=[
            pltpu.VMEM((sections, 2 * ca, LANES), F32),
            pltpu.VMEM(((owners + 2 * n_plane) * 32, LANES), F32),
            pltpu.VMEM((5, owners, SLOTS), F32),
            pltpu.VMEM((sections, span), F32),
            pltpu.VMEM((rows, span), BF16),
            pltpu.VMEM((rows, span), BF16),
            pltpu.VMEM((cb, span), BF16),
            pltpu.VMEM((cb, span), BF16),
            pltpu.SMEM(plume_width.shape, F32),
            pltpu.SemaphoreType.DMA,
            pltpu.SemaphoreType.DMA((PIECES + 1,)),
        ],
        compiler_params=pltpu.CompilerParams(vmem_limit_bytes=VMEM_BYTES),
    )(
        pltpu.with_memory_space_constraint(held, pltpu.VMEM),
        pltpu.with_memory_space_constraint(rows_in, pltpu.VMEM),
        plume_width,
    )
    out = out.reshape(rows // 8, 2, 8, LANES).transpose(0, 2, 1, 3)
    return out.reshape(1, sections, ca, cb)


def solution(mesh):
    return jax.shard_map(
        functools.partial(body, mesh.shape["slab"], mesh.shape["plane"]),
        mesh=mesh,
        in_specs=(
            P("group", None, "slab", "plane"),
            P(),
            P(),
            P(),
            P(("slab", "plane"), None),
            P(("slab", "plane"), None),
            P(("slab", "plane"), None),
        ),
        out_specs=P("group", None, "slab", "plane"),
        check_vma=False,
    )
```

```python
import functools

import jax
import jax.numpy as jnp
import numpy as np
from jax import lax
from jax.experimental import pallas as pl
from jax.experimental.pallas import tpu as pltpu
from jax.sharding import PartitionSpec as P

MESH = pl.DeviceIdType.MESH
F32 = jnp.float32
BF16 = jnp.bfloat16
LANES = 128
SLOTS = 256
CHUNK = 8
PAD = 8
SOURCES = 4
PIECES = 2
VMEM_BYTES = 56 * 1024 * 1024

cfl_nozzle = 0.35
diffusion = 0.2
relax_rate = 5.0
relax_step = 0.1
collide_step = 0.25


def fold_matrix(sections):
    kept = [(i, j) for i in range(sections) for j in range(i // 8 * 8, sections)]
    fold = np.zeros((sections * sections, len(kept)), np.float32)
    for q, (i, j) in enumerate(kept):
        fold[i * sections + j, q] = 1.0
        if j // 8 > i // 8:
            fold[j * sections + i, q] = 1.0
    return fold


def pair_terms(m):
    sections, width = m.shape
    pieces = []
    for i in range(sections):
        low = i // 8 * 8
        pieces.append(jnp.broadcast_to(m[i : i + 1], (sections - low, width)) * m[low:])
    return jnp.concatenate(pieces, axis=0).astype(BF16)


def split_hi_lo(x):
    hi = x.astype(BF16)
    lo = (x - hi.astype(F32)).astype(BF16)
    return hi, lo


def dot_last(a, b):
    return lax.dot_general(a, b, (((1,), (1,)), ((), ())), preferred_element_type=F32)


def kernel(
    n_slab, n_plane, sections, ca, cb, exit_rows,
    fields_hbm, evap_hbm, coal_hbm, fold_hbm, owner_hbm, cell_hbm, pid_hbm,
    obuf, recv_buf,
    fbuf, tbuf, edge_in, hbuf, fold, cols_out, cols_in, par, send_buf,
    evap_ref, coal_ref, owner_ref, cell_ref, pid_ref, picks, in_slot,
    in_sem, arg_sem, halo_send, halo_recv, row_send, row_recv,
):
    owners = n_slab * n_plane
    rows = sections * ca
    g = lax.axis_index("group")
    s = lax.axis_index("slab")
    p = lax.axis_index("plane")
    me = s * n_plane + p

    fpad = fbuf.reshape(sections, 2 * ca + PAD, LANES).at[:, pl.ds(0, 2 * ca), :]
    opad = obuf.reshape(sections, 2 * ca + PAD, LANES).at[:, pl.ds(0, 2 * ca), :]
    load = pltpu.make_async_copy(
        fields_hbm.reshape(sections, 2 * ca, LANES), fpad, in_sem
    )
    load.start()
    nozzle_args = [
        pltpu.make_async_copy(source, target, arg_sem.at[k])
        for k, (source, target) in enumerate(
            ((owner_hbm, owner_ref), (cell_hbm, cell_ref), (pid_hbm, pid_ref))
        )
    ]
    spray_args = [
        pltpu.make_async_copy(source, target, arg_sem.at[k])
        for k, (source, target) in enumerate(
            ((evap_hbm, evap_ref), (coal_hbm, coal_ref), (fold_hbm, fold))
        )
    ]

    @pl.when(g == 0)
    def _():
        for copy in nozzle_args:
            copy.start()

    @pl.when(g == 1)
    def _():
        for copy in spray_args:
            copy.start()

    barrier = pltpu.get_barrier_semaphore()
    sides = [
        (s > 0, (g, s - 1, p)),
        (s < n_slab - 1, (g, s + 1, p)),
        (p > 0, (g, s, p - 1)),
        (p < n_plane - 1, (g, s, p + 1)),
    ]
    near = 0
    for there, target in sides:
        near = near + there.astype(jnp.int32)

        @pl.when(there)
        def _():
            pl.semaphore_signal(barrier, inc=1, device_id=target, device_id_type=MESH)

    @pl.when(g == 1)
    def _():
        @pl.loop(0, owners)
        def _(o):
            pl.semaphore_signal(
                barrier, inc=1, device_id=(0, o // n_plane, o % n_plane), device_id_type=MESH
            )

    load.wait()

    def lines(a, h):
        return pl.ds(a // 8 * 16 + h * 8 + a % 8, sections, stride=2 * ca + PAD)

    def gather_row(ref, a):
        return jnp.concatenate([ref[lines(a, h), :] for h in range(2)], axis=1)

    def half(ref, h):
        return ref[...].reshape(rows // 8, 2, 8, LANES)[:, h].reshape(rows, LANES)

    def halo(kind, target):
        source, landing = (
            (tbuf.at[ca], edge_in.at[0]),
            (tbuf.at[1], edge_in.at[1]),
            (cols_out.at[1], cols_in.at[0]),
            (cols_out.at[0], cols_in.at[1]),
        )[kind]
        return pltpu.make_async_remote_copy(
            src_ref=source,
            dst_ref=landing,
            send_sem=halo_send.at[kind],
            recv_sem=halo_recv.at[kind],
            device_id=target,
            device_id_type=MESH,
        )

    outgoing = (sides[1], sides[0], sides[3], sides[2])
    def start_halo(kinds):
        for kind in kinds:

            @pl.when(outgoing[kind][0])
            def _():
                halo(kind, outgoing[kind][1]).start()

    def extract_columns():
        for a in (0, ca - 1):
            tbuf[a + 1] = gather_row(fbuf, a)

        lane = lax.broadcasted_iota(jnp.int32, (8, LANES), 1)
        for h, at in ((0, 0), (1, LANES - 1)):
            select = (lane == at).astype(BF16)
            cols_out[h] = dot_last(select, half(fpad, h).astype(BF16))[0:1]

    def fill_rows():
        @pl.loop(1, ca - 1)
        def _(a):
            tbuf[a + 1] = gather_row(fbuf, a)

        for kind, landing in enumerate((edge_in.at[0], edge_in.at[1], cols_in.at[0], cols_in.at[1])):

            @pl.when(jnp.logical_not(sides[kind][0]))
            def _():
                landing[...] = jnp.zeros(landing.shape, F32)

    def wait_halo():
        for kind in range(4):

            @pl.when(outgoing[kind][0])
            def _():
                halo(kind, outgoing[kind][1]).wait_send()

            @pl.when(sides[kind][0])
            def _():
                halo(kind, outgoing[kind][1]).wait_recv()

    def placed_columns():
        sub = lax.broadcasted_iota(jnp.int32, (16, cb), 0)
        lanes = lax.broadcasted_iota(jnp.int32, (16, cb), 1)
        stack = jnp.concatenate([cols_in[0], cols_in[1], jnp.zeros((14, rows), F32)], axis=0)
        place = jnp.logical_or(
            jnp.logical_and(sub == 0, lanes == 0), jnp.logical_and(sub == 1, lanes == cb - 1)
        ).astype(BF16)
        return jnp.dot(stack.T.astype(BF16), place, preferred_element_type=F32)

    col_lane = lax.broadcasted_iota(jnp.int32, (sections, cb), 1)
    col_row = lax.broadcasted_iota(jnp.int32, (sections, cb), 0)

    def column_halo(a):
        return jnp.concatenate(
            [hbuf[h, pl.ds(a, sections, stride=ca + PAD), :] for h in range(2)], axis=1
        )

    def neighbours(a, with_columns):
        c = tbuf[a + 1]
        up = tbuf[a]
        left = jnp.where(col_lane == 0, 0.0, pltpu.roll(c, 1, 1))
        right = jnp.where(col_lane == cb - 1, 0.0, pltpu.roll(c, cb - 1, 1))
        beside = left + right
        if with_columns:
            beside += column_halo(a)
        lap = up + tbuf[a + 2] + beside - 4.0 * c
        return c, up, lap

    def scatter_row(a, value):
        for h in range(2):
            obuf[lines(a, h), :] = value[:, h * LANES : (h + 1) * LANES]

    @pl.when(g == 0)
    def _():
        for copy in nozzle_args:
            copy.wait()
        owner = owner_ref[...]
        slots = []
        below = lax.broadcasted_iota(jnp.int32, (256, 256), 0)
        after = lax.broadcasted_iota(jnp.int32, (256, 256), 1)
        upto = (below <= after).astype(BF16)
        names = lax.broadcasted_iota(jnp.int32, (owners, 256), 0)
        carry = jnp.zeros((owners, 1), F32)
        for j in range(exit_rows // 256):
            hit = (owner[:, j * 256 : (j + 1) * 256] == names).astype(F32)
            count = jnp.dot(hit.astype(BF16), upto, preferred_element_type=F32) + carry
            slots.append(jnp.sum(hit * (count - 1.0), axis=0, keepdims=True))
            carry = count[:, 255:256]
        slot = jnp.concatenate(slots, axis=1)
        cell = cell_ref[...]
        across = jnp.bitwise_and(cell, cb - 1)
        along = jnp.right_shift(cell, cb.bit_length() - 1)
        par[4:5] = (pid_ref[...] * ca + along).astype(F32)
        par[5:6] = across.astype(F32)
        number = lax.broadcasted_iota(jnp.int32, (1, exit_rows), 1)
        half_cb = cb // 2
        par[6:7] = jnp.bitwise_and(number, half_cb - 1).astype(F32)
        par[7:8] = (jnp.right_shift(number, half_cb.bit_length() - 1) + 1).astype(F32)
        places = lax.broadcasted_iota(jnp.int32, (SLOTS, exit_rows), 0).astype(F32)
        in_slot[...] = (slot == places).astype(BF16)
        group = 16
        label = jnp.right_shift(lax.broadcasted_iota(jnp.int32, (group * 8, exit_rows), 0), 3)

        @pl.loop(0, owners // group)
        def _(b):
            picks[pl.ds(pl.multiple_of(b * group * 8, group * 8), group * 8)] = (
                owner == label + b * group
            ).astype(BF16)

        halve = jnp.where(
            jnp.right_shift(lax.broadcasted_iota(jnp.int32, (cb, cb // 2), 0), 1)
            == lax.broadcasted_iota(jnp.int32, (cb, cb // 2), 1),
            0.25,
            0.0,
        ).astype(BF16)

        layers = sections // 4
        plane_row = lax.broadcasted_iota(jnp.int32, (ca, cb), 0)
        plane_lane = lax.broadcasted_iota(jnp.int32, (ca, cb), 1)

        def plane(k):
            tiles = fbuf[pl.ds(k * (2 * ca + PAD), 2 * ca), :].reshape(ca // 8, 2, 8, LANES)
            return jnp.concatenate([tiles[:, h].reshape(ca, LANES) for h in range(2)], axis=1)

        def plane_lap(c):
            up = jnp.where(plane_row == 0, 0.0, pltpu.roll(c, 1, 0))
            down = jnp.where(plane_row == ca - 1, 0.0, pltpu.roll(c, ca - 1, 0))
            left = jnp.where(plane_lane == 0, 0.0, pltpu.roll(c, 1, 1))
            right = jnp.where(plane_lane == cb - 1, 0.0, pltpu.roll(c, cb - 1, 1))
            return up + down + (left + right) - 4.0 * c

        last = [v * layers + layers - 1 for v in range(4)]
        d, m, q, e = (plane(k) for k in last)
        if layers > 1:
            dm, dq, de = (x - plane(k - 1) for x, k in zip((m, q, e), last[1:]))
        else:
            dm, dq, de = m, q, e
        relaxing = relax_rate / (1.0 + d * d)
        skew = e - 2.0 * q
        new_flux = m - cfl_nozzle * (dm + dq) + diffusion * plane_lap(m)
        new_skew = (
            skew
            - cfl_nozzle * (de - 2.0 * dq)
            - (2.0 * relax_step) * relaxing * (e - q)
            + diffusion * plane_lap(skew)
        )
        planes = jnp.concatenate([new_flux, new_skew, diffusion * m, diffusion * skew], axis=0)
        paired = planes + pltpu.roll(planes, 4 * ca - 1, 0)
        edge_rows = jnp.concatenate(
            [planes[(2 + v) * ca + a : (2 + v) * ca + a + 1] for a in (0, ca - 1) for v in range(2)]
            + [jnp.zeros((4, cb), F32)],
            axis=0,
        )
        summed = jnp.concatenate([paired[: 2 * ca], edge_rows], axis=0)
        hi = summed.astype(BF16)
        rest = summed - hi.astype(F32)
        mid, low = split_hi_lo(rest)
        count = 2 * ca + 8
        sums = jnp.dot(
            jnp.concatenate([hi, mid, low], axis=0), halve, preferred_element_type=F32
        )
        coarse = sums[:count] + sums[count : 2 * count] + sums[2 * count :]
        for v in range(2):
            for k, part in enumerate(split_hi_lo(coarse[v * ca : (v + 1) * ca])):
                part = part.astype(F32)
                for i in range(ca // 2):
                    par[2 * v + k : 2 * v + k + 1, i * (cb // 2) : (i + 1) * (cb // 2)] = part[
                        2 * i : 2 * i + 1
                    ]
        side_hi, side_lo = split_hi_lo(0.25 * paired[2 * ca :])
        lane = lax.broadcasted_iota(jnp.int32, (8, cb), 1)
        line = lax.broadcasted_iota(jnp.int32, (8, cb), 0)
        ends = jnp.logical_or(
            jnp.logical_and(line == 0, lane == 0), jnp.logical_and(line == 1, lane == cb - 1)
        ).astype(BF16)
        side = dot_last(ends, jnp.concatenate([side_hi, side_lo], axis=0))
        edge_hi, edge_lo = split_hi_lo(coarse[2 * ca :])
        edge_hi, edge_lo = edge_hi.astype(F32), edge_lo.astype(F32)
        edges = jnp.concatenate(
            [x[n : n + 1] for n in range(4) for x in (edge_hi, edge_lo)] + [side], axis=0
        ).astype(BF16)

        values = par[...].astype(BF16)
        tiled = jnp.concatenate([values] * group, axis=0)

        @pl.loop(0, owners // group)
        def _(b):
            picked = tiled * picks[pl.ds(pl.multiple_of(b * group * 8, group * 8), group * 8)]
            packed = dot_last(picked, in_slot[...]).reshape(group, 8, SLOTS)
            send_buf[pl.ds(b * group, group)] = jnp.concatenate(
                [
                    packed[:, :, :LANES].astype(BF16),
                    packed[:, :, LANES:].astype(BF16),
                    jnp.broadcast_to(edges[None], (group, 16, LANES)),
                ],
                axis=1,
            )

        pl.semaphore_wait(barrier, near + owners)

        @pl.loop(0, owners)
        def _(k):
            o = jnp.where(2 * s < n_slab, owners - 1 - k, k)
            pltpu.make_async_remote_copy(
                src_ref=send_buf.at[o],
                dst_ref=recv_buf.at[me],
                send_sem=row_send.at[o],
                recv_sem=row_recv.at[me],
                device_id=(1, o // n_plane, o % n_plane),
                device_id_type=MESH,
            ).start()

        extract_columns()
        start_halo((0, 1, 2, 3))
        fill_rows()
        for a in (0, ca + 1):
            tbuf[a] = jnp.zeros((sections, cb), F32)

        @pl.loop(0, ca // CHUNK)
        def _(step):
            for t in range(CHUNK):
                a = step * CHUNK + t
                c, _, lap = neighbours(a, False)
                back = jnp.where(jnp.bitwise_and(col_row, layers - 1) == 0, 0.0, pltpu.roll(c, 1, 0))
                du = c - back
                d, m, q, e = (c[v * layers : (v + 1) * layers] for v in range(4))
                dm, dq, de = (du[v * layers : (v + 1) * layers] for v in (1, 2, 3))
                relaxing = relax_rate / (1.0 + d * d)
                fresh = diffusion * lap + jnp.concatenate(
                    [
                        d - cfl_nozzle * dm,
                        m - cfl_nozzle * (dm + dq),
                        q + relax_step * relaxing * (e - q) - cfl_nozzle * dq,
                        e - cfl_nozzle * de,
                    ],
                    axis=0,
                )
                scatter_row(a, fresh)

        wait_halo()
        placed = diffusion * placed_columns()
        opad[...] += jnp.stack(
            [placed[:, h * LANES : (h + 1) * LANES].reshape(rows // 8, 8, LANES) for h in range(2)],
            axis=1,
        ).reshape(sections, 2 * ca, LANES)
        for side, a in enumerate((0, ca - 1)):
            for h in range(2):
                obuf[lines(a, h), :] += diffusion * edge_in[side, :, h * LANES : (h + 1) * LANES]

        @pl.loop(0, owners)
        def _(o):
            pltpu.make_async_remote_copy(
                src_ref=send_buf.at[o],
                dst_ref=recv_buf.at[me],
                send_sem=row_send.at[o],
                recv_sem=row_recv.at[me],
                device_id=(1, o // n_plane, o % n_plane),
                device_id_type=MESH,
            ).wait_send()

    @pl.when(g == 1)
    def _():
        extract_columns()
        pl.semaphore_wait(barrier, near)
        start_halo((0, 1, 2, 3))
        fill_rows()
        for copy in spray_args:
            copy.wait()
        folded = jnp.dot(coal_ref[...], fold[...], preferred_element_type=F32).astype(BF16)
        evap = jnp.zeros((sections, cb), F32)
        for k in range(sections):
            evap = jnp.where(col_row == k, evap_ref[k], evap)
        speeds = 0.2 + 0.5 * col_row.astype(F32) / (sections - 1)

        wait_halo()
        for side, a in enumerate((0, ca + 1)):
            tbuf[a] = edge_in[side]
        placed = placed_columns()
        for h in range(2):
            hbuf.reshape(2, sections, ca + PAD, LANES)[h, :, pl.ds(0, ca), :] = placed[
                :, h * LANES : (h + 1) * LANES
            ].reshape(sections, ca, LANES)

        @pl.loop(0, ca // CHUNK)
        def _(step):
            parts = []
            for t in range(CHUNK):
                c, up, lap = neighbours(step * CHUNK + t, True)
                lost = evap * c
                gained = jnp.where(
                    col_row == sections - 1, 0.0, pltpu.roll(lost, sections - 1, 0)
                )
                parts.append(c - speeds * (c - up) + diffusion * lap - lost + gained)
            size = CHUNK // 2
            moved = [
                jnp.concatenate(parts[z * size : (z + 1) * size], axis=1) for z in range(2)
            ]
            first = [
                jnp.dot(folded, pair_terms(x), preferred_element_type=F32) for x in moved
            ]
            middle = [x + (0.5 * collide_step) * y for x, y in zip(moved, first)]
            second = [
                jnp.dot(folded, pair_terms(x), preferred_element_type=F32) for x in middle
            ]
            for z in range(2):
                mixed = moved[z] + collide_step * second[z]
                for t in range(size):
                    scatter_row(step * CHUNK + z * size + t, mixed[:, t * cb : (t + 1) * cb])

        @pl.loop(0, owners)
        def _(o):
            pltpu.make_async_remote_copy(
                src_ref=send_buf.at[o],
                dst_ref=recv_buf.at[o],
                send_sem=row_send.at[o],
                recv_sem=row_recv.at[o],
                device_id=(0, s, p),
                device_id_type=MESH,
            ).wait_recv()


def finish(
    n_plane, owners, sections, ca, cb,
    held, rows_in, width_hbm,
    out_hbm,
    obuf, flat, par, mass, left_even, left_odd, right_even, right_odd, width_ref, arg_sem, out_sem,
):
    plumes = width_ref.shape[0]
    rows = sections * ca
    g = lax.axis_index("group")
    whole = held.reshape(sections, 2 * ca + PAD, LANES).at[:, pl.ds(0, 2 * ca), :]
    out_whole = out_hbm.reshape(sections, 2 * ca, LANES)

    @pl.when(g == 0)
    def _():
        copy = pltpu.make_async_copy(whole, out_whole, out_sem.at[0])
        copy.start()
        copy.wait()

    @pl.when(g == 1)
    def _():
        fetch = pltpu.make_async_copy(width_hbm, width_ref, arg_sem)
        fetch.start()
        fill = pltpu.make_async_copy(whole, obuf, out_sem.at[PIECES])
        fill.start()
        pad = n_plane * 32
        half_cb = cb // 2
        flat[pl.ds(0, pad)] = jnp.zeros((pad, LANES), F32)
        flat[pl.ds(pad + owners * 32, pad)] = jnp.zeros((pad, LANES), F32)

        @pl.loop(0, owners // 8, unroll=2)
        def _(b):
            at = pl.ds(pl.multiple_of(pad + b * 256, 128), 256)
            flat[at] = rows_in[pl.ds(b * 8, 8)].astype(F32).reshape(256, LANES)

        fetch.wait()
        sub = lax.broadcasted_iota(jnp.int32, (8, LANES), 0)

        @pl.loop(0, owners // 8, unroll=2)
        def _(b):
            def take(shift, line):
                return flat[pl.ds(pad + (b * 8 + shift) * 32 + line, 8, stride=32), :]

            plane_at = lax.rem(b * 8 + sub, n_plane)
            first_plane = plane_at == 0
            last_plane = plane_at == n_plane - 1
            above = [take(-n_plane, 16 + 4 + x) for x in range(4)]
            below = [take(n_plane, 16 + x) for x in range(4)]
            before = jnp.where(first_plane, 0.0, take(-1, 16 + 9))
            behind = jnp.where(last_plane, 0.0, take(1, 16 + 8))

            def pick(table, index):
                return jnp.take_along_axis(table, index, axis=1, mode="promise_in_bounds")

            for h in range(2):
                got = [take(0, h * 8 + x) for x in range(8)]
                spot = got[6].astype(jnp.int32)
                line = got[7].astype(jnp.int32)
                slot_line = 2 * jnp.maximum(line - 1, 0)
                flux = got[0] + got[1]
                skew = got[2] + got[3]
                for tables, here in ((above, line == 1), (below, line == ca // 2)):
                    f0, f1, u0, u1 = (pick(table, spot) for table in tables)
                    flux += jnp.where(here, f0 + f1, 0.0)
                    skew += jnp.where(here, u0 + u1, 0.0)
                for table, here in ((before, spot == 0), (behind, spot == half_cb - 1)):
                    f0, u0, f1, u1 = (pick(table, slot_line + ca * x) for x in range(4))
                    flux += jnp.where(here, f0 + f1, 0.0)
                    skew += jnp.where(here, u0 + u1, 0.0)
                code = got[4].astype(jnp.int32)
                plume = jnp.right_shift(code, ca.bit_length() - 1)
                spread = jnp.full((8, LANES), width_ref[0], F32)
                for k in range(1, plumes):
                    spread = jnp.where(plume == k, width_ref[k], spread)
                values = (
                    jnp.where(line > 0, jnp.sqrt(1.0 + flux * flux), 0.0),
                    (sections - 1) * jax.nn.sigmoid(skew),
                    1.0 / spread,
                    jnp.bitwise_and(code, ca - 1).astype(F32),
                    got[5],
                )
                for x, value in enumerate(values):
                    par[x, pl.ds(pl.multiple_of(b * 8, 8), 8), h * LANES : (h + 1) * LANES] = value

        span = SOURCES * SLOTS
        level = lax.broadcasted_iota(jnp.int32, (sections, span), 0).astype(F32)
        index_a = lax.broadcasted_iota(jnp.int32, (ca, span), 0).astype(F32).astype(BF16)
        index_b = lax.broadcasted_iota(jnp.int32, (cb, span), 0).astype(F32).astype(BF16)

        def build(step, left, right):
            strength, center, inverse, along, across = (
                jnp.concatenate(
                    [par[x, pl.ds(step * SOURCES + t, 1), :] for t in range(SOURCES)], axis=1
                )
                for x in range(5)
            )
            scaled = (level - center) * inverse
            weights = 1.0 / (1.0 + scaled * scaled)
            mass[...] = weights * (strength / jnp.sum(weights, axis=0, keepdims=True))
            mask = jnp.where(along.astype(BF16) == index_a, jnp.ones((),BF16), jnp.zeros((),BF16))
            right[...] = jnp.where(across.astype(BF16) == index_b, jnp.ones((),BF16), jnp.zeros((),BF16))
            for k in range(sections):
                left[k * ca : (k + 1) * ca] = (
                    jnp.broadcast_to(mass[k : k + 1], (ca, span)).astype(BF16) * mask
                )

        def add(left, right, first, count):
            added = dot_last(left[first * ca : (first + count) * ca], right[...])
            tiles = jnp.stack(
                [
                    added[:, h * LANES : (h + 1) * LANES].reshape(count * ca // 8, 8, LANES)
                    for h in range(2)
                ],
                axis=1,
            )
            obuf[first : first + count] += tiles.reshape(count, 2 * ca, LANES)

        build(0, left_even, right_even)
        fill.wait()
        steps = owners // SOURCES

        @pl.loop(0, steps // 2 - 1)
        def _(i):
            add(left_even, right_even, 0, sections)
            build(2 * i + 1, left_odd, right_odd)
            add(left_odd, right_odd, 0, sections)
            build(2 * i + 2, left_even, right_even)

        add(left_even, right_even, 0, sections)
        build(steps - 1, left_odd, right_odd)
        each = sections // PIECES
        stores = []
        for c in range(PIECES):
            add(left_odd, right_odd, c * each, each)
            at = pl.ds(c * each, each)
            stores.append(
                pltpu.make_async_copy(obuf.at[at], out_whole.at[at], out_sem.at[c])
            )
            stores[-1].start()
        for store in stores:
            store.wait()


def body(n_slab, n_plane, fields, evap_rates, coal_kernel, plume_width, owner_map, deposit_cell, plume_ids):
    _, sections, ca, cb = fields.shape
    exit_rows = owner_map.shape[1]
    owners = n_slab * n_plane
    rows = sections * ca
    fold = jnp.asarray(fold_matrix(sections), BF16)
    kept = fold.shape[1]
    hbm = pl.BlockSpec(memory_space=pl.ANY)
    vmem = pl.BlockSpec(memory_space=pltpu.VMEM)
    held, rows_in = pl.pallas_call(
        functools.partial(kernel, n_slab, n_plane, sections, ca, cb, exit_rows),
        out_shape=[
            pltpu.VMEM((2 * rows + sections * PAD, LANES), F32),
            pltpu.VMEM((owners, 32, LANES), BF16),
        ],
        in_specs=[hbm] * 7,
        out_specs=[vmem] * 2,
        scratch_shapes=[
            pltpu.VMEM((2 * rows + sections * PAD, LANES), F32),
            pltpu.VMEM((ca + 2, sections, cb), F32),
            pltpu.VMEM((2, sections, cb), F32),
            pltpu.VMEM((2, rows + sections * PAD, LANES), F32),
            pltpu.VMEM((sections * sections, kept), BF16),
            pltpu.VMEM((2, 1, rows), F32),
            pltpu.VMEM((2, 1, rows), F32),
            pltpu.VMEM((8, exit_rows), F32),
            pltpu.VMEM((owners, 32, LANES), BF16),
            pltpu.SMEM(evap_rates.shape, F32),
            pltpu.VMEM(coal_kernel.shape, BF16),
            pltpu.VMEM((1, exit_rows), jnp.int32),
            pltpu.VMEM((1, exit_rows), jnp.int32),
            pltpu.VMEM((1, exit_rows), jnp.int32),
            pltpu.VMEM((owners * 8, exit_rows), BF16),
            pltpu.VMEM((SLOTS, exit_rows), BF16),
            pltpu.SemaphoreType.DMA,
            pltpu.SemaphoreType.DMA((4,)),
            pltpu.SemaphoreType.DMA((4,)),
            pltpu.SemaphoreType.DMA((4,)),
            pltpu.SemaphoreType.DMA((owners,)),
            pltpu.SemaphoreType.DMA((owners,)),
        ],
        compiler_params=pltpu.CompilerParams(
            collective_id=0, has_side_effects=True, vmem_limit_bytes=VMEM_BYTES
        ),
    )(
        fields.reshape(rows // 8, 8, 2, LANES).transpose(0, 2, 1, 3).reshape(2 * rows, LANES), evap_rates, coal_kernel, fold,
        owner_map, deposit_cell, plume_ids,
    )
    span = SOURCES * SLOTS
    out = pl.pallas_call(
        functools.partial(finish, n_plane, owners, sections, ca, cb),
        out_shape=jax.ShapeDtypeStruct((2 * rows, LANES), F32),
        in_specs=[vmem, vmem, hbm],
        out_specs=hbm,
        scratch_shapes=[
            pltpu.VMEM((sections, 2 * ca, LANES), F32),
            pltpu.VMEM(((owners + 2 * n_plane) * 32, LANES), F32),
            pltpu.VMEM((5, owners, SLOTS), F32),
            pltpu.VMEM((sections, span), F32),
            pltpu.VMEM((rows, span), BF16),
            pltpu.VMEM((rows, span), BF16),
            pltpu.VMEM((cb, span), BF16),
            pltpu.VMEM((cb, span), BF16),
            pltpu.SMEM(plume_width.shape, F32),
            pltpu.SemaphoreType.DMA,
            pltpu.SemaphoreType.DMA((PIECES + 1,)),
        ],
        compiler_params=pltpu.CompilerParams(vmem_limit_bytes=VMEM_BYTES),
    )(
        pltpu.with_memory_space_constraint(held, pltpu.VMEM),
        pltpu.with_memory_space_constraint(rows_in, pltpu.VMEM),
        plume_width,
    )
    out = out.reshape(rows // 8, 2, 8, LANES).transpose(0, 2, 1, 3)
    return out.reshape(1, sections, ca, cb)


def solution(mesh):
    return jax.shard_map(
        functools.partial(body, mesh.shape["slab"], mesh.shape["plane"]),
        mesh=mesh,
        in_specs=(
            P("group", None, "slab", "plane"),
            P(),
            P(),
            P(),
            P(("slab", "plane"), None),
            P(("slab", "plane"), None),
            P(("slab", "plane"), None),
        ),
        out_specs=P("group", None, "slab", "plane"),
        check_vma=False,
    )
```

```python
import functools

import jax
import jax.numpy as jnp
import numpy as np
from jax import lax
from jax.experimental import pallas as pl
from jax.experimental.pallas import tpu as pltpu
from jax.sharding import PartitionSpec as P

MESH = pl.DeviceIdType.MESH
F32 = jnp.float32
BF16 = jnp.bfloat16
LANES = 128
SLOTS = 256
CHUNK = 8
PAD = 8
LINES = 24
SOURCES = 4
PIECES = 2
VMEM_BYTES = 56 * 1024 * 1024

cfl_nozzle = 0.35
diffusion = 0.2
relax_rate = 5.0
relax_step = 0.1
collide_step = 0.25


def fold_matrix(sections):
    kept = [(i, j) for i in range(sections) for j in range(i // 8 * 8, sections)]
    fold = np.zeros((sections * sections, len(kept)), np.float32)
    for q, (i, j) in enumerate(kept):
        fold[i * sections + j, q] = 1.0
        if j // 8 > i // 8:
            fold[j * sections + i, q] = 1.0
    return fold


def pair_terms(m):
    sections, width = m.shape
    pieces = []
    for i in range(sections):
        low = i // 8 * 8
        pieces.append(jnp.broadcast_to(m[i : i + 1], (sections - low, width)) * m[low:])
    return jnp.concatenate(pieces, axis=0).astype(BF16)


def split_hi_lo(x):
    hi = x.astype(BF16)
    lo = (x - hi.astype(F32)).astype(BF16)
    return hi, lo


def dot_last(a, b):
    return lax.dot_general(a, b, (((1,), (1,)), ((), ())), preferred_element_type=F32)


def kernel(
    n_slab, n_plane, sections, ca, cb, exit_rows,
    fields_hbm, evap_hbm, coal_hbm, fold_hbm, owner_hbm, cell_hbm, pid_hbm,
    obuf, recv_buf, side_in,
    fbuf, tbuf, edge_in, upright_buf, fold, cols_out, cols_near, cols_in, par, send_buf,
    evap_ref, coal_ref, owner_ref, cell_ref, pid_ref, picks, in_slot,
    in_sem, arg_sem, halo_send, halo_recv, row_send, row_recv, side_out, side_send, side_recv,
):
    owners = n_slab * n_plane
    rows = sections * ca
    g = lax.axis_index("group")
    s = lax.axis_index("slab")
    p = lax.axis_index("plane")
    me = s * n_plane + p
    barrier = pltpu.get_barrier_semaphore()

    @pl.when(g == 1)
    def _():
        for i in range(n_slab):
            row = jnp.where(2 * s < n_slab, n_slab - 1 - i, i)
            for j in range(n_plane):
                pl.semaphore_signal(barrier, inc=1, device_id=(0, row, j), device_id_type=MESH)


    fpad = fbuf.reshape(sections, 2 * ca + PAD, LANES).at[:, pl.ds(0, 2 * ca), :]
    opad = obuf.reshape(sections, 2 * ca + PAD, LANES).at[:, pl.ds(0, 2 * ca), :]
    load = pltpu.make_async_copy(
        fields_hbm.reshape(sections, 2 * ca, LANES), fpad, in_sem
    )
    load.start()
    nozzle_args = [
        pltpu.make_async_copy(source, target, arg_sem.at[k])
        for k, (source, target) in enumerate(
            ((owner_hbm, owner_ref), (cell_hbm, cell_ref), (pid_hbm, pid_ref))
        )
    ]
    spray_args = [
        pltpu.make_async_copy(source, target, arg_sem.at[k])
        for k, (source, target) in enumerate(
            ((evap_hbm, evap_ref), (coal_hbm, coal_ref), (fold_hbm, fold))
        )
    ]

    @pl.when(g == 0)
    def _():
        for copy in nozzle_args:
            copy.start()

    @pl.when(g == 1)
    def _():
        for copy in spray_args:
            copy.start()

    sides = [
        (s > 0, (g, s - 1, p)),
        (s < n_slab - 1, (g, s + 1, p)),
        (p > 0, (g, s, p - 1)),
        (p < n_plane - 1, (g, s, p + 1)),
    ]
    near = 0
    for there, target in sides:
        near = near + there.astype(jnp.int32)

        @pl.when(there)
        def _():
            pl.semaphore_signal(barrier, inc=1, device_id=target, device_id_type=MESH)

    load.wait()

    def lines(a, h):
        return pl.ds(a // 8 * 16 + h * 8 + a % 8, sections, stride=2 * ca + PAD)

    def gather_row(ref, a):
        return jnp.concatenate([ref[lines(a, h), :] for h in range(2)], axis=1)

    def half(ref, h):
        return ref[...].reshape(rows // 8, 2, 8, LANES)[:, h].reshape(rows, LANES)

    def halo(kind, target):
        source, landing = (
            (tbuf.at[ca], edge_in.at[0]),
            (tbuf.at[1], edge_in.at[1]),
            (cols_out.at[1], cols_in.at[0]),
            (cols_out.at[0], cols_in.at[1]),
        )[kind]
        return pltpu.make_async_remote_copy(
            src_ref=source,
            dst_ref=landing,
            send_sem=halo_send.at[kind],
            recv_sem=halo_recv.at[kind],
            device_id=target,
            device_id_type=MESH,
        )

    outgoing = (sides[1], sides[0], sides[3], sides[2])
    def start_halo(kinds):
        for kind in kinds:

            @pl.when(outgoing[kind][0])
            def _():
                halo(kind, outgoing[kind][1]).start()

    def extract_columns():
        for a in (0, ca - 1):
            tbuf[a + 1] = gather_row(fbuf, a)

        lane = lax.broadcasted_iota(jnp.int32, (8, LANES), 1)
        line = lax.broadcasted_iota(jnp.int32, (8, LANES), 0)
        for h, (outer, inner) in enumerate(((0, 1), (LANES - 1, LANES - 2))):
            select = jnp.logical_or(
                jnp.logical_and(line == 0, lane == outer), jnp.logical_and(line == 1, lane == inner)
            ).astype(BF16)
            columns = dot_last(select, half(fpad, h).astype(BF16))
            for x in range(rows // LANES):
                at = slice(x * LANES, (x + 1) * LANES)
                cols_out[h, x : x + 1] = columns[0:1, at]
                cols_near[h, x : x + 1] = columns[1:2, at]

    def fill_rows():
        @pl.loop(1, ca - 1)
        def _(a):
            tbuf[a + 1] = gather_row(fbuf, a)

        for kind, landing in enumerate((edge_in.at[0], edge_in.at[1], cols_in.at[0], cols_in.at[1])):

            @pl.when(jnp.logical_not(sides[kind][0]))
            def _():
                landing[...] = jnp.zeros(landing.shape, F32)

    def wait_halo():
        for kind in range(4):

            @pl.when(outgoing[kind][0])
            def _():
                halo(kind, outgoing[kind][1]).wait_send()

            @pl.when(sides[kind][0])
            def _():
                halo(kind, outgoing[kind][1]).wait_recv()

    def placed_columns():
        sub = lax.broadcasted_iota(jnp.int32, (16, cb), 0)
        lanes = lax.broadcasted_iota(jnp.int32, (16, cb), 1)
        lined = [
            jnp.concatenate([cols_in[h, x : x + 1] for x in range(rows // LANES)], axis=1)
            for h in range(2)
        ]
        stack = jnp.concatenate(lined + [jnp.zeros((14, rows), F32)], axis=0)
        place = jnp.logical_or(
            jnp.logical_and(sub == 0, lanes == 0), jnp.logical_and(sub == 1, lanes == cb - 1)
        ).astype(BF16)
        return jnp.dot(stack.T.astype(BF16), place, preferred_element_type=F32)

    col_lane = lax.broadcasted_iota(jnp.int32, (sections, cb), 1)
    col_row = lax.broadcasted_iota(jnp.int32, (sections, cb), 0)

    def neighbours(a):
        c = tbuf[a + 1]
        up = tbuf[a]
        left = jnp.where(col_lane == 0, 0.0, pltpu.roll(c, 1, 1))
        right = jnp.where(col_lane == cb - 1, 0.0, pltpu.roll(c, cb - 1, 1))
        lap = up + tbuf[a + 2] + (left + right) - 4.0 * c
        return c, up, lap

    def scatter_row(a, value):
        for h in range(2):
            obuf[lines(a, h), :] = value[:, h * LANES : (h + 1) * LANES]

    @pl.when(g == 0)
    def _():
        for copy in nozzle_args:
            copy.wait()
        owner = owner_ref[...]
        slots = []
        below = lax.broadcasted_iota(jnp.int32, (256, 256), 0)
        after = lax.broadcasted_iota(jnp.int32, (256, 256), 1)
        upto = (below <= after).astype(BF16)
        names = lax.broadcasted_iota(jnp.int32, (owners, 256), 0)
        carry = jnp.zeros((owners, 1), F32)
        for j in range(exit_rows // 256):
            hit = (owner[:, j * 256 : (j + 1) * 256] == names).astype(F32)
            count = jnp.dot(hit.astype(BF16), upto, preferred_element_type=F32) + carry
            slots.append(jnp.sum(hit * (count - 1.0), axis=0, keepdims=True))
            carry = count[:, 255:256]
        slot = jnp.concatenate(slots, axis=1)
        cell = cell_ref[...]
        across = jnp.bitwise_and(cell, cb - 1)
        along = jnp.right_shift(cell, cb.bit_length() - 1)
        par[3:4] = pid_ref[...].astype(F32)
        par[4:5] = along.astype(F32)
        par[5:6] = across.astype(F32)
        half_cb = cb // 2
        last_line = ca // 2 - 1
        number = lax.broadcasted_iota(jnp.int32, (1, exit_rows), 1)
        spot = jnp.bitwise_and(number, half_cb - 1)
        line = jnp.right_shift(number, half_cb.bit_length() - 1)
        beside = half_cb + 1 + line
        place = jnp.where(spot == half_cb - 1, -beside, half_cb + ca)
        place = jnp.where(spot == 0, beside, place)
        place = jnp.where(line == last_line, -1 - spot, place)
        par[6:7] = jnp.where(line == 0, 1 + spot, place).astype(F32)
        par[7:8] = jnp.zeros((1, exit_rows), F32)
        places = lax.broadcasted_iota(jnp.int32, (SLOTS, exit_rows), 0).astype(F32)
        in_slot[...] = (slot == places).astype(BF16)
        group = 16
        label = jnp.right_shift(lax.broadcasted_iota(jnp.int32, (group * 8, exit_rows), 0), 3)

        @pl.loop(0, owners // group)
        def _(b):
            picks[pl.ds(pl.multiple_of(b * group * 8, group * 8), group * 8)] = (
                owner == label + b * group
            ).astype(BF16)

        halve = jnp.where(
            jnp.right_shift(lax.broadcasted_iota(jnp.int32, (cb, cb // 2), 0), 1)
            == lax.broadcasted_iota(jnp.int32, (cb, cb // 2), 1),
            0.25,
            0.0,
        ).astype(BF16)

        layers = sections // 4
        plane_row = lax.broadcasted_iota(jnp.int32, (ca, cb), 0)
        plane_lane = lax.broadcasted_iota(jnp.int32, (ca, cb), 1)

        def plane(k):
            tiles = fbuf[pl.ds(k * (2 * ca + PAD), 2 * ca), :].reshape(ca // 8, 2, 8, LANES)
            return jnp.concatenate([tiles[:, h].reshape(ca, LANES) for h in range(2)], axis=1)

        def plane_lap(c):
            up = jnp.where(plane_row == 0, 0.0, pltpu.roll(c, 1, 0))
            down = jnp.where(plane_row == ca - 1, 0.0, pltpu.roll(c, ca - 1, 0))
            left = jnp.where(plane_lane == 0, 0.0, pltpu.roll(c, 1, 1))
            right = jnp.where(plane_lane == cb - 1, 0.0, pltpu.roll(c, cb - 1, 1))
            return up + down + (left + right) - 4.0 * c

        last = [v * layers + layers - 1 for v in range(4)]
        d, m, q, e = (plane(k) for k in last)
        if layers > 1:
            dm, dq, de = (x - plane(k - 1) for x, k in zip((m, q, e), last[1:]))
        else:
            dm, dq, de = m, q, e
        relaxing = relax_rate / (1.0 + d * d)
        skew = e - 2.0 * q
        new_flux = m - cfl_nozzle * (dm + dq) + diffusion * plane_lap(m)
        new_skew = (
            skew
            - cfl_nozzle * (de - 2.0 * dq)
            - (2.0 * relax_step) * relaxing * (e - q)
            + diffusion * plane_lap(skew)
        )
        planes = jnp.concatenate([new_flux, new_skew, diffusion * m, diffusion * skew], axis=0)
        paired = planes + pltpu.roll(planes, 4 * ca - 1, 0)
        edge_rows = jnp.concatenate(
            [planes[(2 + v) * ca + a : (2 + v) * ca + a + 1] for a in (0, ca - 1) for v in range(2)]
            + [jnp.zeros((4, cb), F32)],
            axis=0,
        )
        summed = jnp.concatenate([paired[: 2 * ca], edge_rows], axis=0)
        hi = summed.astype(BF16)
        rest = summed - hi.astype(F32)
        mid, low = split_hi_lo(rest)
        count = 2 * ca + 8
        sums = jnp.dot(
            jnp.concatenate([hi, mid, low], axis=0), halve, preferred_element_type=F32
        )
        coarse = sums[:count] + sums[count : 2 * count] + sums[2 * count :]
        flux_part = coarse[:ca].astype(BF16).astype(F32)
        skew_hi, skew_lo = split_hi_lo(coarse[ca : 2 * ca])
        for k, part in enumerate((flux_part, skew_hi.astype(F32), skew_lo.astype(F32))):
            for i in range(ca // 2):
                par[k : k + 1, i * (cb // 2) : (i + 1) * (cb // 2)] = part[2 * i : 2 * i + 1]
        side_hi, side_lo = split_hi_lo(0.25 * paired[2 * ca :])
        lane = lax.broadcasted_iota(jnp.int32, (8, cb), 1)
        line = lax.broadcasted_iota(jnp.int32, (8, cb), 0)
        ends = jnp.logical_or(
            jnp.logical_and(line == 0, lane == 0), jnp.logical_and(line == 1, lane == cb - 1)
        ).astype(BF16)
        side = dot_last(ends, side_hi) + dot_last(ends, side_lo)
        edge = coarse[2 * ca :]
        side_out[0] = jnp.concatenate([side[0:1], side[1:2]], axis=1)
        side_out[1] = edge[1:2]
        side_out[2] = edge[3:4]
        blank = jnp.zeros((7, LANES), F32)
        edges = [jnp.concatenate([blank, edge[2 * x : 2 * x + 1]], axis=0) for x in range(2)]

        values = par[...].astype(BF16)
        tiled = jnp.concatenate([values] * group, axis=0)

        @pl.loop(0, owners // group)
        def _(b):
            picked = tiled * picks[pl.ds(pl.multiple_of(b * group * 8, group * 8), group * 8)]
            packed = dot_last(picked, in_slot[...]).reshape(group, 8, SLOTS)
            send_buf[pl.ds(b * group, group)] = jnp.concatenate(
                [packed[:, :, :LANES] + edges[0][None], packed[:, :, LANES:] + edges[1][None]],
                axis=1,
            ).astype(BF16)

        pl.semaphore_wait(barrier, near + owners)

        for i in range(n_slab):
            row = jnp.where(2 * s < n_slab, n_slab - 1 - i, i)
            for j in range(n_plane):
                pltpu.make_async_remote_copy(
                    src_ref=side_out,
                    dst_ref=side_in.at[me],
                    send_sem=side_send.at[row * n_plane + j],
                    recv_sem=side_recv.at[me],
                    device_id=(1, row, j),
                    device_id_type=MESH,
                ).start()

        for i in range(n_slab):
            row = jnp.where(2 * s < n_slab, n_slab - 1 - i, i)
            for j in range(n_plane):
                pltpu.make_async_remote_copy(
                    src_ref=send_buf.at[row * n_plane + j],
                    dst_ref=recv_buf.at[me],
                    send_sem=row_send.at[row * n_plane + j],
                    recv_sem=row_recv.at[me],
                    device_id=(1, row, j),
                    device_id_type=MESH,
                ).start()

        extract_columns()
        start_halo((0, 1, 2, 3))
        fill_rows()
        for a in (0, ca + 1):
            tbuf[a] = jnp.zeros((sections, cb), F32)

        @pl.loop(0, ca // CHUNK)
        def _(step):
            for t in range(CHUNK):
                a = step * CHUNK + t
                c, _, lap = neighbours(a)
                back = jnp.where(jnp.bitwise_and(col_row, layers - 1) == 0, 0.0, pltpu.roll(c, 1, 0))
                du = c - back
                d, m, q, e = (c[v * layers : (v + 1) * layers] for v in range(4))
                dm, dq, de = (du[v * layers : (v + 1) * layers] for v in (1, 2, 3))
                relaxing = relax_rate / (1.0 + d * d)
                fresh = diffusion * lap + jnp.concatenate(
                    [
                        d - cfl_nozzle * dm,
                        m - cfl_nozzle * (dm + dq),
                        q + relax_step * relaxing * (e - q) - cfl_nozzle * dq,
                        e - cfl_nozzle * de,
                    ],
                    axis=0,
                )
                scatter_row(a, fresh)

        wait_halo()
        placed = diffusion * placed_columns()
        opad[...] += jnp.stack(
            [placed[:, h * LANES : (h + 1) * LANES].reshape(rows // 8, 8, LANES) for h in range(2)],
            axis=1,
        ).reshape(sections, 2 * ca, LANES)
        for side, a in enumerate((0, ca - 1)):
            for h in range(2):
                obuf[lines(a, h), :] += diffusion * edge_in[side, :, h * LANES : (h + 1) * LANES]

        @pl.loop(0, owners)
        def _(o):
            pltpu.make_async_remote_copy(
                src_ref=send_buf.at[o],
                dst_ref=recv_buf.at[me],
                send_sem=row_send.at[o],
                recv_sem=row_recv.at[me],
                device_id=(1, o // n_plane, o % n_plane),
                device_id_type=MESH,
            ).wait_send()

            pltpu.make_async_remote_copy(
                src_ref=side_out,
                dst_ref=side_in.at[me],
                send_sem=side_send.at[o],
                recv_sem=side_recv.at[me],
                device_id=(1, o // n_plane, o % n_plane),
                device_id_type=MESH,
            ).wait_send()

    @pl.when(g == 1)
    def _():
        extract_columns()
        pl.semaphore_wait(barrier, near)
        start_halo((0, 1, 2, 3))
        fill_rows()
        for copy in spray_args:
            copy.wait()
        folded = jnp.dot(coal_ref[...], fold[...], preferred_element_type=F32).astype(BF16)
        evap = jnp.zeros((sections, cb), F32)
        for k in range(sections):
            evap = jnp.where(col_row == k, evap_ref[k], evap)
        speeds = 0.2 + 0.5 * col_row.astype(F32) / (sections - 1)
        for a in (0, ca + 1):
            tbuf[a] = jnp.zeros((sections, cb), F32)

        def moved_from(c, up, lap):
            width = c.shape[1]
            lost = evap[:, :width] * c
            gained = jnp.where(
                col_row[:, :width] == sections - 1, 0.0, pltpu.roll(lost, sections - 1, 0)
            )
            return c - speeds[:, :width] * (c - up) + diffusion * lap - lost + gained

        def collide(moved):
            first = [jnp.dot(folded, pair_terms(x), preferred_element_type=F32) for x in moved]
            middle = [x + (0.5 * collide_step) * y for x, y in zip(moved, first)]
            second = [jnp.dot(folded, pair_terms(x), preferred_element_type=F32) for x in middle]
            return [x + collide_step * y for x, y in zip(moved, second)]

        @pl.loop(0, ca // CHUNK)
        def _(step):
            size = CHUNK // 2
            moved = [
                jnp.concatenate(
                    [moved_from(*neighbours(step * CHUNK + z * size + t)) for t in range(size)],
                    axis=1,
                )
                for z in range(2)
            ]
            for z, mixed in enumerate(collide(moved)):
                for t in range(size):
                    scatter_row(step * CHUNK + z * size + t, mixed[:, t * cb : (t + 1) * cb])

        wait_halo()
        for side, a in enumerate((0, ca + 1)):
            tbuf[a] = edge_in[side]
        tile_lane = lax.broadcasted_iota(jnp.int32, (8, LANES), 1)
        wide_lane = lax.broadcasted_iota(jnp.int32, (sections, LANES), 1)

        def upright(x, pair):
            folds = LANES // ca
            for k in range(folds):
                turned = [
                    pltpu.roll(pair[h], (LANES + (h - k) * ca) % LANES, 1) for h in range(2)
                ]
                upright_buf[x, pl.ds(k, sections // folds, stride=folds), :] = jnp.where(
                    tile_lane < ca, turned[0], turned[1]
                )
            return upright_buf[x]

        own = upright(0, (cols_out[0], cols_out[1]))
        inner = upright(1, (cols_near[0], cols_near[1]))
        outer = upright(2, (cols_in[0], cols_in[1]))
        above = pltpu.roll(own, 1, 1)
        below = pltpu.roll(own, LANES - 1, 1)
        parts = []
        for a in (0, ca - 1):
            c, up, lap = neighbours(a)
            lap += jnp.where(col_lane == 0, outer[:, a : a + 1], 0.0)
            lap += jnp.where(col_lane == cb - 1, outer[:, ca + a : ca + a + 1], 0.0)
            parts.append(moved_from(c, up, lap))
        parts.append(moved_from(own, above, above + below + inner + outer - 4.0 * own))
        (mixed,) = collide([jnp.concatenate(parts, axis=1)])
        columns = mixed[:, 2 * cb :]
        for a in range(1, ca - 1):
            for h, target in enumerate((0, LANES - 1)):
                at = lines(a, h)
                obuf[at, :] = jnp.where(
                    wide_lane == target,
                    pltpu.roll(columns, (LANES + target - h * ca - a) % LANES, 1),
                    obuf[at, :],
                )
        for x, a in enumerate((0, ca - 1)):
            scatter_row(a, mixed[:, x * cb : (x + 1) * cb])

        @pl.loop(0, owners)
        def _(o):
            pltpu.make_async_remote_copy(
                src_ref=send_buf.at[o],
                dst_ref=recv_buf.at[o],
                send_sem=row_send.at[o],
                recv_sem=row_recv.at[o],
                device_id=(0, s, p),
                device_id_type=MESH,
            ).wait_recv()

            pltpu.make_async_remote_copy(
                src_ref=side_out,
                dst_ref=side_in.at[o],
                send_sem=side_send.at[o],
                recv_sem=side_recv.at[o],
                device_id=(0, s, p),
                device_id_type=MESH,
            ).wait_recv()


def finish(
    n_plane, owners, sections, ca, cb,
    held, rows_in, sides_in, width_hbm,
    out_hbm,
    obuf, flat, par, mass, left_even, left_odd, right_even, right_odd, width_ref, arg_sem, out_sem,
):
    plumes = width_ref.shape[0]
    rows = sections * ca
    g = lax.axis_index("group")
    whole = held.reshape(sections, 2 * ca + PAD, LANES).at[:, pl.ds(0, 2 * ca), :]
    out_whole = out_hbm.reshape(sections, 2 * ca, LANES)

    @pl.when(g == 0)
    def _():
        copy = pltpu.make_async_copy(whole, out_whole, out_sem.at[0])
        copy.start()
        copy.wait()

    @pl.when(g == 1)
    def _():
        fetch = pltpu.make_async_copy(width_hbm, width_ref, arg_sem)
        fetch.start()
        fill = pltpu.make_async_copy(whole, obuf, out_sem.at[PIECES])
        fill.start()
        half_cb = cb // 2
        pad = n_plane * LINES
        flat[pl.ds(0, pad)] = jnp.zeros((pad, LANES), F32)
        flat[pl.ds(pad + owners * LINES, pad)] = jnp.zeros((pad, LANES), F32)

        @pl.loop(0, owners // 8, unroll=2)
        def _(b):
            for o in range(8):
                at = pl.multiple_of(pad + (b * 8 + o) * LINES, 8)
                flat[pl.ds(at, 16)] = rows_in[b * 8 + o].astype(F32)
                for x in range(3):
                    flat[pl.ds(at + 16 + x, 1)] = sides_in[b * 8 + o, x]

        fetch.wait()
        sub = lax.broadcasted_iota(jnp.int32, (8, LANES), 0)

        @pl.loop(0, owners // 8, unroll=2)
        def _(b):
            def take(shift, line):
                return flat[pl.ds(pad + (b * 8 + shift) * LINES + line, 8, stride=LINES), :]

            plane_at = lax.rem(b * 8 + sub, n_plane)
            above = take(-n_plane, 15), take(-n_plane, 18)
            below = take(n_plane, 7), take(n_plane, 17)
            before = jnp.where(plane_at == 0, 0.0, take(-1, 16))
            behind = jnp.where(plane_at == n_plane - 1, 0.0, take(1, 16))

            def pick(table, index):
                return jnp.take_along_axis(table, index, axis=1, mode="promise_in_bounds")

            for h in range(2):
                got = [take(0, h * 8 + x) for x in range(7)]
                place = got[6].astype(jnp.int32)
                size = jnp.abs(place)
                on_row = size <= half_cb
                spot = jnp.clip(size - 1, 0, half_cb - 1)
                line = jnp.clip(size - half_cb - 1, 0, ca // 2 - 1)
                line = jnp.where(on_row, jnp.where(place < 0, ca // 2 - 1, 0), line)
                inside = size == half_cb + ca
                in_column = jnp.logical_not(jnp.logical_or(on_row, inside))
                first_row = jnp.logical_and(on_row, place > 0)
                last_row = jnp.logical_and(on_row, place < 0)
                first_column = jnp.logical_or(size == 1, jnp.logical_and(in_column, place > 0))
                last_column = jnp.logical_or(
                    size == half_cb, jnp.logical_and(in_column, place < 0)
                )
                flux = got[0]
                skew = got[1] + got[2]
                for tables, here in ((above, first_row), (below, last_row)):
                    flux += jnp.where(here, pick(tables[0], spot), 0.0)
                    skew += jnp.where(here, pick(tables[1], spot), 0.0)
                for table, base, here in (
                    (before, 2 * ca, first_column),
                    (behind, 0, last_column),
                ):
                    flux += jnp.where(here, pick(table, 2 * line + base), 0.0)
                    skew += jnp.where(here, pick(table, 2 * line + base + ca), 0.0)
                spread = jnp.full((8, LANES), width_ref[0], F32)
                for k in range(1, plumes):
                    spread = jnp.where(got[3] == float(k), width_ref[k], spread)
                values = (
                    jnp.where(place != 0, jnp.sqrt(1.0 + flux * flux), 0.0),
                    (sections - 1) * jax.nn.sigmoid(skew),
                    1.0 / spread,
                    got[4],
                    got[5],
                )
                for x, value in enumerate(values):
                    par[x, pl.ds(pl.multiple_of(b * 8, 8), 8), h * LANES : (h + 1) * LANES] = value

        span = SOURCES * SLOTS
        level = lax.broadcasted_iota(jnp.int32, (sections, span), 0).astype(F32)
        index_a = lax.broadcasted_iota(jnp.int32, (ca, span), 0).astype(F32).astype(BF16)
        index_b = lax.broadcasted_iota(jnp.int32, (cb, span), 0).astype(F32).astype(BF16)

        def build(step, left, right):
            strength, center, inverse, along, across = (
                jnp.concatenate(
                    [par[x, pl.ds(step * SOURCES + t, 1), :] for t in range(SOURCES)], axis=1
                )
                for x in range(5)
            )
            scaled = (level - center) * inverse
            weights = 1.0 / (1.0 + scaled * scaled)
            mass[...] = weights * (strength / jnp.sum(weights, axis=0, keepdims=True))
            mask = jnp.where(along.astype(BF16) == index_a, jnp.ones((),BF16), jnp.zeros((),BF16))
            right[...] = jnp.where(across.astype(BF16) == index_b, jnp.ones((),BF16), jnp.zeros((),BF16))
            for k in range(sections):
                left[k * ca : (k + 1) * ca] = (
                    jnp.broadcast_to(mass[k : k + 1], (ca, span)).astype(BF16) * mask
                )

        def add(left, right, first, count):
            added = dot_last(left[first * ca : (first + count) * ca], right[...])
            tiles = jnp.stack(
                [
                    added[:, h * LANES : (h + 1) * LANES].reshape(count * ca // 8, 8, LANES)
                    for h in range(2)
                ],
                axis=1,
            )
            obuf[first : first + count] += tiles.reshape(count, 2 * ca, LANES)

        build(0, left_even, right_even)
        fill.wait()
        steps = owners // SOURCES

        @pl.loop(0, steps // 2 - 1)
        def _(i):
            add(left_even, right_even, 0, sections)
            build(2 * i + 1, left_odd, right_odd)
            add(left_odd, right_odd, 0, sections)
            build(2 * i + 2, left_even, right_even)

        add(left_even, right_even, 0, sections)
        build(steps - 1, left_odd, right_odd)
        each = sections // PIECES
        stores = []
        for c in range(PIECES):
            add(left_odd, right_odd, c * each, each)
            at = pl.ds(c * each, each)
            stores.append(
                pltpu.make_async_copy(obuf.at[at], out_whole.at[at], out_sem.at[c])
            )
            stores[-1].start()
        for store in stores:
            store.wait()


def body(n_slab, n_plane, fields, evap_rates, coal_kernel, plume_width, owner_map, deposit_cell, plume_ids):
    _, sections, ca, cb = fields.shape
    exit_rows = owner_map.shape[1]
    owners = n_slab * n_plane
    rows = sections * ca
    fold = jnp.asarray(fold_matrix(sections), BF16)
    kept = fold.shape[1]
    hbm = pl.BlockSpec(memory_space=pl.ANY)
    vmem = pl.BlockSpec(memory_space=pltpu.VMEM)
    held, rows_in, sides_in = pl.pallas_call(
        functools.partial(kernel, n_slab, n_plane, sections, ca, cb, exit_rows),
        out_shape=[
            pltpu.VMEM((2 * rows + sections * PAD, LANES), F32),
            pltpu.VMEM((owners, 16, LANES), BF16),
            pltpu.VMEM((owners, 3, 1, LANES), F32),
        ],
        in_specs=[hbm] * 7,
        out_specs=[vmem] * 3,
        scratch_shapes=[
            pltpu.VMEM((2 * rows + sections * PAD, LANES), F32),
            pltpu.VMEM((ca + 2, sections, cb), F32),
            pltpu.VMEM((2, sections, cb), F32),
            pltpu.VMEM((3, sections, LANES), F32),
            pltpu.VMEM((sections * sections, kept), BF16),
            pltpu.VMEM((2, rows // LANES, LANES), F32),
            pltpu.VMEM((2, rows // LANES, LANES), F32),
            pltpu.VMEM((2, rows // LANES, LANES), F32),
            pltpu.VMEM((8, exit_rows), F32),
            pltpu.VMEM((owners, 16, LANES), BF16),
            pltpu.SMEM(evap_rates.shape, F32),
            pltpu.VMEM(coal_kernel.shape, BF16),
            pltpu.VMEM((1, exit_rows), jnp.int32),
            pltpu.VMEM((1, exit_rows), jnp.int32),
            pltpu.VMEM((1, exit_rows), jnp.int32),
            pltpu.VMEM((owners * 8, exit_rows), BF16),
            pltpu.VMEM((SLOTS, exit_rows), BF16),
            pltpu.SemaphoreType.DMA,
            pltpu.SemaphoreType.DMA((4,)),
            pltpu.SemaphoreType.DMA((4,)),
            pltpu.SemaphoreType.DMA((4,)),
            pltpu.SemaphoreType.DMA((owners,)),
            pltpu.SemaphoreType.DMA((owners,)),
            pltpu.VMEM((3, 1, LANES), F32),
            pltpu.SemaphoreType.DMA((owners,)),
            pltpu.SemaphoreType.DMA((owners,)),
        ],
        compiler_params=pltpu.CompilerParams(
            collective_id=0, has_side_effects=True, vmem_limit_bytes=VMEM_BYTES
        ),
    )(
        fields.reshape(rows // 8, 8, 2, LANES).transpose(0, 2, 1, 3).reshape(2 * rows, LANES), evap_rates, coal_kernel, fold,
        owner_map, deposit_cell, plume_ids,
    )
    span = SOURCES * SLOTS
    out = pl.pallas_call(
        functools.partial(finish, n_plane, owners, sections, ca, cb),
        out_shape=jax.ShapeDtypeStruct((2 * rows, LANES), F32),
        in_specs=[vmem, vmem, vmem, hbm],
        out_specs=hbm,
        scratch_shapes=[
            pltpu.VMEM((sections, 2 * ca, LANES), F32),
            pltpu.VMEM(((owners + 2 * n_plane) * LINES, LANES), F32),
            pltpu.VMEM((5, owners, SLOTS), F32),
            pltpu.VMEM((sections, span), F32),
            pltpu.VMEM((rows, span), BF16),
            pltpu.VMEM((rows, span), BF16),
            pltpu.VMEM((cb, span), BF16),
            pltpu.VMEM((cb, span), BF16),
            pltpu.SMEM(plume_width.shape, F32),
            pltpu.SemaphoreType.DMA,
            pltpu.SemaphoreType.DMA((PIECES + 1,)),
        ],
        compiler_params=pltpu.CompilerParams(vmem_limit_bytes=VMEM_BYTES),
    )(
        pltpu.with_memory_space_constraint(held, pltpu.VMEM),
        pltpu.with_memory_space_constraint(rows_in, pltpu.VMEM),
        pltpu.with_memory_space_constraint(sides_in, pltpu.VMEM),
        plume_width,
    )
    out = out.reshape(rows // 8, 2, 8, LANES).transpose(0, 2, 1, 3)
    return out.reshape(1, sections, ca, cb)


def solution(mesh):
    return jax.shard_map(
        functools.partial(body, mesh.shape["slab"], mesh.shape["plane"]),
        mesh=mesh,
        in_specs=(
            P("group", None, "slab", "plane"),
            P(),
            P(),
            P(),
            P(("slab", "plane"), None),
            P(("slab", "plane"), None),
            P(("slab", "plane"), None),
        ),
        out_specs=P("group", None, "slab", "plane"),
        check_vma=False,
    )
```

```python
import functools

import jax
import jax.numpy as jnp
import numpy as np
from jax import lax
from jax.experimental import pallas as pl
from jax.experimental.pallas import tpu as pltpu
from jax.sharding import PartitionSpec as P

MESH = pl.DeviceIdType.MESH
F32 = jnp.float32
BF16 = jnp.bfloat16
LANES = 128
SLOTS = 256
CHUNK = 8
PAD = 8
LINES = 24
SOURCES = 4
PIECES = 2
VMEM_BYTES = 56 * 1024 * 1024

cfl_nozzle = 0.35
diffusion = 0.2
relax_rate = 5.0
relax_step = 0.1
collide_step = 0.25


def fold_matrix(sections):
    kept = [(i, j) for i in range(sections) for j in range(i // 8 * 8, sections)]
    fold = np.zeros((sections * sections, len(kept)), np.float32)
    for q, (i, j) in enumerate(kept):
        fold[i * sections + j, q] = 1.0
        if j // 8 > i // 8:
            fold[j * sections + i, q] = 1.0
    return fold


def pair_terms(m):
    sections, width = m.shape
    pieces = []
    for i in range(sections):
        low = i // 8 * 8
        pieces.append(jnp.broadcast_to(m[i : i + 1], (sections - low, width)) * m[low:])
    return jnp.concatenate(pieces, axis=0).astype(BF16)


def split_hi_lo(x):
    hi = x.astype(BF16)
    lo = (x - hi.astype(F32)).astype(BF16)
    return hi, lo


def dot_last(a, b):
    return lax.dot_general(a, b, (((1,), (1,)), ((), ())), preferred_element_type=F32)


def kernel(
    n_slab, n_plane, sections, ca, cb, exit_rows,
    fields_hbm, evap_hbm, coal_hbm, fold_hbm, owner_hbm, cell_hbm, pid_hbm,
    obuf, recv_buf,
    fbuf, tbuf, edge_in, upright_buf, fold, cols_out, cols_near, cols_in, par, send_buf,
    evap_ref, coal_ref, owner_ref, cell_ref, pid_ref, picks, in_slot,
    in_sem, arg_sem, halo_send, halo_recv, row_send, row_recv,
):
    owners = n_slab * n_plane
    rows = sections * ca
    g = lax.axis_index("group")
    s = lax.axis_index("slab")
    p = lax.axis_index("plane")
    me = s * n_plane + p
    barrier = pltpu.get_barrier_semaphore()

    @pl.when(g == 1)
    def _():
        for i in range(n_slab):
            row = jnp.where(2 * s < n_slab, n_slab - 1 - i, i)
            for j in range(n_plane):
                pl.semaphore_signal(barrier, inc=1, device_id=(0, row, j), device_id_type=MESH)


    fpad = fbuf.reshape(sections, 2 * ca + PAD, LANES).at[:, pl.ds(0, 2 * ca), :]
    opad = obuf.reshape(sections, 2 * ca + PAD, LANES).at[:, pl.ds(0, 2 * ca), :]
    load = pltpu.make_async_copy(
        fields_hbm.reshape(sections, 2 * ca, LANES), fpad, in_sem
    )
    load.start()
    nozzle_args = [
        pltpu.make_async_copy(source, target, arg_sem.at[k])
        for k, (source, target) in enumerate(
            ((owner_hbm, owner_ref), (cell_hbm, cell_ref), (pid_hbm, pid_ref))
        )
    ]
    spray_args = [
        pltpu.make_async_copy(source, target, arg_sem.at[k])
        for k, (source, target) in enumerate(
            ((evap_hbm, evap_ref), (coal_hbm, coal_ref), (fold_hbm, fold))
        )
    ]

    @pl.when(g == 0)
    def _():
        for copy in nozzle_args:
            copy.start()

    @pl.when(g == 1)
    def _():
        for copy in spray_args:
            copy.start()

    sides = [
        (s > 0, (g, s - 1, p)),
        (s < n_slab - 1, (g, s + 1, p)),
        (p > 0, (g, s, p - 1)),
        (p < n_plane - 1, (g, s, p + 1)),
    ]
    near = 0
    for there, target in sides:
        near = near + there.astype(jnp.int32)

        @pl.when(there)
        def _():
            pl.semaphore_signal(barrier, inc=1, device_id=target, device_id_type=MESH)

    load.wait()

    def lines(a, h):
        return pl.ds(a // 8 * 16 + h * 8 + a % 8, sections, stride=2 * ca + PAD)

    def gather_row(ref, a):
        return jnp.concatenate([ref[lines(a, h), :] for h in range(2)], axis=1)

    def half(ref, h):
        return ref[...].reshape(rows // 8, 2, 8, LANES)[:, h].reshape(rows, LANES)

    def halo(kind, target):
        source, landing = (
            (tbuf.at[ca], edge_in.at[0]),
            (tbuf.at[1], edge_in.at[1]),
            (cols_out.at[1], cols_in.at[0]),
            (cols_out.at[0], cols_in.at[1]),
        )[kind]
        return pltpu.make_async_remote_copy(
            src_ref=source,
            dst_ref=landing,
            send_sem=halo_send.at[kind],
            recv_sem=halo_recv.at[kind],
            device_id=target,
            device_id_type=MESH,
        )

    outgoing = (sides[1], sides[0], sides[3], sides[2])
    def start_halo(kinds):
        for kind in kinds:

            @pl.when(outgoing[kind][0])
            def _():
                halo(kind, outgoing[kind][1]).start()

    def extract_columns():
        for a in (0, ca - 1):
            tbuf[a + 1] = gather_row(fbuf, a)

        lane = lax.broadcasted_iota(jnp.int32, (8, LANES), 1)
        line = lax.broadcasted_iota(jnp.int32, (8, LANES), 0)
        for h, (outer, inner) in enumerate(((0, 1), (LANES - 1, LANES - 2))):
            select = jnp.logical_or(
                jnp.logical_and(line == 0, lane == outer), jnp.logical_and(line == 1, lane == inner)
            ).astype(BF16)
            columns = dot_last(select, half(fpad, h).astype(BF16))
            for x in range(rows // LANES):
                at = slice(x * LANES, (x + 1) * LANES)
                cols_out[h, x : x + 1] = columns[0:1, at]
                cols_near[h, x : x + 1] = columns[1:2, at]

    def fill_rows():
        @pl.loop(1, ca - 1)
        def _(a):
            tbuf[a + 1] = gather_row(fbuf, a)

        for kind, landing in enumerate((edge_in.at[0], edge_in.at[1], cols_in.at[0], cols_in.at[1])):

            @pl.when(jnp.logical_not(sides[kind][0]))
            def _():
                landing[...] = jnp.zeros(landing.shape, F32)

    def wait_halo():
        for kind in range(4):

            @pl.when(outgoing[kind][0])
            def _():
                halo(kind, outgoing[kind][1]).wait_send()

            @pl.when(sides[kind][0])
            def _():
                halo(kind, outgoing[kind][1]).wait_recv()

    def placed_columns():
        sub = lax.broadcasted_iota(jnp.int32, (16, cb), 0)
        lanes = lax.broadcasted_iota(jnp.int32, (16, cb), 1)
        lined = [
            jnp.concatenate([cols_in[h, x : x + 1] for x in range(rows // LANES)], axis=1)
            for h in range(2)
        ]
        stack = jnp.concatenate(lined + [jnp.zeros((14, rows), F32)], axis=0)
        place = jnp.logical_or(
            jnp.logical_and(sub == 0, lanes == 0), jnp.logical_and(sub == 1, lanes == cb - 1)
        ).astype(BF16)
        return jnp.dot(stack.T.astype(BF16), place, preferred_element_type=F32)

    col_lane = lax.broadcasted_iota(jnp.int32, (sections, cb), 1)
    col_row = lax.broadcasted_iota(jnp.int32, (sections, cb), 0)

    def neighbours(a):
        c = tbuf[a + 1]
        up = tbuf[a]
        left = jnp.where(col_lane == 0, 0.0, pltpu.roll(c, 1, 1))
        right = jnp.where(col_lane == cb - 1, 0.0, pltpu.roll(c, cb - 1, 1))
        lap = up + tbuf[a + 2] + (left + right) - 4.0 * c
        return c, up, lap

    def scatter_row(a, value):
        for h in range(2):
            obuf[lines(a, h), :] = value[:, h * LANES : (h + 1) * LANES]

    @pl.when(g == 0)
    def _():
        for copy in nozzle_args:
            copy.wait()
        owner = owner_ref[...]
        slots = []
        below = lax.broadcasted_iota(jnp.int32, (256, 256), 0)
        after = lax.broadcasted_iota(jnp.int32, (256, 256), 1)
        upto = (below <= after).astype(BF16)
        names = lax.broadcasted_iota(jnp.int32, (owners, 256), 0)
        carry = jnp.zeros((owners, 1), F32)
        for j in range(exit_rows // 256):
            hit = (owner[:, j * 256 : (j + 1) * 256] == names).astype(F32)
            count = jnp.dot(hit.astype(BF16), upto, preferred_element_type=F32) + carry
            slots.append(jnp.sum(hit * (count - 1.0), axis=0, keepdims=True))
            carry = count[:, 255:256]
        slot = jnp.concatenate(slots, axis=1)
        cell = cell_ref[...]
        across = jnp.bitwise_and(cell, cb - 1)
        along = jnp.right_shift(cell, cb.bit_length() - 1)
        par[3:4] = pid_ref[...].astype(F32)
        par[4:5] = along.astype(F32)
        par[5:6] = across.astype(F32)
        half_cb = cb // 2
        last_line = ca // 2 - 1
        number = lax.broadcasted_iota(jnp.int32, (1, exit_rows), 1)
        spot = jnp.bitwise_and(number, half_cb - 1)
        line = jnp.right_shift(number, half_cb.bit_length() - 1)
        beside = half_cb + 1 + line
        place = jnp.where(spot == half_cb - 1, -beside, half_cb + ca)
        place = jnp.where(spot == 0, beside, place)
        place = jnp.where(line == last_line, -1 - spot, place)
        par[6:7] = jnp.where(line == 0, 1 + spot, place).astype(F32)
        par[7:8] = jnp.zeros((1, exit_rows), F32)
        places = lax.broadcasted_iota(jnp.int32, (SLOTS, exit_rows), 0).astype(F32)
        in_slot[...] = (slot == places).astype(BF16)
        group = 16
        label = jnp.right_shift(lax.broadcasted_iota(jnp.int32, (group * 8, exit_rows), 0), 3)

        @pl.loop(0, owners // group)
        def _(b):
            picks[pl.ds(pl.multiple_of(b * group * 8, group * 8), group * 8)] = (
                owner == label + b * group
            ).astype(BF16)

        halve = jnp.where(
            jnp.right_shift(lax.broadcasted_iota(jnp.int32, (cb, cb // 2), 0), 1)
            == lax.broadcasted_iota(jnp.int32, (cb, cb // 2), 1),
            0.25,
            0.0,
        ).astype(BF16)

        layers = sections // 4
        plane_row = lax.broadcasted_iota(jnp.int32, (ca, cb), 0)
        plane_lane = lax.broadcasted_iota(jnp.int32, (ca, cb), 1)

        def plane(k):
            tiles = fbuf[pl.ds(k * (2 * ca + PAD), 2 * ca), :].reshape(ca // 8, 2, 8, LANES)
            return jnp.concatenate([tiles[:, h].reshape(ca, LANES) for h in range(2)], axis=1)

        def plane_lap(c):
            up = jnp.where(plane_row == 0, 0.0, pltpu.roll(c, 1, 0))
            down = jnp.where(plane_row == ca - 1, 0.0, pltpu.roll(c, ca - 1, 0))
            left = jnp.where(plane_lane == 0, 0.0, pltpu.roll(c, 1, 1))
            right = jnp.where(plane_lane == cb - 1, 0.0, pltpu.roll(c, cb - 1, 1))
            return up + down + (left + right) - 4.0 * c

        last = [v * layers + layers - 1 for v in range(4)]
        d, m, q, e = (plane(k) for k in last)
        if layers > 1:
            dm, dq, de = (x - plane(k - 1) for x, k in zip((m, q, e), last[1:]))
        else:
            dm, dq, de = m, q, e
        relaxing = relax_rate / (1.0 + d * d)
        skew = e - 2.0 * q
        new_flux = m - cfl_nozzle * (dm + dq) + diffusion * plane_lap(m)
        new_skew = (
            skew
            - cfl_nozzle * (de - 2.0 * dq)
            - (2.0 * relax_step) * relaxing * (e - q)
            + diffusion * plane_lap(skew)
        )
        planes = jnp.concatenate([new_flux, new_skew, diffusion * m, diffusion * skew], axis=0)
        paired = planes + pltpu.roll(planes, 4 * ca - 1, 0)
        edge_rows = jnp.concatenate(
            [planes[(2 + v) * ca + a : (2 + v) * ca + a + 1] for a in (0, ca - 1) for v in range(2)]
            + [jnp.zeros((4, cb), F32)],
            axis=0,
        )
        summed = jnp.concatenate([paired[: 2 * ca], edge_rows], axis=0)
        hi = summed.astype(BF16)
        rest = summed - hi.astype(F32)
        mid, low = split_hi_lo(rest)
        count = 2 * ca + 8
        sums = jnp.dot(
            jnp.concatenate([hi, mid, low], axis=0), halve, preferred_element_type=F32
        )
        coarse = sums[:count] + sums[count : 2 * count] + sums[2 * count :]
        flux_part = coarse[:ca].astype(BF16).astype(F32)
        skew_hi, skew_lo = split_hi_lo(coarse[ca : 2 * ca])
        for k, part in enumerate((flux_part, skew_hi.astype(F32), skew_lo.astype(F32))):
            for i in range(ca // 2):
                par[k : k + 1, i * (cb // 2) : (i + 1) * (cb // 2)] = part[2 * i : 2 * i + 1]
        side_hi, side_lo = split_hi_lo(0.25 * paired[2 * ca :])
        lane = lax.broadcasted_iota(jnp.int32, (8, cb), 1)
        line = lax.broadcasted_iota(jnp.int32, (8, cb), 0)
        ends = jnp.logical_or(
            jnp.logical_and(line == 0, lane == 0), jnp.logical_and(line == 1, lane == cb - 1)
        ).astype(BF16)
        side = dot_last(ends, side_hi) + dot_last(ends, side_lo)
        edge = coarse[2 * ca :]
        more = jnp.concatenate(
            [
                jnp.concatenate([side[0:1], side[1:2]], axis=1),
                edge[1:2],
                edge[3:4],
                jnp.zeros((5, LANES), F32),
            ],
            axis=0,
        )
        blank = jnp.zeros((7, LANES), F32)
        edges = [jnp.concatenate([blank, edge[2 * x : 2 * x + 1]], axis=0) for x in range(2)]

        values = par[...].astype(BF16)
        tiled = jnp.concatenate([values] * group, axis=0)

        @pl.loop(0, owners // group)
        def _(b):
            picked = tiled * picks[pl.ds(pl.multiple_of(b * group * 8, group * 8), group * 8)]
            packed = dot_last(picked, in_slot[...]).reshape(group, 8, SLOTS)
            send_buf[pl.ds(b * group, group)] = jnp.concatenate(
                [
                    packed[:, :, :LANES] + edges[0][None],
                    packed[:, :, LANES:] + edges[1][None],
                    jnp.broadcast_to(more[None], (group, 8, LANES)),
                ],
                axis=1,
            ).astype(BF16)

        pl.semaphore_wait(barrier, near + owners)

        for i in range(n_slab):
            row = jnp.where(2 * s < n_slab, n_slab - 1 - i, i)
            for j in range(n_plane):
                pltpu.make_async_remote_copy(
                    src_ref=send_buf.at[row * n_plane + j],
                    dst_ref=recv_buf.at[me],
                    send_sem=row_send.at[row * n_plane + j],
                    recv_sem=row_recv.at[me],
                    device_id=(1, row, j),
                    device_id_type=MESH,
                ).start()

        extract_columns()
        start_halo((0, 1, 2, 3))
        fill_rows()
        for a in (0, ca + 1):
            tbuf[a] = jnp.zeros((sections, cb), F32)

        @pl.loop(0, ca // CHUNK)
        def _(step):
            for t in range(CHUNK):
                a = step * CHUNK + t
                c, _, lap = neighbours(a)
                back = jnp.where(jnp.bitwise_and(col_row, layers - 1) == 0, 0.0, pltpu.roll(c, 1, 0))
                du = c - back
                d, m, q, e = (c[v * layers : (v + 1) * layers] for v in range(4))
                dm, dq, de = (du[v * layers : (v + 1) * layers] for v in (1, 2, 3))
                relaxing = relax_rate / (1.0 + d * d)
                fresh = diffusion * lap + jnp.concatenate(
                    [
                        d - cfl_nozzle * dm,
                        m - cfl_nozzle * (dm + dq),
                        q + relax_step * relaxing * (e - q) - cfl_nozzle * dq,
                        e - cfl_nozzle * de,
                    ],
                    axis=0,
                )
                scatter_row(a, fresh)

        wait_halo()
        placed = diffusion * placed_columns()
        opad[...] += jnp.stack(
            [placed[:, h * LANES : (h + 1) * LANES].reshape(rows // 8, 8, LANES) for h in range(2)],
            axis=1,
        ).reshape(sections, 2 * ca, LANES)
        for side, a in enumerate((0, ca - 1)):
            for h in range(2):
                obuf[lines(a, h), :] += diffusion * edge_in[side, :, h * LANES : (h + 1) * LANES]

        @pl.loop(0, owners)
        def _(o):
            pltpu.make_async_remote_copy(
                src_ref=send_buf.at[o],
                dst_ref=recv_buf.at[me],
                send_sem=row_send.at[o],
                recv_sem=row_recv.at[me],
                device_id=(1, o // n_plane, o % n_plane),
                device_id_type=MESH,
            ).wait_send()

    @pl.when(g == 1)
    def _():
        extract_columns()
        pl.semaphore_wait(barrier, near)
        start_halo((0, 1, 2, 3))
        fill_rows()
        for copy in spray_args:
            copy.wait()
        folded = jnp.dot(coal_ref[...], fold[...], preferred_element_type=F32).astype(BF16)
        evap = jnp.zeros((sections, cb), F32)
        for k in range(sections):
            evap = jnp.where(col_row == k, evap_ref[k], evap)
        speeds = 0.2 + 0.5 * col_row.astype(F32) / (sections - 1)
        for a in (0, ca + 1):
            tbuf[a] = jnp.zeros((sections, cb), F32)

        def moved_from(c, up, lap):
            width = c.shape[1]
            lost = evap[:, :width] * c
            gained = jnp.where(
                col_row[:, :width] == sections - 1, 0.0, pltpu.roll(lost, sections - 1, 0)
            )
            return c - speeds[:, :width] * (c - up) + diffusion * lap - lost + gained

        def collide(moved):
            first = [jnp.dot(folded, pair_terms(x), preferred_element_type=F32) for x in moved]
            middle = [x + (0.5 * collide_step) * y for x, y in zip(moved, first)]
            second = [jnp.dot(folded, pair_terms(x), preferred_element_type=F32) for x in middle]
            return [x + collide_step * y for x, y in zip(moved, second)]

        @pl.loop(0, ca // CHUNK)
        def _(step):
            size = CHUNK // 2
            moved = [
                jnp.concatenate(
                    [moved_from(*neighbours(step * CHUNK + z * size + t)) for t in range(size)],
                    axis=1,
                )
                for z in range(2)
            ]
            for z, mixed in enumerate(collide(moved)):
                for t in range(size):
                    scatter_row(step * CHUNK + z * size + t, mixed[:, t * cb : (t + 1) * cb])

        wait_halo()
        for side, a in enumerate((0, ca + 1)):
            tbuf[a] = edge_in[side]
        tile_lane = lax.broadcasted_iota(jnp.int32, (8, LANES), 1)
        wide_lane = lax.broadcasted_iota(jnp.int32, (sections, LANES), 1)

        def upright(x, pair):
            folds = LANES // ca
            for k in range(folds):
                turned = [
                    pltpu.roll(pair[h], (LANES + (h - k) * ca) % LANES, 1) for h in range(2)
                ]
                upright_buf[x, pl.ds(k, sections // folds, stride=folds), :] = jnp.where(
                    tile_lane < ca, turned[0], turned[1]
                )
            return upright_buf[x]

        own = upright(0, (cols_out[0], cols_out[1]))
        inner = upright(1, (cols_near[0], cols_near[1]))
        outer = upright(2, (cols_in[0], cols_in[1]))
        above = pltpu.roll(own, 1, 1)
        below = pltpu.roll(own, LANES - 1, 1)
        parts = []
        for a in (0, ca - 1):
            c, up, lap = neighbours(a)
            lap += jnp.where(col_lane == 0, outer[:, a : a + 1], 0.0)
            lap += jnp.where(col_lane == cb - 1, outer[:, ca + a : ca + a + 1], 0.0)
            parts.append(moved_from(c, up, lap))
        parts.append(moved_from(own, above, above + below + inner + outer - 4.0 * own))
        (mixed,) = collide([jnp.concatenate(parts, axis=1)])
        columns = mixed[:, 2 * cb :]
        for a in range(1, ca - 1):
            for h, target in enumerate((0, LANES - 1)):
                at = lines(a, h)
                obuf[at, :] = jnp.where(
                    wide_lane == target,
                    pltpu.roll(columns, (LANES + target - h * ca - a) % LANES, 1),
                    obuf[at, :],
                )
        for x, a in enumerate((0, ca - 1)):
            scatter_row(a, mixed[:, x * cb : (x + 1) * cb])

        @pl.loop(0, owners)
        def _(o):
            pltpu.make_async_remote_copy(
                src_ref=send_buf.at[o],
                dst_ref=recv_buf.at[o],
                send_sem=row_send.at[o],
                recv_sem=row_recv.at[o],
                device_id=(0, s, p),
                device_id_type=MESH,
            ).wait_recv()


def finish(
    n_plane, owners, sections, ca, cb,
    held, rows_in, width_hbm,
    out_hbm,
    obuf, flat, par, mass, left_even, left_odd, right_even, right_odd, width_ref, arg_sem, out_sem,
):
    plumes = width_ref.shape[0]
    rows = sections * ca
    g = lax.axis_index("group")
    whole = held.reshape(sections, 2 * ca + PAD, LANES).at[:, pl.ds(0, 2 * ca), :]
    out_whole = out_hbm.reshape(sections, 2 * ca, LANES)

    @pl.when(g == 0)
    def _():
        copy = pltpu.make_async_copy(whole, out_whole, out_sem.at[0])
        copy.start()
        copy.wait()

    @pl.when(g == 1)
    def _():
        fetch = pltpu.make_async_copy(width_hbm, width_ref, arg_sem)
        fetch.start()
        half_cb = cb // 2
        pad = n_plane * LINES
        flat[pl.ds(0, pad)] = jnp.zeros((pad, LANES), F32)
        flat[pl.ds(pad + owners * LINES, pad)] = jnp.zeros((pad, LANES), F32)

        @pl.loop(0, owners // 8, unroll=2)
        def _(b):
            for o in range(8):
                at = pl.multiple_of(pad + (b * 8 + o) * LINES, 8)
                flat[pl.ds(at, LINES)] = rows_in[b * 8 + o].astype(F32)

        fetch.wait()
        sub = lax.broadcasted_iota(jnp.int32, (8, LANES), 0)

        @pl.loop(0, owners // 8, unroll=2)
        def _(b):
            def take(shift, line):
                return flat[pl.ds(pad + (b * 8 + shift) * LINES + line, 8, stride=LINES), :]

            plane_at = lax.rem(b * 8 + sub, n_plane)
            above = take(-n_plane, 15), take(-n_plane, 18)
            below = take(n_plane, 7), take(n_plane, 17)
            before = jnp.where(plane_at == 0, 0.0, take(-1, 16))
            behind = jnp.where(plane_at == n_plane - 1, 0.0, take(1, 16))

            def pick(table, index):
                return jnp.take_along_axis(table, index, axis=1, mode="promise_in_bounds")

            for h in range(2):
                got = [take(0, h * 8 + x) for x in range(7)]
                place = got[6].astype(jnp.int32)
                size = jnp.abs(place)
                on_row = size <= half_cb
                spot = jnp.clip(size - 1, 0, half_cb - 1)
                line = jnp.clip(size - half_cb - 1, 0, ca // 2 - 1)
                line = jnp.where(on_row, jnp.where(place < 0, ca // 2 - 1, 0), line)
                inside = size == half_cb + ca
                in_column = jnp.logical_not(jnp.logical_or(on_row, inside))
                first_row = jnp.logical_and(on_row, place > 0)
                last_row = jnp.logical_and(on_row, place < 0)
                first_column = jnp.logical_or(size == 1, jnp.logical_and(in_column, place > 0))
                last_column = jnp.logical_or(
                    size == half_cb, jnp.logical_and(in_column, place < 0)
                )
                flux = got[0]
                skew = got[1] + got[2]
                for tables, here in ((above, first_row), (below, last_row)):
                    flux += jnp.where(here, pick(tables[0], spot), 0.0)
                    skew += jnp.where(here, pick(tables[1], spot), 0.0)
                for table, base, here in (
                    (before, 2 * ca, first_column),
                    (behind, 0, last_column),
                ):
                    flux += jnp.where(here, pick(table, 2 * line + base), 0.0)
                    skew += jnp.where(here, pick(table, 2 * line + base + ca), 0.0)
                spread = jnp.full((8, LANES), width_ref[0], F32)
                for k in range(1, plumes):
                    spread = jnp.where(got[3] == float(k), width_ref[k], spread)
                values = (
                    jnp.where(place != 0, jnp.sqrt(1.0 + flux * flux), 0.0),
                    (sections - 1) * jax.nn.sigmoid(skew),
                    1.0 / spread,
                    got[4],
                    got[5],
                )
                for x, value in enumerate(values):
                    par[x, pl.ds(pl.multiple_of(b * 8, 8), 8), h * LANES : (h + 1) * LANES] = value

        span = SOURCES * SLOTS
        level = lax.broadcasted_iota(jnp.int32, (sections, span), 0).astype(F32)
        index_a = lax.broadcasted_iota(jnp.int32, (ca, span), 0).astype(F32).astype(BF16)
        index_b = lax.broadcasted_iota(jnp.int32, (cb, span), 0).astype(F32).astype(BF16)

        def build(step, left, right):
            strength, center, inverse, along, across = (
                jnp.concatenate(
                    [par[x, pl.ds(step * SOURCES + t, 1), :] for t in range(SOURCES)], axis=1
                )
                for x in range(5)
            )
            scaled = (level - center) * inverse
            weights = 1.0 / (1.0 + scaled * scaled)
            mass[...] = weights * (strength / jnp.sum(weights, axis=0, keepdims=True))
            mask = jnp.where(along.astype(BF16) == index_a, jnp.ones((),BF16), jnp.zeros((),BF16))
            right[...] = jnp.where(across.astype(BF16) == index_b, jnp.ones((),BF16), jnp.zeros((),BF16))
            for k in range(sections):
                left[k * ca : (k + 1) * ca] = (
                    jnp.broadcast_to(mass[k : k + 1], (ca, span)).astype(BF16) * mask
                )

        def add(left, right, first, count, base):
            added = dot_last(left[first * ca : (first + count) * ca], right[...])
            tiles = jnp.stack(
                [
                    added[:, h * LANES : (h + 1) * LANES].reshape(count * ca // 8, 8, LANES)
                    for h in range(2)
                ],
                axis=1,
            )
            obuf[first : first + count] = base[first : first + count] + tiles.reshape(
                count, 2 * ca, LANES
            )

        build(0, left_even, right_even)
        steps = owners // SOURCES

        add(left_even, right_even, 0, sections, whole)
        build(1, left_odd, right_odd)

        @pl.loop(1, steps // 2)
        def _(i):
            add(left_odd, right_odd, 0, sections, obuf)
            build(2 * i, left_even, right_even)
            add(left_even, right_even, 0, sections, obuf)
            build(2 * i + 1, left_odd, right_odd)

        each = sections // PIECES
        stores = []
        for c in range(PIECES):
            add(left_odd, right_odd, c * each, each, obuf)
            at = pl.ds(c * each, each)
            stores.append(
                pltpu.make_async_copy(obuf.at[at], out_whole.at[at], out_sem.at[c])
            )
            stores[-1].start()
        for store in stores:
            store.wait()


def body(n_slab, n_plane, fields, evap_rates, coal_kernel, plume_width, owner_map, deposit_cell, plume_ids):
    _, sections, ca, cb = fields.shape
    exit_rows = owner_map.shape[1]
    owners = n_slab * n_plane
    rows = sections * ca
    fold = jnp.asarray(fold_matrix(sections), BF16)
    kept = fold.shape[1]
    hbm = pl.BlockSpec(memory_space=pl.ANY)
    vmem = pl.BlockSpec(memory_space=pltpu.VMEM)
    held, rows_in = pl.pallas_call(
        functools.partial(kernel, n_slab, n_plane, sections, ca, cb, exit_rows),
        out_shape=[
            pltpu.VMEM((2 * rows + sections * PAD, LANES), F32),
            pltpu.VMEM((owners, LINES, LANES), BF16),
        ],
        in_specs=[hbm] * 7,
        out_specs=[vmem] * 2,
        scratch_shapes=[
            pltpu.VMEM((2 * rows + sections * PAD, LANES), F32),
            pltpu.VMEM((ca + 2, sections, cb), F32),
            pltpu.VMEM((2, sections, cb), F32),
            pltpu.VMEM((3, sections, LANES), F32),
            pltpu.VMEM((sections * sections, kept), BF16),
            pltpu.VMEM((2, rows // LANES, LANES), F32),
            pltpu.VMEM((2, rows // LANES, LANES), F32),
            pltpu.VMEM((2, rows // LANES, LANES), F32),
            pltpu.VMEM((8, exit_rows), F32),
            pltpu.VMEM((owners, LINES, LANES), BF16),
            pltpu.SMEM(evap_rates.shape, F32),
            pltpu.VMEM(coal_kernel.shape, BF16),
            pltpu.VMEM((1, exit_rows), jnp.int32),
            pltpu.VMEM((1, exit_rows), jnp.int32),
            pltpu.VMEM((1, exit_rows), jnp.int32),
            pltpu.VMEM((owners * 8, exit_rows), BF16),
            pltpu.VMEM((SLOTS, exit_rows), BF16),
            pltpu.SemaphoreType.DMA,
            pltpu.SemaphoreType.DMA((4,)),
            pltpu.SemaphoreType.DMA((4,)),
            pltpu.SemaphoreType.DMA((4,)),
            pltpu.SemaphoreType.DMA((owners,)),
            pltpu.SemaphoreType.DMA((owners,)),
        ],
        compiler_params=pltpu.CompilerParams(
            collective_id=0, has_side_effects=True, vmem_limit_bytes=VMEM_BYTES
        ),
    )(
        fields.reshape(rows // 8, 8, 2, LANES).transpose(0, 2, 1, 3).reshape(2 * rows, LANES), evap_rates, coal_kernel, fold,
        owner_map, deposit_cell, plume_ids,
    )
    span = SOURCES * SLOTS
    out = pl.pallas_call(
        functools.partial(finish, n_plane, owners, sections, ca, cb),
        out_shape=jax.ShapeDtypeStruct((2 * rows, LANES), F32),
        in_specs=[vmem, vmem, hbm],
        out_specs=hbm,
        scratch_shapes=[
            pltpu.VMEM((sections, 2 * ca, LANES), F32),
            pltpu.VMEM(((owners + 2 * n_plane) * LINES, LANES), F32),
            pltpu.VMEM((5, owners, SLOTS), F32),
            pltpu.VMEM((sections, span), F32),
            pltpu.VMEM((rows, span), BF16),
            pltpu.VMEM((rows, span), BF16),
            pltpu.VMEM((cb, span), BF16),
            pltpu.VMEM((cb, span), BF16),
            pltpu.SMEM(plume_width.shape, F32),
            pltpu.SemaphoreType.DMA,
            pltpu.SemaphoreType.DMA((PIECES,)),
        ],
        compiler_params=pltpu.CompilerParams(vmem_limit_bytes=VMEM_BYTES),
    )(
        pltpu.with_memory_space_constraint(held, pltpu.VMEM),
        pltpu.with_memory_space_constraint(rows_in, pltpu.VMEM),
        plume_width,
    )
    out = out.reshape(rows // 8, 2, 8, LANES).transpose(0, 2, 1, 3)
    return out.reshape(1, sections, ca, cb)


def solution(mesh):
    return jax.shard_map(
        functools.partial(body, mesh.shape["slab"], mesh.shape["plane"]),
        mesh=mesh,
        in_specs=(
            P("group", None, "slab", "plane"),
            P(),
            P(),
            P(),
            P(("slab", "plane"), None),
            P(("slab", "plane"), None),
            P(("slab", "plane"), None),
        ),
        out_specs=P("group", None, "slab", "plane"),
        check_vma=False,
    )
```

```python
import functools

import jax
import jax.numpy as jnp
import numpy as np
from jax import lax
from jax.experimental import pallas as pl
from jax.experimental.pallas import tpu as pltpu
from jax.sharding import PartitionSpec as P

MESH = pl.DeviceIdType.MESH
F32 = jnp.float32
BF16 = jnp.bfloat16
LANES = 128
SLOTS = 256
CHUNK = 8
PAD = 8
LINES = 24
SOURCES = 4
PIECES = 2
VMEM_BYTES = 56 * 1024 * 1024

cfl_nozzle = 0.35
diffusion = 0.2
relax_rate = 5.0
relax_step = 0.1
collide_step = 0.25


def fold_matrix(sections):
    kept = [(i, j) for i in range(sections) for j in range(i // 8 * 8, sections)]
    fold = np.zeros((sections * sections, len(kept)), np.float32)
    for q, (i, j) in enumerate(kept):
        fold[i * sections + j, q] = 1.0
        if j // 8 > i // 8:
            fold[j * sections + i, q] = 1.0
    return fold


def pair_terms(m):
    sections, width = m.shape
    pieces = []
    for i in range(sections):
        low = i // 8 * 8
        pieces.append(jnp.broadcast_to(m[i : i + 1], (sections - low, width)) * m[low:])
    return jnp.concatenate(pieces, axis=0).astype(BF16)


def split_hi_lo(x):
    hi = x.astype(BF16)
    lo = (x - hi.astype(F32)).astype(BF16)
    return hi, lo


def dot_last(a, b):
    return lax.dot_general(a, b, (((1,), (1,)), ((), ())), preferred_element_type=F32)


def kernel(
    n_slab, n_plane, sections, ca, cb, exit_rows,
    fields_hbm, evap_hbm, coal_hbm, fold_hbm, width_hbm, owner_hbm, cell_hbm, pid_hbm,
    obuf, recv_buf, side_in, widths,
    fbuf, tbuf, edge_in, upright_buf, fold, cols_out, cols_near, cols_in, par, send_buf,
    evap_ref, coal_ref, width_ref, owner_ref, cell_ref, pid_ref, picks, in_slot,
    in_sem, arg_sem, halo_send, halo_recv, row_send, row_recv, side_out, side_send, side_recv,
):
    owners = n_slab * n_plane
    rows = sections * ca
    g = lax.axis_index("group")
    s = lax.axis_index("slab")
    p = lax.axis_index("plane")
    me = s * n_plane + p
    barrier = pltpu.get_barrier_semaphore()

    @pl.when(g == 1)
    def _():
        for i in range(n_slab):
            row = jnp.where(2 * s < n_slab, n_slab - 1 - i, i)
            for j in range(n_plane):
                pl.semaphore_signal(barrier, inc=1, device_id=(0, row, j), device_id_type=MESH)


    fpad = fbuf.reshape(sections, 2 * ca + PAD, LANES).at[:, pl.ds(0, 2 * ca), :]
    opad = obuf.reshape(sections, 2 * ca + PAD, LANES).at[:, pl.ds(0, 2 * ca), :]
    load = pltpu.make_async_copy(
        fields_hbm.reshape(sections, 2 * ca, LANES), fpad, in_sem
    )
    load.start()
    nozzle_args = [
        pltpu.make_async_copy(source, target, arg_sem.at[k])
        for k, (source, target) in enumerate(
            ((owner_hbm, owner_ref), (cell_hbm, cell_ref), (pid_hbm, pid_ref))
        )
    ]
    spray_args = [
        pltpu.make_async_copy(source, target, arg_sem.at[k])
        for k, (source, target) in enumerate(
            ((evap_hbm, evap_ref), (coal_hbm, coal_ref), (fold_hbm, fold), (width_hbm, width_ref))
        )
    ]

    @pl.when(g == 0)
    def _():
        for copy in nozzle_args:
            copy.start()

    @pl.when(g == 1)
    def _():
        for copy in spray_args:
            copy.start()

    sides = [
        (s > 0, (g, s - 1, p)),
        (s < n_slab - 1, (g, s + 1, p)),
        (p > 0, (g, s, p - 1)),
        (p < n_plane - 1, (g, s, p + 1)),
    ]
    near = 0
    for there, target in sides:
        near = near + there.astype(jnp.int32)

        @pl.when(there)
        def _():
            pl.semaphore_signal(barrier, inc=1, device_id=target, device_id_type=MESH)

    load.wait()

    def lines(a, h):
        return pl.ds(a // 8 * 16 + h * 8 + a % 8, sections, stride=2 * ca + PAD)

    def gather_row(ref, a):
        return jnp.concatenate([ref[lines(a, h), :] for h in range(2)], axis=1)

    def half(ref, h):
        return ref[...].reshape(rows // 8, 2, 8, LANES)[:, h].reshape(rows, LANES)

    def halo(kind, target):
        source, landing = (
            (tbuf.at[ca], edge_in.at[0]),
            (tbuf.at[1], edge_in.at[1]),
            (cols_out.at[1], cols_in.at[0]),
            (cols_out.at[0], cols_in.at[1]),
        )[kind]
        return pltpu.make_async_remote_copy(
            src_ref=source,
            dst_ref=landing,
            send_sem=halo_send.at[kind],
            recv_sem=halo_recv.at[kind],
            device_id=target,
            device_id_type=MESH,
        )

    outgoing = (sides[1], sides[0], sides[3], sides[2])
    def start_halo(kinds):
        for kind in kinds:

            @pl.when(outgoing[kind][0])
            def _():
                halo(kind, outgoing[kind][1]).start()

    def extract_columns():
        for a in (0, ca - 1):
            tbuf[a + 1] = gather_row(fbuf, a)

        lane = lax.broadcasted_iota(jnp.int32, (8, LANES), 1)
        line = lax.broadcasted_iota(jnp.int32, (8, LANES), 0)
        for h, (outer, inner) in enumerate(((0, 1), (LANES - 1, LANES - 2))):
            select = jnp.logical_or(
                jnp.logical_and(line == 0, lane == outer), jnp.logical_and(line == 1, lane == inner)
            ).astype(BF16)
            columns = dot_last(select, half(fpad, h).astype(BF16))
            for x in range(rows // LANES):
                at = slice(x * LANES, (x + 1) * LANES)
                cols_out[h, x : x + 1] = columns[0:1, at]
                cols_near[h, x : x + 1] = columns[1:2, at]

    def fill_rows():
        @pl.loop(1, ca - 1)
        def _(a):
            tbuf[a + 1] = gather_row(fbuf, a)

        for kind, landing in enumerate((edge_in.at[0], edge_in.at[1], cols_in.at[0], cols_in.at[1])):

            @pl.when(jnp.logical_not(sides[kind][0]))
            def _():
                landing[...] = jnp.zeros(landing.shape, F32)

    def wait_halo():
        for kind in range(4):

            @pl.when(outgoing[kind][0])
            def _():
                halo(kind, outgoing[kind][1]).wait_send()

            @pl.when(sides[kind][0])
            def _():
                halo(kind, outgoing[kind][1]).wait_recv()

    def placed_columns():
        sub = lax.broadcasted_iota(jnp.int32, (16, cb), 0)
        lanes = lax.broadcasted_iota(jnp.int32, (16, cb), 1)
        lined = [
            jnp.concatenate([cols_in[h, x : x + 1] for x in range(rows // LANES)], axis=1)
            for h in range(2)
        ]
        stack = jnp.concatenate(lined + [jnp.zeros((14, rows), F32)], axis=0)
        place = jnp.logical_or(
            jnp.logical_and(sub == 0, lanes == 0), jnp.logical_and(sub == 1, lanes == cb - 1)
        ).astype(BF16)
        return jnp.dot(stack.T.astype(BF16), place, preferred_element_type=F32)

    col_lane = lax.broadcasted_iota(jnp.int32, (sections, cb), 1)
    col_row = lax.broadcasted_iota(jnp.int32, (sections, cb), 0)

    def neighbours(a):
        c = tbuf[a + 1]
        up = tbuf[a]
        left = jnp.where(col_lane == 0, 0.0, pltpu.roll(c, 1, 1))
        right = jnp.where(col_lane == cb - 1, 0.0, pltpu.roll(c, cb - 1, 1))
        lap = up + tbuf[a + 2] + (left + right) - 4.0 * c
        return c, up, lap

    def scatter_row(a, value):
        for h in range(2):
            obuf[lines(a, h), :] = value[:, h * LANES : (h + 1) * LANES]

    @pl.when(g == 0)
    def _():
        for copy in nozzle_args:
            copy.wait()
        owner = owner_ref[...]
        slots = []
        below = lax.broadcasted_iota(jnp.int32, (256, 256), 0)
        after = lax.broadcasted_iota(jnp.int32, (256, 256), 1)
        upto = (below <= after).astype(BF16)
        names = lax.broadcasted_iota(jnp.int32, (owners, 256), 0)
        carry = jnp.zeros((owners, 1), F32)
        for j in range(exit_rows // 256):
            hit = (owner[:, j * 256 : (j + 1) * 256] == names).astype(F32)
            count = jnp.dot(hit.astype(BF16), upto, preferred_element_type=F32) + carry
            slots.append(jnp.sum(hit * (count - 1.0), axis=0, keepdims=True))
            carry = count[:, 255:256]
        slot = jnp.concatenate(slots, axis=1)
        cell = cell_ref[...]
        across = jnp.bitwise_and(cell, cb - 1)
        along = jnp.right_shift(cell, cb.bit_length() - 1)
        par[3:4] = pid_ref[...].astype(F32)
        par[4:5] = along.astype(F32)
        par[5:6] = across.astype(F32)
        half_cb = cb // 2
        last_line = ca // 2 - 1
        number = lax.broadcasted_iota(jnp.int32, (1, exit_rows), 1)
        spot = jnp.bitwise_and(number, half_cb - 1)
        line = jnp.right_shift(number, half_cb.bit_length() - 1)
        beside = half_cb + 1 + line
        place = jnp.where(spot == half_cb - 1, -beside, half_cb + ca)
        place = jnp.where(spot == 0, beside, place)
        place = jnp.where(line == last_line, -1 - spot, place)
        par[6:7] = jnp.where(line == 0, 1 + spot, place).astype(F32)
        par[7:8] = jnp.zeros((1, exit_rows), F32)
        places = lax.broadcasted_iota(jnp.int32, (SLOTS, exit_rows), 0).astype(F32)
        in_slot[...] = (slot == places).astype(BF16)
        group = 16
        label = jnp.right_shift(lax.broadcasted_iota(jnp.int32, (group * 8, exit_rows), 0), 3)

        @pl.loop(0, owners // group)
        def _(b):
            picks[pl.ds(pl.multiple_of(b * group * 8, group * 8), group * 8)] = (
                owner == label + b * group
            ).astype(BF16)

        halve = jnp.where(
            jnp.right_shift(lax.broadcasted_iota(jnp.int32, (cb, cb // 2), 0), 1)
            == lax.broadcasted_iota(jnp.int32, (cb, cb // 2), 1),
            0.25,
            0.0,
        ).astype(BF16)

        layers = sections // 4
        plane_row = lax.broadcasted_iota(jnp.int32, (ca, cb), 0)
        plane_lane = lax.broadcasted_iota(jnp.int32, (ca, cb), 1)

        def plane(k):
            tiles = fbuf[pl.ds(k * (2 * ca + PAD), 2 * ca), :].reshape(ca // 8, 2, 8, LANES)
            return jnp.concatenate([tiles[:, h].reshape(ca, LANES) for h in range(2)], axis=1)

        def plane_lap(c):
            up = jnp.where(plane_row == 0, 0.0, pltpu.roll(c, 1, 0))
            down = jnp.where(plane_row == ca - 1, 0.0, pltpu.roll(c, ca - 1, 0))
            left = jnp.where(plane_lane == 0, 0.0, pltpu.roll(c, 1, 1))
            right = jnp.where(plane_lane == cb - 1, 0.0, pltpu.roll(c, cb - 1, 1))
            return up + down + (left + right) - 4.0 * c

        last = [v * layers + layers - 1 for v in range(4)]
        d, m, q, e = (plane(k) for k in last)
        if layers > 1:
            dm, dq, de = (x - plane(k - 1) for x, k in zip((m, q, e), last[1:]))
        else:
            dm, dq, de = m, q, e
        relaxing = relax_rate / (1.0 + d * d)
        skew = e - 2.0 * q
        new_flux = m - cfl_nozzle * (dm + dq) + diffusion * plane_lap(m)
        new_skew = (
            skew
            - cfl_nozzle * (de - 2.0 * dq)
            - (2.0 * relax_step) * relaxing * (e - q)
            + diffusion * plane_lap(skew)
        )
        planes = jnp.concatenate([new_flux, new_skew, diffusion * m, diffusion * skew], axis=0)
        paired = planes + pltpu.roll(planes, 4 * ca - 1, 0)
        edge_rows = jnp.concatenate(
            [planes[(2 + v) * ca + a : (2 + v) * ca + a + 1] for a in (0, ca - 1) for v in range(2)]
            + [jnp.zeros((4, cb), F32)],
            axis=0,
        )
        summed = jnp.concatenate([paired[: 2 * ca], edge_rows], axis=0)
        hi = summed.astype(BF16)
        rest = summed - hi.astype(F32)
        mid, low = split_hi_lo(rest)
        count = 2 * ca + 8
        sums = jnp.dot(
            jnp.concatenate([hi, mid, low], axis=0), halve, preferred_element_type=F32
        )
        coarse = sums[:count] + sums[count : 2 * count] + sums[2 * count :]
        flux_part = coarse[:ca].astype(BF16).astype(F32)
        skew_hi, skew_lo = split_hi_lo(coarse[ca : 2 * ca])
        for k, part in enumerate((flux_part, skew_hi.astype(F32), skew_lo.astype(F32))):
            for i in range(ca // 2):
                par[k : k + 1, i * (cb // 2) : (i + 1) * (cb // 2)] = part[2 * i : 2 * i + 1]
        side_hi, side_lo = split_hi_lo(0.25 * paired[2 * ca :])
        lane = lax.broadcasted_iota(jnp.int32, (8, cb), 1)
        line = lax.broadcasted_iota(jnp.int32, (8, cb), 0)
        ends = jnp.logical_or(
            jnp.logical_and(line == 0, lane == 0), jnp.logical_and(line == 1, lane == cb - 1)
        ).astype(BF16)
        side = dot_last(ends, side_hi) + dot_last(ends, side_lo)
        edge = coarse[2 * ca :]
        side_out[0] = jnp.concatenate([side[0:1], side[1:2]], axis=1)
        side_out[1] = edge[1:2]
        side_out[2] = edge[3:4]
        blank = jnp.zeros((7, LANES), F32)
        edges = [jnp.concatenate([blank, edge[2 * x : 2 * x + 1]], axis=0) for x in range(2)]

        values = par[...].astype(BF16)
        tiled = jnp.concatenate([values] * group, axis=0)

        @pl.loop(0, owners // group)
        def _(b):
            picked = tiled * picks[pl.ds(pl.multiple_of(b * group * 8, group * 8), group * 8)]
            packed = dot_last(picked, in_slot[...]).reshape(group, 8, SLOTS)
            send_buf[pl.ds(b * group, group)] = jnp.concatenate(
                [packed[:, :, :LANES] + edges[0][None], packed[:, :, LANES:] + edges[1][None]],
                axis=1,
            ).astype(BF16)

        pl.semaphore_wait(barrier, near + owners)

        for i in range(n_slab):
            row = jnp.where(2 * s < n_slab, n_slab - 1 - i, i)
            for j in range(n_plane):
                pltpu.make_async_remote_copy(
                    src_ref=side_out,
                    dst_ref=side_in.at[me],
                    send_sem=side_send.at[row * n_plane + j],
                    recv_sem=side_recv,
                    device_id=(1, row, j),
                    device_id_type=MESH,
                ).start()
            for j in range(n_plane):
                pltpu.make_async_remote_copy(
                    src_ref=send_buf.at[row * n_plane + j],
                    dst_ref=recv_buf.at[me],
                    send_sem=row_send.at[row * n_plane + j],
                    recv_sem=row_recv,
                    device_id=(1, row, j),
                    device_id_type=MESH,
                ).start()

        extract_columns()
        start_halo((0, 1, 2, 3))
        fill_rows()
        for a in (0, ca + 1):
            tbuf[a] = jnp.zeros((sections, cb), F32)

        @pl.loop(0, ca // CHUNK)
        def _(step):
            for t in range(CHUNK):
                a = step * CHUNK + t
                c, _, lap = neighbours(a)
                back = jnp.where(jnp.bitwise_and(col_row, layers - 1) == 0, 0.0, pltpu.roll(c, 1, 0))
                du = c - back
                d, m, q, e = (c[v * layers : (v + 1) * layers] for v in range(4))
                dm, dq, de = (du[v * layers : (v + 1) * layers] for v in (1, 2, 3))
                relaxing = relax_rate / (1.0 + d * d)
                fresh = diffusion * lap + jnp.concatenate(
                    [
                        d - cfl_nozzle * dm,
                        m - cfl_nozzle * (dm + dq),
                        q + relax_step * relaxing * (e - q) - cfl_nozzle * dq,
                        e - cfl_nozzle * de,
                    ],
                    axis=0,
                )
                scatter_row(a, fresh)

        wait_halo()
        placed = diffusion * placed_columns()
        opad[...] += jnp.stack(
            [placed[:, h * LANES : (h + 1) * LANES].reshape(rows // 8, 8, LANES) for h in range(2)],
            axis=1,
        ).reshape(sections, 2 * ca, LANES)
        for side, a in enumerate((0, ca - 1)):
            for h in range(2):
                obuf[lines(a, h), :] += diffusion * edge_in[side, :, h * LANES : (h + 1) * LANES]

        @pl.loop(0, owners)
        def _(o):
            pltpu.make_async_remote_copy(
                src_ref=send_buf.at[o],
                dst_ref=recv_buf.at[me],
                send_sem=row_send.at[o],
                recv_sem=row_recv,
                device_id=(1, o // n_plane, o % n_plane),
                device_id_type=MESH,
            ).wait_send()

            pltpu.make_async_remote_copy(
                src_ref=side_out,
                dst_ref=side_in.at[me],
                send_sem=side_send.at[o],
                recv_sem=side_recv,
                device_id=(1, o // n_plane, o % n_plane),
                device_id_type=MESH,
            ).wait_send()

    @pl.when(g == 1)
    def _():
        extract_columns()
        pl.semaphore_wait(barrier, near)
        start_halo((0, 1, 2, 3))
        fill_rows()
        for copy in spray_args:
            copy.wait()
        folded = jnp.dot(coal_ref[...], fold[...], preferred_element_type=F32).astype(BF16)
        evap = jnp.zeros((sections, cb), F32)
        for k in range(sections):
            evap = jnp.where(col_row == k, evap_ref[k], evap)
        speeds = 0.2 + 0.5 * col_row.astype(F32) / (sections - 1)
        for k in range(width_ref.shape[0]):
            widths[k] = jnp.full((8, LANES), width_ref[k], F32)
        for a in (0, ca + 1):
            tbuf[a] = jnp.zeros((sections, cb), F32)

        def moved_from(c, up, lap):
            width = c.shape[1]
            lost = evap[:, :width] * c
            gained = jnp.where(
                col_row[:, :width] == sections - 1, 0.0, pltpu.roll(lost, sections - 1, 0)
            )
            return c - speeds[:, :width] * (c - up) + diffusion * lap - lost + gained

        def collide(moved):
            first = [jnp.dot(folded, pair_terms(x), preferred_element_type=F32) for x in moved]
            middle = [x + (0.5 * collide_step) * y for x, y in zip(moved, first)]
            second = [jnp.dot(folded, pair_terms(x), preferred_element_type=F32) for x in middle]
            return [x + collide_step * y for x, y in zip(moved, second)]

        @pl.loop(0, ca // CHUNK)
        def _(step):
            size = CHUNK // 2
            moved = [
                jnp.concatenate(
                    [moved_from(*neighbours(step * CHUNK + z * size + t)) for t in range(size)],
                    axis=1,
                )
                for z in range(2)
            ]
            for z, mixed in enumerate(collide(moved)):
                for t in range(size):
                    scatter_row(step * CHUNK + z * size + t, mixed[:, t * cb : (t + 1) * cb])

        wait_halo()
        for side, a in enumerate((0, ca + 1)):
            tbuf[a] = edge_in[side]
        tile_lane = lax.broadcasted_iota(jnp.int32, (8, LANES), 1)
        wide_lane = lax.broadcasted_iota(jnp.int32, (sections, LANES), 1)

        def upright(x, pair):
            folds = LANES // ca
            for k in range(folds):
                turned = [
                    pltpu.roll(pair[h], (LANES + (h - k) * ca) % LANES, 1) for h in range(2)
                ]
                upright_buf[x, pl.ds(k, sections // folds, stride=folds), :] = jnp.where(
                    tile_lane < ca, turned[0], turned[1]
                )
            return upright_buf[x]

        own = upright(0, (cols_out[0], cols_out[1]))
        inner = upright(1, (cols_near[0], cols_near[1]))
        outer = upright(2, (cols_in[0], cols_in[1]))
        above = pltpu.roll(own, 1, 1)
        below = pltpu.roll(own, LANES - 1, 1)
        parts = []
        for a in (0, ca - 1):
            c, up, lap = neighbours(a)
            lap += jnp.where(col_lane == 0, outer[:, a : a + 1], 0.0)
            lap += jnp.where(col_lane == cb - 1, outer[:, ca + a : ca + a + 1], 0.0)
            parts.append(moved_from(c, up, lap))
        parts.append(moved_from(own, above, above + below + inner + outer - 4.0 * own))
        (mixed,) = collide([jnp.concatenate(parts, axis=1)])
        columns = mixed[:, 2 * cb :]
        for a in range(1, ca - 1):
            for h, target in enumerate((0, LANES - 1)):
                at = lines(a, h)
                obuf[at, :] = jnp.where(
                    wide_lane == target,
                    pltpu.roll(columns, (LANES + target - h * ca - a) % LANES, 1),
                    obuf[at, :],
                )
        for x, a in enumerate((0, ca - 1)):
            scatter_row(a, mixed[:, x * cb : (x + 1) * cb])

        for whole, sent, got in (
            (recv_buf, row_send, row_recv),
            (side_in, side_send, side_recv),
        ):
            pltpu.make_async_remote_copy(
                src_ref=whole,
                dst_ref=whole,
                send_sem=sent.at[0],
                recv_sem=got,
                device_id=(0, s, p),
                device_id_type=MESH,
            ).wait_recv()


def finish(
    n_plane, owners, sections, ca, cb,
    held, rows_in, sides_in, widths,
    out_hbm,
    obuf, flat, par, mass, left_even, left_odd, right_even, right_odd, out_sem,
):
    plumes = widths.shape[0]
    rows = sections * ca
    g = lax.axis_index("group")
    whole = held.reshape(sections, 2 * ca + PAD, LANES).at[:, pl.ds(0, 2 * ca), :]
    out_whole = out_hbm.reshape(sections, 2 * ca, LANES)

    @pl.when(g == 0)
    def _():
        copy = pltpu.make_async_copy(whole, out_whole, out_sem.at[0])
        copy.start()
        copy.wait()

    @pl.when(g == 1)
    def _():
        half_cb = cb // 2
        pad = n_plane * LINES
        flat[pl.ds(0, pad)] = jnp.zeros((pad, LANES), F32)
        flat[pl.ds(pad + owners * LINES, pad)] = jnp.zeros((pad, LANES), F32)

        @pl.loop(0, owners // 8, unroll=2)
        def _(b):
            for o in range(8):
                at = pl.multiple_of(pad + (b * 8 + o) * LINES, 8)
                flat[pl.ds(at, 16)] = rows_in[b * 8 + o].astype(F32)
                for x in range(3):
                    flat[pl.ds(at + 16 + x, 1)] = sides_in[b * 8 + o, x]

        sub = lax.broadcasted_iota(jnp.int32, (8, LANES), 0)

        @pl.loop(0, owners // 8, unroll=2)
        def _(b):
            def take(shift, line):
                return flat[pl.ds(pad + (b * 8 + shift) * LINES + line, 8, stride=LINES), :]

            plane_at = lax.rem(b * 8 + sub, n_plane)
            above = take(-n_plane, 15), take(-n_plane, 18)
            below = take(n_plane, 7), take(n_plane, 17)
            before = jnp.where(plane_at == 0, 0.0, take(-1, 16))
            behind = jnp.where(plane_at == n_plane - 1, 0.0, take(1, 16))

            def pick(table, index):
                return jnp.take_along_axis(table, index, axis=1, mode="promise_in_bounds")

            for h in range(2):
                got = [take(0, h * 8 + x) for x in range(7)]
                place = got[6].astype(jnp.int32)
                size = jnp.abs(place)
                on_row = size <= half_cb
                spot = jnp.clip(size - 1, 0, half_cb - 1)
                line = jnp.clip(size - half_cb - 1, 0, ca // 2 - 1)
                line = jnp.where(on_row, jnp.where(place < 0, ca // 2 - 1, 0), line)
                inside = size == half_cb + ca
                in_column = jnp.logical_not(jnp.logical_or(on_row, inside))
                first_row = jnp.logical_and(on_row, place > 0)
                last_row = jnp.logical_and(on_row, place < 0)
                first_column = jnp.logical_or(size == 1, jnp.logical_and(in_column, place > 0))
                last_column = jnp.logical_or(
                    size == half_cb, jnp.logical_and(in_column, place < 0)
                )
                flux = got[0]
                skew = got[1] + got[2]
                for tables, here in ((above, first_row), (below, last_row)):
                    flux += jnp.where(here, pick(tables[0], spot), 0.0)
                    skew += jnp.where(here, pick(tables[1], spot), 0.0)
                for table, base, here in (
                    (before, 2 * ca, first_column),
                    (behind, 0, last_column),
                ):
                    flux += jnp.where(here, pick(table, 2 * line + base), 0.0)
                    skew += jnp.where(here, pick(table, 2 * line + base + ca), 0.0)
                spread = widths[0]
                for k in range(1, plumes):
                    spread = jnp.where(got[3] == float(k), widths[k], spread)
                values = (
                    jnp.where(place != 0, jnp.sqrt(1.0 + flux * flux), 0.0),
                    (sections - 1) * jax.nn.sigmoid(skew),
                    1.0 / spread,
                    got[4],
                    got[5],
                )
                for x, value in enumerate(values):
                    par[x, pl.ds(pl.multiple_of(b * 8, 8), 8), h * LANES : (h + 1) * LANES] = value

        span = SOURCES * SLOTS
        level = lax.broadcasted_iota(jnp.int32, (sections, span), 0).astype(F32)
        index_a = lax.broadcasted_iota(jnp.int32, (ca, span), 0).astype(F32).astype(BF16)
        index_b = lax.broadcasted_iota(jnp.int32, (cb, span), 0).astype(F32).astype(BF16)

        def build(step, left, right):
            strength, center, inverse, along, across = (
                jnp.concatenate(
                    [par[x, pl.ds(step * SOURCES + t, 1), :] for t in range(SOURCES)], axis=1
                )
                for x in range(5)
            )
            scaled = (level - center) * inverse
            weights = 1.0 / (1.0 + scaled * scaled)
            mass[...] = weights * (strength / jnp.sum(weights, axis=0, keepdims=True))
            mask = jnp.where(along.astype(BF16) == index_a, jnp.ones((),BF16), jnp.zeros((),BF16))
            right[...] = jnp.where(across.astype(BF16) == index_b, jnp.ones((),BF16), jnp.zeros((),BF16))
            for k in range(sections):
                left[k * ca : (k + 1) * ca] = (
                    jnp.broadcast_to(mass[k : k + 1], (ca, span)).astype(BF16) * mask
                )

        def add(left, right, first, count, base):
            added = dot_last(left[first * ca : (first + count) * ca], right[...])
            tiles = jnp.stack(
                [
                    added[:, h * LANES : (h + 1) * LANES].reshape(count * ca // 8, 8, LANES)
                    for h in range(2)
                ],
                axis=1,
            )
            obuf[first : first + count] = base[first : first + count] + tiles.reshape(
                count, 2 * ca, LANES
            )

        build(0, left_even, right_even)
        steps = owners // SOURCES

        add(left_even, right_even, 0, sections, whole)
        build(1, left_odd, right_odd)

        @pl.loop(1, steps // 2)
        def _(i):
            add(left_odd, right_odd, 0, sections, obuf)
            build(2 * i, left_even, right_even)
            add(left_even, right_even, 0, sections, obuf)
            build(2 * i + 1, left_odd, right_odd)

        each = sections // PIECES
        stores = []
        for c in range(PIECES):
            add(left_odd, right_odd, c * each, each, obuf)
            at = pl.ds(c * each, each)
            stores.append(
                pltpu.make_async_copy(obuf.at[at], out_whole.at[at], out_sem.at[c])
            )
            stores[-1].start()
        for store in stores:
            store.wait()


def body(n_slab, n_plane, fields, evap_rates, coal_kernel, plume_width, owner_map, deposit_cell, plume_ids):
    _, sections, ca, cb = fields.shape
    exit_rows = owner_map.shape[1]
    owners = n_slab * n_plane
    rows = sections * ca
    fold = jnp.asarray(fold_matrix(sections), BF16)
    kept = fold.shape[1]
    hbm = pl.BlockSpec(memory_space=pl.ANY)
    vmem = pl.BlockSpec(memory_space=pltpu.VMEM)
    held, rows_in, sides_in, widths = pl.pallas_call(
        functools.partial(kernel, n_slab, n_plane, sections, ca, cb, exit_rows),
        out_shape=[
            pltpu.VMEM((2 * rows + sections * PAD, LANES), F32),
            pltpu.VMEM((owners, 16, LANES), BF16),
            pltpu.VMEM((owners, 3, 1, LANES), F32),
            pltpu.VMEM(plume_width.shape + (8, LANES), F32),
        ],
        in_specs=[hbm] * 8,
        out_specs=[vmem] * 4,
        scratch_shapes=[
            pltpu.VMEM((2 * rows + sections * PAD, LANES), F32),
            pltpu.VMEM((ca + 2, sections, cb), F32),
            pltpu.VMEM((2, sections, cb), F32),
            pltpu.VMEM((3, sections, LANES), F32),
            pltpu.VMEM((sections * sections, kept), BF16),
            pltpu.VMEM((2, rows // LANES, LANES), F32),
            pltpu.VMEM((2, rows // LANES, LANES), F32),
            pltpu.VMEM((2, rows // LANES, LANES), F32),
            pltpu.VMEM((8, exit_rows), F32),
            pltpu.VMEM((owners, 16, LANES), BF16),
            pltpu.SMEM(evap_rates.shape, F32),
            pltpu.VMEM(coal_kernel.shape, BF16),
            pltpu.SMEM(plume_width.shape, F32),
            pltpu.VMEM((1, exit_rows), jnp.int32),
            pltpu.VMEM((1, exit_rows), jnp.int32),
            pltpu.VMEM((1, exit_rows), jnp.int32),
            pltpu.VMEM((owners * 8, exit_rows), BF16),
            pltpu.VMEM((SLOTS, exit_rows), BF16),
            pltpu.SemaphoreType.DMA,
            pltpu.SemaphoreType.DMA((4,)),
            pltpu.SemaphoreType.DMA((4,)),
            pltpu.SemaphoreType.DMA((4,)),
            pltpu.SemaphoreType.DMA((owners,)),
            pltpu.SemaphoreType.DMA,
            pltpu.VMEM((3, 1, LANES), F32),
            pltpu.SemaphoreType.DMA((owners,)),
            pltpu.SemaphoreType.DMA,
        ],
        compiler_params=pltpu.CompilerParams(
            collective_id=0, has_side_effects=True, vmem_limit_bytes=VMEM_BYTES
        ),
    )(
        fields.reshape(rows // 8, 8, 2, LANES).transpose(0, 2, 1, 3).reshape(2 * rows, LANES), evap_rates, coal_kernel, fold, plume_width,
        owner_map, deposit_cell, plume_ids,
    )
    span = SOURCES * SLOTS
    out = pl.pallas_call(
        functools.partial(finish, n_plane, owners, sections, ca, cb),
        out_shape=jax.ShapeDtypeStruct((2 * rows, LANES), F32),
        in_specs=[vmem] * 4,
        out_specs=hbm,
        scratch_shapes=[
            pltpu.VMEM((sections, 2 * ca, LANES), F32),
            pltpu.VMEM(((owners + 2 * n_plane) * LINES, LANES), F32),
            pltpu.VMEM((5, owners, SLOTS), F32),
            pltpu.VMEM((sections, span), F32),
            pltpu.VMEM((rows, span), BF16),
            pltpu.VMEM((rows, span), BF16),
            pltpu.VMEM((cb, span), BF16),
            pltpu.VMEM((cb, span), BF16),
            pltpu.SemaphoreType.DMA((PIECES,)),
        ],
        compiler_params=pltpu.CompilerParams(vmem_limit_bytes=VMEM_BYTES),
    )(
        pltpu.with_memory_space_constraint(held, pltpu.VMEM),
        pltpu.with_memory_space_constraint(rows_in, pltpu.VMEM),
        pltpu.with_memory_space_constraint(sides_in, pltpu.VMEM),
        pltpu.with_memory_space_constraint(widths, pltpu.VMEM),
    )
    out = out.reshape(rows // 8, 2, 8, LANES).transpose(0, 2, 1, 3)
    return out.reshape(1, sections, ca, cb)


def solution(mesh):
    return jax.shard_map(
        functools.partial(body, mesh.shape["slab"], mesh.shape["plane"]),
        mesh=mesh,
        in_specs=(
            P("group", None, "slab", "plane"),
            P(),
            P(),
            P(),
            P(("slab", "plane"), None),
            P(("slab", "plane"), None),
            P(("slab", "plane"), None),
        ),
        out_specs=P("group", None, "slab", "plane"),
        check_vma=False,
    )
```

```python
import functools

import jax
import jax.numpy as jnp
import numpy as np
from jax import lax
from jax.experimental import pallas as pl
from jax.experimental.pallas import tpu as pltpu
from jax.sharding import PartitionSpec as P

MESH = pl.DeviceIdType.MESH
F32 = jnp.float32
BF16 = jnp.bfloat16
LANES = 128
SLOTS = 256
CHUNK = 8
PAD = 8
LINES = 24
SOURCES = 4
PIECES = (3, 1)
VMEM_BYTES = 56 * 1024 * 1024

cfl_nozzle = 0.35
diffusion = 0.2
relax_rate = 5.0
relax_step = 0.1
collide_step = 0.25


def fold_matrix(sections):
    kept = [(i, j) for i in range(sections) for j in range(i // 8 * 8, sections)]
    fold = np.zeros((sections * sections, len(kept)), np.float32)
    for q, (i, j) in enumerate(kept):
        fold[i * sections + j, q] = 1.0
        if j // 8 > i // 8:
            fold[j * sections + i, q] = 1.0
    return fold


def pair_terms(m):
    sections, width = m.shape
    pieces = []
    for i in range(sections):
        low = i // 8 * 8
        pieces.append(jnp.broadcast_to(m[i : i + 1], (sections - low, width)) * m[low:])
    return jnp.concatenate(pieces, axis=0).astype(BF16)


def split_hi_lo(x):
    hi = x.astype(BF16)
    lo = (x - hi.astype(F32)).astype(BF16)
    return hi, lo


def dot_last(a, b):
    return lax.dot_general(a, b, (((1,), (1,)), ((), ())), preferred_element_type=F32)


def kernel(
    n_slab, n_plane, sections, ca, cb, exit_rows,
    fields_hbm, evap_hbm, coal_hbm, fold_hbm, width_hbm, owner_hbm, cell_hbm, pid_hbm,
    obuf, recv_buf, side_in, widths,
    fbuf, tbuf, edge_out, edge_in, upright_buf, fold, cols_out, cols_near, cols_in, par, send_buf,
    evap_ref, coal_ref, width_ref, owner_ref, cell_ref, pid_ref, picks, in_slot,
    in_sem, arg_sem, halo_send, halo_recv, row_send, row_recv, side_out, side_send, side_recv,
):
    owners = n_slab * n_plane
    rows = sections * ca
    g = lax.axis_index("group")
    s = lax.axis_index("slab")
    p = lax.axis_index("plane")
    me = s * n_plane + p
    barrier = pltpu.get_barrier_semaphore()

    @pl.when(g == 1)
    def _():
        for i in range(n_slab):
            row = jnp.where(2 * s < n_slab, n_slab - 1 - i, i)
            for j in range(n_plane):
                pl.semaphore_signal(barrier, inc=1, device_id=(0, row, j), device_id_type=MESH)


    fpad = fbuf.reshape(sections, 2 * ca + PAD, LANES).at[:, pl.ds(0, 2 * ca), :]
    opad = obuf.reshape(sections, 2 * ca + PAD, LANES).at[:, pl.ds(0, 2 * ca), :]
    load = pltpu.make_async_copy(
        fields_hbm.reshape(sections, 2 * ca, LANES), fpad, in_sem
    )
    load.start()
    nozzle_args = [
        pltpu.make_async_copy(source, target, arg_sem.at[k])
        for k, (source, target) in enumerate(
            ((owner_hbm, owner_ref), (cell_hbm, cell_ref), (pid_hbm, pid_ref))
        )
    ]
    spray_args = [
        pltpu.make_async_copy(source, target, arg_sem.at[k])
        for k, (source, target) in enumerate(
            ((evap_hbm, evap_ref), (coal_hbm, coal_ref), (fold_hbm, fold), (width_hbm, width_ref))
        )
    ]

    @pl.when(g == 0)
    def _():
        for copy in nozzle_args:
            copy.start()

    @pl.when(g == 1)
    def _():
        for copy in spray_args:
            copy.start()

    sides = [
        (s > 0, (g, s - 1, p)),
        (s < n_slab - 1, (g, s + 1, p)),
        (p > 0, (g, s, p - 1)),
        (p < n_plane - 1, (g, s, p + 1)),
    ]
    near = 0
    for there, target in sides:
        near = near + there.astype(jnp.int32)

        @pl.when(there)
        def _():
            pl.semaphore_signal(barrier, inc=1, device_id=target, device_id_type=MESH)

    load.wait()

    def lines(a, h):
        return pl.ds(a // 8 * 16 + h * 8 + a % 8, sections, stride=2 * ca + PAD)

    def gather_row(ref, a):
        return jnp.concatenate([ref[lines(a, h), :] for h in range(2)], axis=1)

    def half(ref, h):
        return ref[...].reshape(rows // 8, 2, 8, LANES)[:, h].reshape(rows, LANES)

    def halo(kind, target):
        source, landing = (
            (edge_out.at[1], edge_in.at[0]),
            (edge_out.at[0], edge_in.at[1]),
            (cols_out.at[1], cols_in.at[0]),
            (cols_out.at[0], cols_in.at[1]),
        )[kind]
        return pltpu.make_async_remote_copy(
            src_ref=source,
            dst_ref=landing,
            send_sem=halo_send.at[kind],
            recv_sem=halo_recv.at[kind],
            device_id=target,
            device_id_type=MESH,
        )

    outgoing = (sides[1], sides[0], sides[3], sides[2])
    def start_halo(kinds):
        for kind in kinds:

            @pl.when(outgoing[kind][0])
            def _():
                halo(kind, outgoing[kind][1]).start()

    def extract_columns():
        for x, a in enumerate((0, ca - 1)):
            edge = gather_row(fbuf, a)
            tbuf[a + 1] = edge
            edge_out[x] = edge.astype(BF16)

        lane = lax.broadcasted_iota(jnp.int32, (8, LANES), 1)
        line = lax.broadcasted_iota(jnp.int32, (8, LANES), 0)
        for h, (outer, inner) in enumerate(((0, 1), (LANES - 1, LANES - 2))):
            select = jnp.logical_or(
                jnp.logical_and(line == 0, lane == outer), jnp.logical_and(line == 1, lane == inner)
            ).astype(BF16)
            columns = dot_last(select, half(fpad, h).astype(BF16))
            for x in range(rows // LANES):
                at = slice(x * LANES, (x + 1) * LANES)
                cols_out[h, x : x + 1] = columns[0:1, at]
                cols_near[h, x : x + 1] = columns[1:2, at]

    def fill_rows():
        @pl.loop(1, ca - 1)
        def _(a):
            tbuf[a + 1] = gather_row(fbuf, a)

        for kind, landing in enumerate((edge_in.at[0], edge_in.at[1], cols_in.at[0], cols_in.at[1])):

            @pl.when(jnp.logical_not(sides[kind][0]))
            def _():
                landing[...] = jnp.zeros(landing.shape, landing.dtype)

    def wait_halo():
        for kind in range(4):

            @pl.when(outgoing[kind][0])
            def _():
                halo(kind, outgoing[kind][1]).wait_send()

            @pl.when(sides[kind][0])
            def _():
                halo(kind, outgoing[kind][1]).wait_recv()

    def placed_columns():
        sub = lax.broadcasted_iota(jnp.int32, (16, cb), 0)
        lanes = lax.broadcasted_iota(jnp.int32, (16, cb), 1)
        lined = [
            jnp.concatenate([cols_in[h, x : x + 1] for x in range(rows // LANES)], axis=1)
            for h in range(2)
        ]
        stack = jnp.concatenate(lined + [jnp.zeros((14, rows), F32)], axis=0)
        place = jnp.logical_or(
            jnp.logical_and(sub == 0, lanes == 0), jnp.logical_and(sub == 1, lanes == cb - 1)
        ).astype(BF16)
        return jnp.dot(stack.T.astype(BF16), place, preferred_element_type=F32)

    col_lane = lax.broadcasted_iota(jnp.int32, (sections, cb), 1)
    col_row = lax.broadcasted_iota(jnp.int32, (sections, cb), 0)

    def neighbours(a):
        c = tbuf[a + 1]
        up = tbuf[a]
        left = jnp.where(col_lane == 0, 0.0, pltpu.roll(c, 1, 1))
        right = jnp.where(col_lane == cb - 1, 0.0, pltpu.roll(c, cb - 1, 1))
        lap = up + tbuf[a + 2] + (left + right) - 4.0 * c
        return c, up, lap

    def scatter_row(a, value):
        for h in range(2):
            obuf[lines(a, h), :] = value[:, h * LANES : (h + 1) * LANES]

    @pl.when(g == 0)
    def _():
        for copy in nozzle_args:
            copy.wait()
        owner = owner_ref[...]
        slots = []
        below = lax.broadcasted_iota(jnp.int32, (256, 256), 0)
        after = lax.broadcasted_iota(jnp.int32, (256, 256), 1)
        upto = (below <= after).astype(BF16)
        names = lax.broadcasted_iota(jnp.int32, (owners, 256), 0)
        carry = jnp.zeros((owners, 1), F32)
        for j in range(exit_rows // 256):
            hit = (owner[:, j * 256 : (j + 1) * 256] == names).astype(F32)
            count = jnp.dot(hit.astype(BF16), upto, preferred_element_type=F32) + carry
            slots.append(jnp.sum(hit * (count - 1.0), axis=0, keepdims=True))
            carry = count[:, 255:256]
        slot = jnp.concatenate(slots, axis=1)
        cell = cell_ref[...]
        across = jnp.bitwise_and(cell, cb - 1)
        along = jnp.right_shift(cell, cb.bit_length() - 1)
        par[3:4] = pid_ref[...].astype(F32)
        par[4:5] = along.astype(F32)
        par[5:6] = across.astype(F32)
        half_cb = cb // 2
        last_line = ca // 2 - 1
        number = lax.broadcasted_iota(jnp.int32, (1, exit_rows), 1)
        spot = jnp.bitwise_and(number, half_cb - 1)
        line = jnp.right_shift(number, half_cb.bit_length() - 1)
        beside = half_cb + 1 + line
        place = jnp.where(spot == half_cb - 1, -beside, half_cb + ca)
        place = jnp.where(spot == 0, beside, place)
        place = jnp.where(line == last_line, -1 - spot, place)
        par[6:7] = jnp.where(line == 0, 1 + spot, place).astype(F32)
        par[7:8] = jnp.zeros((1, exit_rows), F32)
        places = lax.broadcasted_iota(jnp.int32, (SLOTS, exit_rows), 0).astype(F32)
        in_slot[...] = (slot == places).astype(BF16)
        group = 16
        label = jnp.right_shift(lax.broadcasted_iota(jnp.int32, (group * 8, exit_rows), 0), 3)

        @pl.loop(0, owners // group)
        def _(b):
            picks[pl.ds(pl.multiple_of(b * group * 8, group * 8), group * 8)] = (
                owner == label + b * group
            ).astype(BF16)

        halve = jnp.where(
            jnp.right_shift(lax.broadcasted_iota(jnp.int32, (cb, cb // 2), 0), 1)
            == lax.broadcasted_iota(jnp.int32, (cb, cb // 2), 1),
            0.25,
            0.0,
        ).astype(BF16)

        layers = sections // 4
        plane_row = lax.broadcasted_iota(jnp.int32, (ca, cb), 0)
        plane_lane = lax.broadcasted_iota(jnp.int32, (ca, cb), 1)

        def plane(k):
            tiles = fbuf[pl.ds(k * (2 * ca + PAD), 2 * ca), :].reshape(ca // 8, 2, 8, LANES)
            return jnp.concatenate([tiles[:, h].reshape(ca, LANES) for h in range(2)], axis=1)

        def plane_lap(c):
            up = jnp.where(plane_row == 0, 0.0, pltpu.roll(c, 1, 0))
            down = jnp.where(plane_row == ca - 1, 0.0, pltpu.roll(c, ca - 1, 0))
            left = jnp.where(plane_lane == 0, 0.0, pltpu.roll(c, 1, 1))
            right = jnp.where(plane_lane == cb - 1, 0.0, pltpu.roll(c, cb - 1, 1))
            return up + down + (left + right) - 4.0 * c

        last = [v * layers + layers - 1 for v in range(4)]
        d, m, q, e = (plane(k) for k in last)
        if layers > 1:
            dm, dq, de = (x - plane(k - 1) for x, k in zip((m, q, e), last[1:]))
        else:
            dm, dq, de = m, q, e
        relaxing = relax_rate / (1.0 + d * d)
        skew = e - 2.0 * q
        new_flux = m - cfl_nozzle * (dm + dq) + diffusion * plane_lap(m)
        new_skew = (
            skew
            - cfl_nozzle * (de - 2.0 * dq)
            - (2.0 * relax_step) * relaxing * (e - q)
            + diffusion * plane_lap(skew)
        )
        planes = jnp.concatenate([new_flux, new_skew, diffusion * m, diffusion * skew], axis=0)
        paired = planes + pltpu.roll(planes, 4 * ca - 1, 0)
        edge_rows = jnp.concatenate(
            [planes[(2 + v) * ca + a : (2 + v) * ca + a + 1] for a in (0, ca - 1) for v in range(2)]
            + [jnp.zeros((4, cb), F32)],
            axis=0,
        )
        summed = jnp.concatenate([paired[: 2 * ca], edge_rows], axis=0)
        hi = summed.astype(BF16)
        rest = summed - hi.astype(F32)
        mid, low = split_hi_lo(rest)
        count = 2 * ca + 8
        sums = jnp.dot(
            jnp.concatenate([hi, mid, low], axis=0), halve, preferred_element_type=F32
        )
        coarse = sums[:count] + sums[count : 2 * count] + sums[2 * count :]
        flux_part = coarse[:ca].astype(BF16).astype(F32)
        skew_hi, skew_lo = split_hi_lo(coarse[ca : 2 * ca])
        for k, part in enumerate((flux_part, skew_hi.astype(F32), skew_lo.astype(F32))):
            for i in range(ca // 2):
                par[k : k + 1, i * (cb // 2) : (i + 1) * (cb // 2)] = part[2 * i : 2 * i + 1]
        side_hi, side_lo = split_hi_lo(0.25 * paired[2 * ca :])
        lane = lax.broadcasted_iota(jnp.int32, (8, cb), 1)
        line = lax.broadcasted_iota(jnp.int32, (8, cb), 0)
        ends = jnp.logical_or(
            jnp.logical_and(line == 0, lane == 0), jnp.logical_and(line == 1, lane == cb - 1)
        ).astype(BF16)
        side = dot_last(ends, side_hi) + dot_last(ends, side_lo)
        edge = coarse[2 * ca :]
        side_out[0] = jnp.concatenate([side[0:1], side[1:2]], axis=1)
        side_out[1] = edge[1:2]
        side_out[2] = edge[3:4]
        blank = jnp.zeros((7, LANES), F32)
        edges = [jnp.concatenate([blank, edge[2 * x : 2 * x + 1]], axis=0) for x in range(2)]

        values = par[...].astype(BF16)
        tiled = jnp.concatenate([values] * group, axis=0)

        @pl.loop(0, owners // group)
        def _(b):
            picked = tiled * picks[pl.ds(pl.multiple_of(b * group * 8, group * 8), group * 8)]
            packed = dot_last(picked, in_slot[...]).reshape(group, 8, SLOTS)
            send_buf[pl.ds(b * group, group)] = jnp.concatenate(
                [packed[:, :, :LANES] + edges[0][None], packed[:, :, LANES:] + edges[1][None]],
                axis=1,
            ).astype(BF16)

        pl.semaphore_wait(barrier, near + owners)

        for i in range(n_slab):
            row = i
            for j in range(n_plane):
                pltpu.make_async_remote_copy(
                    src_ref=side_out,
                    dst_ref=side_in.at[me],
                    send_sem=side_send.at[row * n_plane + j],
                    recv_sem=side_recv,
                    device_id=(1, row, j),
                    device_id_type=MESH,
                ).start()
            for j in range(n_plane):
                pltpu.make_async_remote_copy(
                    src_ref=send_buf.at[row * n_plane + j],
                    dst_ref=recv_buf.at[me],
                    send_sem=row_send.at[row * n_plane + j],
                    recv_sem=row_recv,
                    device_id=(1, row, j),
                    device_id_type=MESH,
                ).start()

        extract_columns()
        start_halo((0, 1, 2, 3))
        fill_rows()
        for a in (0, ca + 1):
            tbuf[a] = jnp.zeros((sections, cb), F32)

        @pl.loop(0, ca // CHUNK)
        def _(step):
            for t in range(CHUNK):
                a = step * CHUNK + t
                c, _, lap = neighbours(a)
                back = jnp.where(jnp.bitwise_and(col_row, layers - 1) == 0, 0.0, pltpu.roll(c, 1, 0))
                du = c - back
                d, m, q, e = (c[v * layers : (v + 1) * layers] for v in range(4))
                dm, dq, de = (du[v * layers : (v + 1) * layers] for v in (1, 2, 3))
                relaxing = relax_rate / (1.0 + d * d)
                fresh = diffusion * lap + jnp.concatenate(
                    [
                        d - cfl_nozzle * dm,
                        m - cfl_nozzle * (dm + dq),
                        q + relax_step * relaxing * (e - q) - cfl_nozzle * dq,
                        e - cfl_nozzle * de,
                    ],
                    axis=0,
                )
                scatter_row(a, fresh)

        wait_halo()
        placed = diffusion * placed_columns()
        opad[...] += jnp.stack(
            [placed[:, h * LANES : (h + 1) * LANES].reshape(rows // 8, 8, LANES) for h in range(2)],
            axis=1,
        ).reshape(sections, 2 * ca, LANES)
        for side, a in enumerate((0, ca - 1)):
            edge = diffusion * edge_in[side].astype(F32)
            for h in range(2):
                obuf[lines(a, h), :] += edge[:, h * LANES : (h + 1) * LANES]

        @pl.loop(0, owners)
        def _(o):
            pltpu.make_async_remote_copy(
                src_ref=send_buf.at[o],
                dst_ref=recv_buf.at[me],
                send_sem=row_send.at[o],
                recv_sem=row_recv,
                device_id=(1, o // n_plane, o % n_plane),
                device_id_type=MESH,
            ).wait_send()

            pltpu.make_async_remote_copy(
                src_ref=side_out,
                dst_ref=side_in.at[me],
                send_sem=side_send.at[o],
                recv_sem=side_recv,
                device_id=(1, o // n_plane, o % n_plane),
                device_id_type=MESH,
            ).wait_send()

    @pl.when(g == 1)
    def _():
        extract_columns()
        pl.semaphore_wait(barrier, near)
        start_halo((0, 1, 2, 3))
        fill_rows()
        for copy in spray_args:
            copy.wait()
        folded = jnp.dot(coal_ref[...], fold[...], preferred_element_type=F32).astype(BF16)
        evap = jnp.zeros((sections, cb), F32)
        for k in range(sections):
            evap = jnp.where(col_row == k, evap_ref[k], evap)
        speeds = 0.2 + 0.5 * col_row.astype(F32) / (sections - 1)
        for k in range(width_ref.shape[0]):
            widths[k] = jnp.full((8, LANES), width_ref[k], F32)
        for a in (0, ca + 1):
            tbuf[a] = jnp.zeros((sections, cb), F32)

        def moved_from(c, up, lap):
            width = c.shape[1]
            lost = evap[:, :width] * c
            gained = jnp.where(
                col_row[:, :width] == sections - 1, 0.0, pltpu.roll(lost, sections - 1, 0)
            )
            return c - speeds[:, :width] * (c - up) + diffusion * lap - lost + gained

        def collide(moved):
            first = [jnp.dot(folded, pair_terms(x), preferred_element_type=F32) for x in moved]
            middle = [x + (0.5 * collide_step) * y for x, y in zip(moved, first)]
            second = [jnp.dot(folded, pair_terms(x), preferred_element_type=F32) for x in middle]
            return [x + collide_step * y for x, y in zip(moved, second)]

        @pl.loop(0, ca // CHUNK)
        def _(step):
            size = CHUNK // 2
            moved = [
                jnp.concatenate(
                    [moved_from(*neighbours(step * CHUNK + z * size + t)) for t in range(size)],
                    axis=1,
                )
                for z in range(2)
            ]
            for z, mixed in enumerate(collide(moved)):
                for t in range(size):
                    scatter_row(step * CHUNK + z * size + t, mixed[:, t * cb : (t + 1) * cb])

        wait_halo()
        for side, a in enumerate((0, ca + 1)):
            tbuf[a] = edge_in[side].astype(F32)
        tile_lane = lax.broadcasted_iota(jnp.int32, (8, LANES), 1)
        wide_lane = lax.broadcasted_iota(jnp.int32, (sections, LANES), 1)

        def upright(x, pair):
            folds = LANES // ca
            for k in range(folds):
                turned = [
                    pltpu.roll(pair[h], (LANES + (h - k) * ca) % LANES, 1) for h in range(2)
                ]
                upright_buf[x, pl.ds(k, sections // folds, stride=folds), :] = jnp.where(
                    tile_lane < ca, turned[0], turned[1]
                )
            return upright_buf[x]

        own = upright(0, (cols_out[0], cols_out[1]))
        inner = upright(1, (cols_near[0], cols_near[1]))
        outer = upright(2, (cols_in[0], cols_in[1]))
        above = pltpu.roll(own, 1, 1)
        below = pltpu.roll(own, LANES - 1, 1)
        parts = []
        for a in (0, ca - 1):
            c, up, lap = neighbours(a)
            lap += jnp.where(col_lane == 0, outer[:, a : a + 1], 0.0)
            lap += jnp.where(col_lane == cb - 1, outer[:, ca + a : ca + a + 1], 0.0)
            parts.append(moved_from(c, up, lap))
        parts.append(moved_from(own, above, above + below + inner + outer - 4.0 * own))
        (mixed,) = collide([jnp.concatenate(parts, axis=1)])
        columns = mixed[:, 2 * cb :]
        for a in range(1, ca - 1):
            for h, target in enumerate((0, LANES - 1)):
                at = lines(a, h)
                obuf[at, :] = jnp.where(
                    wide_lane == target,
                    pltpu.roll(columns, (LANES + target - h * ca - a) % LANES, 1),
                    obuf[at, :],
                )
        for x, a in enumerate((0, ca - 1)):
            scatter_row(a, mixed[:, x * cb : (x + 1) * cb])

        for whole, sent, got in (
            (recv_buf, row_send, row_recv),
            (side_in, side_send, side_recv),
        ):
            pltpu.make_async_remote_copy(
                src_ref=whole,
                dst_ref=whole,
                send_sem=sent.at[0],
                recv_sem=got,
                device_id=(0, s, p),
                device_id_type=MESH,
            ).wait_recv()


def finish(
    n_plane, owners, sections, ca, cb,
    held, rows_in, sides_in, widths,
    out_hbm,
    obuf, flat, par, mass, left_even, left_odd, right_even, right_odd, out_sem,
):
    plumes = widths.shape[0]
    rows = sections * ca
    g = lax.axis_index("group")
    whole = held.reshape(sections, 2 * ca + PAD, LANES).at[:, pl.ds(0, 2 * ca), :]
    out_whole = out_hbm.reshape(sections, 2 * ca, LANES)

    @pl.when(g == 0)
    def _():
        copy = pltpu.make_async_copy(whole, out_whole, out_sem.at[0])
        copy.start()
        copy.wait()

    @pl.when(g == 1)
    def _():
        half_cb = cb // 2
        pad = n_plane * LINES
        flat[pl.ds(0, pad)] = jnp.zeros((pad, LANES), F32)
        flat[pl.ds(pad + owners * LINES, pad)] = jnp.zeros((pad, LANES), F32)

        @pl.loop(0, owners // 8, unroll=2)
        def _(b):
            for o in range(8):
                at = pl.multiple_of(pad + (b * 8 + o) * LINES, 8)
                flat[pl.ds(at, 16)] = rows_in[b * 8 + o].astype(F32)
                for x in range(3):
                    flat[pl.ds(at + 16 + x, 1)] = sides_in[b * 8 + o, x]

        sub = lax.broadcasted_iota(jnp.int32, (8, LANES), 0)

        @pl.loop(0, owners // 8, unroll=2)
        def _(b):
            def take(shift, line):
                return flat[pl.ds(pad + (b * 8 + shift) * LINES + line, 8, stride=LINES), :]

            plane_at = lax.rem(b * 8 + sub, n_plane)
            above = take(-n_plane, 15), take(-n_plane, 18)
            below = take(n_plane, 7), take(n_plane, 17)
            before = jnp.where(plane_at == 0, 0.0, take(-1, 16))
            behind = jnp.where(plane_at == n_plane - 1, 0.0, take(1, 16))

            def pick(table, index):
                return jnp.take_along_axis(table, index, axis=1, mode="promise_in_bounds")

            for h in range(2):
                got = [take(0, h * 8 + x) for x in range(7)]
                place = got[6].astype(jnp.int32)
                size = jnp.abs(place)
                on_row = size <= half_cb
                spot = jnp.clip(size - 1, 0, half_cb - 1)
                line = jnp.clip(size - half_cb - 1, 0, ca // 2 - 1)
                line = jnp.where(on_row, jnp.where(place < 0, ca // 2 - 1, 0), line)
                inside = size == half_cb + ca
                in_column = jnp.logical_not(jnp.logical_or(on_row, inside))
                first_row = jnp.logical_and(on_row, place > 0)
                last_row = jnp.logical_and(on_row, place < 0)
                first_column = jnp.logical_or(size == 1, jnp.logical_and(in_column, place > 0))
                last_column = jnp.logical_or(
                    size == half_cb, jnp.logical_and(in_column, place < 0)
                )
                flux = got[0]
                skew = got[1] + got[2]
                for tables, here in ((above, first_row), (below, last_row)):
                    flux += jnp.where(here, pick(tables[0], spot), 0.0)
                    skew += jnp.where(here, pick(tables[1], spot), 0.0)
                for table, base, here in (
                    (before, 2 * ca, first_column),
                    (behind, 0, last_column),
                ):
                    flux += jnp.where(here, pick(table, 2 * line + base), 0.0)
                    skew += jnp.where(here, pick(table, 2 * line + base + ca), 0.0)
                spread = widths[0]
                for k in range(1, plumes):
                    spread = jnp.where(got[3] == float(k), widths[k], spread)
                values = (
                    jnp.where(place != 0, jnp.sqrt(1.0 + flux * flux), 0.0),
                    (sections - 1) * jax.nn.sigmoid(skew),
                    1.0 / spread,
                    got[4],
                    got[5],
                )
                for x, value in enumerate(values):
                    par[x, pl.ds(pl.multiple_of(b * 8, 8), 8), h * LANES : (h + 1) * LANES] = value

        span = SOURCES * SLOTS
        level = lax.broadcasted_iota(jnp.int32, (sections, span), 0).astype(F32)
        index_a = lax.broadcasted_iota(jnp.int32, (ca, span), 0).astype(F32).astype(BF16)
        index_b = lax.broadcasted_iota(jnp.int32, (cb, span), 0).astype(F32).astype(BF16)

        def build(step, left, right):
            strength, center, inverse, along, across = (
                jnp.concatenate(
                    [par[x, pl.ds(step * SOURCES + t, 1), :] for t in range(SOURCES)], axis=1
                )
                for x in range(5)
            )
            scaled = (level - center) * inverse
            weights = 1.0 / (1.0 + scaled * scaled)
            mass[...] = weights * (strength / jnp.sum(weights, axis=0, keepdims=True))
            mask = jnp.where(along.astype(BF16) == index_a, jnp.ones((),BF16), jnp.zeros((),BF16))
            right[...] = jnp.where(across.astype(BF16) == index_b, jnp.ones((),BF16), jnp.zeros((),BF16))
            for k in range(sections):
                left[k * ca : (k + 1) * ca] = (
                    jnp.broadcast_to(mass[k : k + 1], (ca, span)).astype(BF16) * mask
                )

        def add(pairs, first, count, base):
            added = sum(
                dot_last(left[first * ca : (first + count) * ca], right[...])
                for left, right in pairs
            )
            tiles = jnp.stack(
                [
                    added[:, h * LANES : (h + 1) * LANES].reshape(count * ca // 8, 8, LANES)
                    for h in range(2)
                ],
                axis=1,
            )
            obuf[first : first + count] = base[first : first + count] + tiles.reshape(
                count, 2 * ca, LANES
            )

        even = left_even, right_even
        odd = left_odd, right_odd
        steps = owners // SOURCES
        build(0, *even)
        add([even], 0, sections, whole)
        build(1, *odd)

        @pl.loop(1, steps // 2 - 1)
        def _(i):
            add([odd], 0, sections, obuf)
            build(2 * i, *even)
            add([even], 0, sections, obuf)
            build(2 * i + 1, *odd)

        add([odd], 0, sections, obuf)
        build(steps - 2, *even)
        build(steps - 1, *odd)
        stores = []
        first = 0
        for c, part in enumerate(PIECES):
            count = part * sections // sum(PIECES)
            add([even, odd], first, count, obuf)
            at = pl.ds(first, count)
            first += count
            stores.append(
                pltpu.make_async_copy(obuf.at[at], out_whole.at[at], out_sem.at[c])
            )
            stores[-1].start()
        for store in stores:
            store.wait()


def body(n_slab, n_plane, fields, evap_rates, coal_kernel, plume_width, owner_map, deposit_cell, plume_ids):
    _, sections, ca, cb = fields.shape
    exit_rows = owner_map.shape[1]
    owners = n_slab * n_plane
    rows = sections * ca
    fold = jnp.asarray(fold_matrix(sections), BF16)
    kept = fold.shape[1]
    hbm = pl.BlockSpec(memory_space=pl.ANY)
    vmem = pl.BlockSpec(memory_space=pltpu.VMEM)
    held, rows_in, sides_in, widths = pl.pallas_call(
        functools.partial(kernel, n_slab, n_plane, sections, ca, cb, exit_rows),
        out_shape=[
            pltpu.VMEM((2 * rows + sections * PAD, LANES), F32),
            pltpu.VMEM((owners, 16, LANES), BF16),
            pltpu.VMEM((owners, 3, 1, LANES), F32),
            pltpu.VMEM(plume_width.shape + (8, LANES), F32),
        ],
        in_specs=[hbm] * 8,
        out_specs=[vmem] * 4,
        scratch_shapes=[
            pltpu.VMEM((2 * rows + sections * PAD, LANES), F32),
            pltpu.VMEM((ca + 2, sections, cb), F32),
            pltpu.VMEM((2, sections, cb), BF16),
            pltpu.VMEM((2, sections, cb), BF16),
            pltpu.VMEM((3, sections, LANES), F32),
            pltpu.VMEM((sections * sections, kept), BF16),
            pltpu.VMEM((2, rows // LANES, LANES), F32),
            pltpu.VMEM((2, rows // LANES, LANES), F32),
            pltpu.VMEM((2, rows // LANES, LANES), F32),
            pltpu.VMEM((8, exit_rows), F32),
            pltpu.VMEM((owners, 16, LANES), BF16),
            pltpu.SMEM(evap_rates.shape, F32),
            pltpu.VMEM(coal_kernel.shape, BF16),
            pltpu.SMEM(plume_width.shape, F32),
            pltpu.VMEM((1, exit_rows), jnp.int32),
            pltpu.VMEM((1, exit_rows), jnp.int32),
            pltpu.VMEM((1, exit_rows), jnp.int32),
            pltpu.VMEM((owners * 8, exit_rows), BF16),
            pltpu.VMEM((SLOTS, exit_rows), BF16),
            pltpu.SemaphoreType.DMA,
            pltpu.SemaphoreType.DMA((4,)),
            pltpu.SemaphoreType.DMA((4,)),
            pltpu.SemaphoreType.DMA((4,)),
            pltpu.SemaphoreType.DMA((owners,)),
            pltpu.SemaphoreType.DMA,
            pltpu.VMEM((3, 1, LANES), F32),
            pltpu.SemaphoreType.DMA((owners,)),
            pltpu.SemaphoreType.DMA,
        ],
        compiler_params=pltpu.CompilerParams(
            collective_id=0, has_side_effects=True, vmem_limit_bytes=VMEM_BYTES
        ),
    )(
        fields.reshape(rows // 8, 8, 2, LANES).transpose(0, 2, 1, 3).reshape(2 * rows, LANES), evap_rates, coal_kernel, fold, plume_width,
        owner_map, deposit_cell, plume_ids,
    )
    span = SOURCES * SLOTS
    out = pl.pallas_call(
        functools.partial(finish, n_plane, owners, sections, ca, cb),
        out_shape=jax.ShapeDtypeStruct((2 * rows, LANES), F32),
        in_specs=[vmem] * 4,
        out_specs=hbm,
        scratch_shapes=[
            pltpu.VMEM((sections, 2 * ca, LANES), F32),
            pltpu.VMEM(((owners + 2 * n_plane) * LINES, LANES), F32),
            pltpu.VMEM((5, owners, SLOTS), F32),
            pltpu.VMEM((sections, span), F32),
            pltpu.VMEM((rows, span), BF16),
            pltpu.VMEM((rows, span), BF16),
            pltpu.VMEM((cb, span), BF16),
            pltpu.VMEM((cb, span), BF16),
            pltpu.SemaphoreType.DMA((len(PIECES),)),
        ],
        compiler_params=pltpu.CompilerParams(vmem_limit_bytes=VMEM_BYTES),
    )(
        pltpu.with_memory_space_constraint(held, pltpu.VMEM),
        pltpu.with_memory_space_constraint(rows_in, pltpu.VMEM),
        pltpu.with_memory_space_constraint(sides_in, pltpu.VMEM),
        pltpu.with_memory_space_constraint(widths, pltpu.VMEM),
    )
    out = out.reshape(rows // 8, 2, 8, LANES).transpose(0, 2, 1, 3)
    return out.reshape(1, sections, ca, cb)


def solution(mesh):
    return jax.shard_map(
        functools.partial(body, mesh.shape["slab"], mesh.shape["plane"]),
        mesh=mesh,
        in_specs=(
            P("group", None, "slab", "plane"),
            P(),
            P(),
            P(),
            P(("slab", "plane"), None),
            P(("slab", "plane"), None),
            P(("slab", "plane"), None),
        ),
        out_specs=P("group", None, "slab", "plane"),
        check_vma=False,
    )
```
